32 devices in a mesh: clip: 8 (over z, core), row: 4 (over y, x).
Axes of the slice: x: 2, y: 2, z: 4, core: 2. Of those that a mesh axis runs over, the one named last changes fastest.
Arguments:
- inputs: bfloat16 [32768, 384], P(('clip', 'row')), may hold values from -6 to 6
- cotangent: bfloat16 [32768, 384], P(('clip', 'row')), may hold values from -6 to 6
- source_of: int32 [32768], P(('clip', 'row')), may hold values from 0 to 32767, as said below
- split_row: int32 [8], P('clip'), may hold values from 32 to 64, as said below
- qkv_weight: bfloat16 [2, 384, 1152], P(None, 'row'), may hold values from -0.3125 to 0.3125
- qv_bias: bfloat16 [2, 2, 384], P(None, None, 'row'), may hold values from -3 to 3
- proj_weight: bfloat16 [2, 384, 384], P(None, 'row'), may hold values from -1.25 to 1.25
- proj_bias: bfloat16 [2, 384], P(None, 'row'), may hold values from -2 to 2
- fc1_weight: bfloat16 [2, 384, 1536], P(None, 'row'), may hold values from -0.3125 to 0.3125
- fc1_bias: bfloat16 [2, 1536], P(None, 'row'), may hold values from -2 to 2
- fc2_weight: bfloat16 [2, 1536, 384], P(None, 'row'), may hold values from -0.21875 to 0.21875
- fc2_bias: bfloat16 [2, 384], P(None, 'row'), may hold values from -2 to 2
- norm_gain: bfloat16 [2, 2, 384], P(None, None, 'row'), may hold values from 0.25 to 1.75
- norm_bias: bfloat16 [2, 2, 384], P(None, None, 'row'), may hold values from -2 to 2
- rel_table: float32 [2, 225, 16], replicated, may hold values from -3 to 3
Outputs:
- output: bfloat16 [32768, 384], P(('clip', 'row'))
- input_grad: float32 [32768, 384], P(('clip', 'row'))
- qkv_grad: float32 [2, 384, 1152], P(None, 'row')
- qv_bias_grad: float32 [2, 2, 384], P(None, None, 'row')
- proj_grad: float32 [2, 384, 384], P(None, 'row')
- proj_bias_grad: float32 [2, 384], P(None, 'row')
- fc1_grad: float32 [2, 384, 1536], P(None, 'row')
- fc1_bias_grad: float32 [2, 1536], P(None, 'row')
- fc2_grad: float32 [2, 1536, 384], P(None, 'row')
- fc2_bias_grad: float32 [2, 384], P(None, 'row')
- gain_grad: float32 [2, 2, 384], P(None, None, 'row')
- norm_bias_grad: float32 [2, 2, 384], P(None, None, 'row')
- table_grad: float32 [2, 225, 16], replicated
The draws below stay inside these ranges and needn't reach their ends.
Inputs may be any that keep to these rules, and one draw needn't show every extreme that they name: `source_of`: A permutation; the slot-layout rows of the device with index j of clip+row have sources on every device, 32 from each, and on device s these sources are its rows j * 32 to (j + 1) * 32 - 1. `split_row`: each entry is 32 or 64; both values occur in every draw.
All inputs are finite; a program needn't handle non-finite values.
Results may differ from the reference program's by a relative error of at most 0.023.
Values may be sent and summed in bfloat16 or wider, within the bound.
A program may use at most 192 MiB of HBM per device.

```python
import jax
import jax.numpy as jnp
from jax import lax

D = 384
HEADS = 16
FF = 1536
WIN = 8
SHIFT = 4
LAYERS = 2
GRID_COLS = 64
TABLE = 225
TOK_DEV = 1024
SLOT_ROWS = 64
SLOTS = 8
SENDERS = 32
BLOCK = 32
ALL = 32768


def draw_source_of(key, part):
    key = jax.random.fold_in(key, 23)
    device_keys = jax.random.split(key, SENDERS)
    orders = jax.vmap(lambda one_key: jax.random.permutation(one_key, TOK_DEV))(device_keys).astype(jnp.int32)
    target = jnp.arange(SENDERS, dtype=jnp.int32)[:, None]
    sources = orders // BLOCK * TOK_DEV + target * BLOCK + orders % BLOCK
    return sources.reshape(-1).astype(jnp.int32)


def draw_split_row(key, part):
    key = jax.random.fold_in(key, 11)
    halves = jax.random.randint(key, (SLOTS,), 0, 2)
    order = jax.random.permutation(jax.random.fold_in(key, 1), SLOTS)
    marked = jnp.zeros((SLOTS,), jnp.int32).at[order[0]].set(1).at[order[1]].set(2)
    chosen = jnp.where(marked == 1, 0, jnp.where(marked == 2, 1, halves))
    return (SLOT_ROWS - chosen * (SLOT_ROWS // 2)).astype(jnp.int32)


def shard_levels(key, shape, shards, least, largest):
    level, own = 1.0, jax.random.fold_in(key, 6)
    for axis_at, shards_of in shards:
        draws = jnp.exp(jax.random.uniform(jax.random.fold_in(own, axis_at), (shards_of,), jnp.float32, least / len(shards), largest / len(shards)))
        level = level * jnp.repeat(draws, shape[axis_at] // shards_of).reshape([-1 if axis == axis_at else 1 for axis in range(len(shape))])
    return level


def gaussian(key, extent, scale, bound, cuts=(), kind=jnp.bfloat16):
    values = scale * jax.random.normal(key, extent, jnp.float32)
    if cuts:
        values = values * shard_levels(key, extent, cuts, -0.22, 0.18)
    return jnp.clip(values, -bound, bound).astype(kind)


def setup_inputs(seed: int = 0) -> dict:
    seeds = jax.random.split(jax.random.key(seed), 16)
    return {
        "inputs": gaussian(seeds[0], (ALL, D), 1.0, 6.0, ((0, 32),)),
        "cotangent": gaussian(seeds[1], (ALL, D), 1.0, 6.0, ((0, 32),)),
        "source_of": draw_source_of(jax.random.fold_in(seeds[15], 71), 0),
        "split_row": draw_split_row(jax.random.fold_in(seeds[15], 71), 0),
        "qkv_weight": gaussian(seeds[4], (LAYERS, D, 3 * D), D ** -0.5, 0.3125, ((1, 4),)),
        "qv_bias": gaussian(seeds[5], (LAYERS, 2, D), 0.5, 3.0, ((2, 4),)),
        "proj_weight": gaussian(seeds[6], (LAYERS, D, D), (D // 16) ** -0.5, 1.25, ((1, 4),)),
        "proj_bias": gaussian(seeds[7], (LAYERS, D), 0.3, 2.0, ((1, 4),)),
        "fc1_weight": gaussian(seeds[8], (LAYERS, D, FF), D ** -0.5, 0.3125, ((1, 4),)),
        "fc1_bias": gaussian(seeds[9], (LAYERS, FF), 0.3, 2.0, ((1, 4),)),
        "fc2_weight": gaussian(seeds[10], (LAYERS, FF, D), (FF // 2) ** -0.5, 0.21875, ((1, 4),)),
        "fc2_bias": gaussian(seeds[11], (LAYERS, D), 0.3, 2.0, ((1, 4),)),
        "norm_gain": jnp.clip(1.0 + 0.15 * jax.random.normal(seeds[12], (LAYERS, 2, D), jnp.float32), 0.25, 1.75).astype(jnp.bfloat16),
        "norm_bias": gaussian(seeds[13], (LAYERS, 2, D), 0.3, 2.0, ((2, 4),)),
        "rel_table": gaussian(seeds[14], (LAYERS, TABLE, HEADS), 0.5, 3.0, (), jnp.float32),
    }


@jax.custom_vjp
def low(v):
    return lax.optimization_barrier(v.astype(jnp.bfloat16)).astype(jnp.float32)

@jax.custom_vjp
def low_back(v):
    return v

def low_keep(v):
    return (low(v), None)

def low_pass(kept, grad):
    return (grad,)

def back_keep(v):
    return (v, None)

def back_low(kept, grad):
    return (low(grad),)
low.defvjp(low_keep, low_pass)
low_back.defvjp(back_keep, back_low)
HIGHEST = lax.Precision.HIGHEST
EPSILON = 1e-05
MASKED = -1000000000.0

def both_ways(values):
    return low(low_back(values))

def matmul(first_operand, second_operand):
    return jnp.dot(first_operand, second_operand, precision=HIGHEST)

def layer_norm(values, gain_row, shift_row):
    centred = values - lax.optimization_barrier(jnp.mean(values, axis=-1, keepdims=True))
    spread = lax.optimization_barrier(jnp.mean(centred * centred, axis=-1, keepdims=True))
    return centred * lax.rsqrt(spread + EPSILON) * gain_row + shift_row

def to_windows(values, grid_rows, grid_cols):
    feature = values.shape[-1]
    shaped = values.reshape(grid_rows // WIN, WIN, grid_cols // WIN, WIN, feature)
    return shaped.transpose(0, 2, 1, 3, 4).reshape(-1, WIN * WIN, feature)

def from_windows(values, grid_rows, grid_cols):
    feature = values.shape[-1]
    shaped = values.reshape(grid_rows // WIN, grid_cols // WIN, WIN, WIN, feature)
    return shaped.transpose(0, 2, 1, 3, 4).reshape(grid_rows * grid_cols, feature)

def relative_index():
    place_ids = jnp.arange(WIN * WIN, dtype=jnp.int32)
    row_of = place_ids // WIN
    col_of = place_ids % WIN
    return (row_of[:, None] - row_of[None, :] + WIN - 1) * (2 * WIN - 1) + col_of[:, None] - col_of[None, :] + WIN - 1

def layer(resid, weights, region):
    w_qkv, bias_qv, w_proj, bias_proj, w_up, bias_up, w_down, bias_down, gain_pair, shift_pair, table_rows = weights
    model_width = resid.shape[1]
    head_count = table_rows.shape[1]
    head_dim = model_width // head_count
    grid_rows = resid.shape[0] // GRID_COLS
    hidden_one = low(layer_norm(resid, gain_pair[0], shift_pair[0]))
    projected = matmul(hidden_one, w_qkv)
    queries = both_ways(projected[:, :model_width] + bias_qv[0])
    keys_all = both_ways(projected[:, model_width:2 * model_width])
    values_all = both_ways(projected[:, 2 * model_width:] + bias_qv[1])

    def heads_of(values):
        return to_windows(values, grid_rows, GRID_COLS).reshape(-1, WIN * WIN, head_count, head_dim)
    window_bias = table_rows[relative_index()].transpose(2, 0, 1)
    region_win = to_windows(region[:, None], grid_rows, GRID_COLS)[:, :, 0]
    same_region = region_win[:, :, None] == region_win[:, None, :]
    raw_scores = jnp.einsum('wihd,wjhd->whij', heads_of(queries), heads_of(keys_all), precision=HIGHEST)
    scores = low_back(jnp.where(same_region[:, None], raw_scores * head_dim ** (-0.5) + window_bias[None], MASKED))
    prob_low = low(jax.nn.softmax(scores, axis=-1))
    mixed_win = jnp.einsum('whij,wjhd->wihd', prob_low, heads_of(values_all), precision=HIGHEST)
    attended = both_ways(from_windows(mixed_win.reshape(-1, WIN * WIN, model_width), grid_rows, GRID_COLS))
    middle = resid + low_back(matmul(attended, w_proj) + bias_proj)
    hidden_two = low(layer_norm(middle, gain_pair[1], shift_pair[1]))
    pre_act = low_back(matmul(hidden_two, w_up) + bias_up)
    activated = low(jax.nn.gelu(pre_act, approximate=False))
    return middle + low_back(matmul(activated, w_down) + bias_down)

def pick_layer(params, layer_index):
    return tuple((piece_array[layer_index] for piece_array in params))

def slot_forward(params, slot_values, split_at):
    row_ids = jnp.arange(SLOT_ROWS, dtype=jnp.int32)
    upper_clip = (row_ids >= split_at).astype(jnp.int32)
    region_one = jnp.broadcast_to(upper_clip[:, None], (SLOT_ROWS, GRID_COLS)).reshape(-1)
    moved_rows = row_ids + SHIFT
    wrapped = (moved_rows >= SLOT_ROWS).astype(jnp.int32)
    row_part = (moved_rows - SLOT_ROWS * wrapped >= split_at).astype(jnp.int32) + 2 * wrapped
    col_wrap = (jnp.arange(GRID_COLS, dtype=jnp.int32) + SHIFT >= GRID_COLS).astype(jnp.int32)
    region_two = (2 * row_part[:, None] + col_wrap[None, :]).reshape(-1)
    model_width = slot_values.shape[1]
    layer_one = layer(slot_values, pick_layer(params, 0), region_one)
    rolled_grid = jnp.roll(layer_one.reshape(SLOT_ROWS, GRID_COLS, model_width), (-SHIFT, -SHIFT), (0, 1))
    layer_two = layer(rolled_grid.reshape(-1, model_width), pick_layer(params, 1), region_two)
    restored = jnp.roll(layer_two.reshape(SLOT_ROWS, GRID_COLS, model_width), (SHIFT, SHIFT), (0, 1))
    return restored.reshape(-1, model_width)

def reference(inputs, cotangent, source_of, split_row, qkv_weight, qv_bias, proj_weight, proj_bias, fc1_weight, fc1_bias, fc2_weight, fc2_bias, norm_gain, norm_bias, rel_table):
    params = tuple((piece_array.astype(jnp.float32) for piece_array in (qkv_weight, qv_bias, proj_weight, proj_bias, fc1_weight, fc1_bias, fc2_weight, fc2_bias, norm_gain, norm_bias, rel_table)))
    model_width = inputs.shape[1]
    slot_tokens = SLOT_ROWS * GRID_COLS
    slot_inputs = inputs.astype(jnp.float32)[source_of].reshape(SLOTS, slot_tokens, model_width)
    slot_cotangent = cotangent.astype(jnp.float32)[source_of].reshape(SLOTS, slot_tokens, model_width)

    def step(running, slot_item):
        values_in, cot_in, split_at = slot_item
        slot_out, pull_back = jax.vjp(lambda weights, values: slot_forward(weights, values, split_at), params, values_in)
        weight_grads, value_grad = pull_back(cot_in)
        running = tuple((first_term + second_term for first_term, second_term in zip(running, weight_grads)))
        return (running, (slot_out, value_grad))
    zero_grads = tuple((jnp.zeros(piece_array.shape, jnp.float32) for piece_array in params))
    totals, (slot_outs, slot_grads) = lax.scan(step, zero_grads, (slot_inputs, slot_cotangent, split_row))
    output = jnp.zeros((ALL, model_width), jnp.float32).at[source_of].set(slot_outs.reshape(ALL, model_width)).astype(jnp.bfloat16)
    input_grad = jnp.zeros((ALL, model_width), jnp.float32).at[source_of].set(slot_grads.reshape(ALL, model_width))
    return (output, input_grad, totals[0], totals[1], totals[2], totals[3], totals[4], totals[5], totals[6], totals[7], totals[8], totals[9], totals[10])
```

```python
import functools

import jax
import jax.numpy as jnp
import numpy as np
from jax import lax
from jax.experimental import pallas as pl
from jax.experimental.pallas import tpu as pltpu
from jax.sharding import PartitionSpec as P

WIN = 8
SHIFT = 4
GRID_COLS = 64
EPSILON = 1e-05
MASKED = -1000000000.0
ROOT_HALF = 0.7071067811865476
INV_ROOT_TAU = 0.3989422804014327

HEADS = 16
HEAD_DIM = 24
D = HEADS * HEAD_DIM
GROUP = 8
CELL = WIN * WIN
BLOCK = SHIFT * SHIFT
WIN_COLS = GRID_COLS // WIN
SPREAD = 2 * WIN - 1
TABLE = SPREAD * SPREAD
TABLE_PAD = 256
SCALE = HEAD_DIM**-0.5
CHUNK = 256
CHUNK_WINS = CHUNK // CELL
VMEM_LIMIT = 56 * 1024 * 1024

f32 = jnp.float32
bf16 = jnp.bfloat16


def window_places():
    spot = np.arange(CELL)
    row = (spot // 32) * SHIFT + (spot % BLOCK) // SHIFT
    col = (spot // BLOCK % 2) * SHIFT + spot % SHIFT
    return row, col


def head_masks():
    feature = np.arange(D) // HEAD_DIM
    rows = (feature[None, :] == np.arange(HEADS)[:, None]).astype(np.float32)
    wide = np.stack(
        [
            np.repeat(rows[GROUP * g : GROUP * (g + 1), 128 * g : 128 * g + 256], CELL, axis=0)
            for g in range(2)
        ]
    )
    return rows, wide


def table_constants():
    row, col = window_places()
    natural = row * WIN + col
    lanes = np.zeros((2, TABLE_PAD, 128), np.float32)
    for half in range(2):
        lanes[half, row * SPREAD + col, half * CELL + np.arange(CELL)] = 1.0
    order = np.zeros((CELL, CELL), np.float32)
    order[np.arange(CELL), natural] = 1.0
    back = np.zeros((CELL, CELL), np.float32)
    back[row * WIN + (WIN - 1 - col), np.arange(CELL)] = 1.0
    return lanes, order, back


def dot_nn(a, b):
    return lax.dot_general(a, b, (((1,), (0,)), ((), ())), preferred_element_type=f32)


def dot_nt(a, b):
    return lax.dot_general(a, b, (((1,), (1,)), ((), ())), preferred_element_type=f32)


def dot_tn(a, b):
    return lax.dot_general(a, b, (((0,), (0,)), ((), ())), preferred_element_type=f32)


def dot_exact(a, b, dims):
    return lax.dot_general(
        a, b, (dims, ((), ())), precision=lax.Precision.HIGHEST, preferred_element_type=f32
    )


def whole(shape):
    zeros = (0,) * len(shape)
    return pl.BlockSpec(shape, lambda i: zeros)


def rows_of(shape):
    return pl.BlockSpec(shape, lambda i: (i, 0))


def norm_parts(values):
    centred = values - jnp.mean(values, axis=-1, keepdims=True)
    inverse = lax.rsqrt(jnp.mean(centred * centred, axis=-1, keepdims=True) + EPSILON)
    return centred * inverse, inverse


def norm_back(upstream, normal, inverse, gain):
    scaled = upstream * gain
    centred = scaled - jnp.mean(scaled, axis=-1, keepdims=True)
    return inverse * (centred - normal * jnp.mean(scaled * normal, axis=-1, keepdims=True))


def column_sum(values):
    return jnp.sum(values, axis=0, keepdims=True)


def bias_kernel(table_ref, lanes_ref, order_ref, out_ref, wide_ref):
    for layer in range(2):
        for pair in range(HEADS // 2):
            halves = []
            for half in range(2):
                row = table_ref[layer, 2 * pair + half : 2 * pair + half + 1, :]
                spread = jnp.broadcast_to(row, (WIN, TABLE_PAD))
                for i in range(WIN):
                    wide_ref[WIN * i : WIN * (i + 1), :] = pltpu.roll(
                        spread, (SPREAD * i - 112) % TABLE_PAD, 1, stride=1, stride_axis=0
                    )
                halves.append(dot_exact(wide_ref[...], lanes_ref[half], ((1,), (0,))))
            out_ref[layer, :, 128 * pair : 128 * (pair + 1)] = dot_exact(
                order_ref[...], halves[0] + halves[1], ((1,), (0,))
            )


def bias_tables(rel_table):
    lanes, order, _ = table_constants()
    rows = jnp.pad(rel_table.transpose(0, 2, 1), ((0, 0), (0, 0), (0, TABLE_PAD - TABLE)))
    return pl.pallas_call(
        bias_kernel,
        out_shape=jax.ShapeDtypeStruct((2, CELL, HEADS * CELL), f32),
        scratch_shapes=[pltpu.VMEM((CELL, TABLE_PAD), f32)],
        name="bias_tables",
    )(rows, jnp.asarray(lanes), jnp.asarray(order))


def table_kernel(one_ref, two_ref, lanes_ref, back_ref, out_ref):
    for layer, grad_ref in enumerate((one_ref, two_ref)):
        for pair in range(HEADS // 2):
            turned = dot_exact(
                back_ref[...], grad_ref[:, 128 * pair : 128 * (pair + 1)], ((1,), (0,))
            )
            for half in range(2):
                spread = dot_exact(turned, lanes_ref[half], ((1,), (1,)))
                total = jnp.zeros((WIN, TABLE_PAD), f32)
                for i in range(WIN):
                    total += pltpu.roll(
                        spread[WIN * i : WIN * (i + 1), :],
                        (112 - SPREAD * i - (WIN - 1)) % TABLE_PAD,
                        1,
                        stride=1,
                        stride_axis=0,
                    )
                out_ref[layer, 2 * pair + half : 2 * pair + half + 1, :] = column_sum(total)


def table_sums(grad_one, grad_two):
    lanes, _, back = table_constants()
    return pl.pallas_call(
        table_kernel,
        out_shape=jax.ShapeDtypeStruct((2, HEADS, TABLE_PAD), f32),
        name="table_sums",
    )(grad_one, grad_two, jnp.asarray(lanes), jnp.asarray(back))


def place_kernel(place_ref, rows_ref, out_ref):
    spots = lax.broadcasted_iota(jnp.int32, (CHUNK, rows_ref.shape[0]), 1)
    pick = jnp.where(spots == place_ref[...], 1.0, 0.0).astype(bf16)
    out_ref[...] = dot_nn(pick, rows_ref[...]).astype(out_ref.dtype)


def place_rows(place, rows):
    tokens, width = rows.shape
    return pl.pallas_call(
        place_kernel,
        grid=(tokens // CHUNK,),
        in_specs=[rows_of((CHUNK, 1)), whole((tokens, width))],
        out_specs=rows_of((CHUNK, width)),
        out_shape=jax.ShapeDtypeStruct((tokens, width), bf16),
        name="place_rows",
    )(place, rows)


def unplace_kernel(place_ref, main_ref, edge_ref, out_ref, wide_ref):
    step = pl.program_id(0)

    @pl.when(step == 0)
    def _():
        assemble_back(main_ref, edge_ref, wide_ref)

    tokens = main_ref.shape[0]
    spots = lax.broadcasted_iota(jnp.int32, (CHUNK, tokens), 0) + step * CHUNK
    pick = jnp.where(spots == place_ref[...], 1.0, 0.0).astype(bf16)
    out_ref[...] = dot_nn(pick, wide_ref[...]).astype(out_ref.dtype)


def quarter(window, sub):
    return pl.ds(CELL * window + BLOCK * sub, BLOCK)


def assemble_back(main_ref, edge_ref, out_ref):
    windows = main_ref.shape[0] // CELL
    for window in range(windows):
        wr, wc = divmod(window, WIN_COLS)
        before = (wc - 1) % WIN_COLS
        out_ref[quarter(window, 3), :] = main_ref[quarter(window, 0), :].astype(out_ref.dtype)
        out_ref[quarter(window, 2), :] = main_ref[
            quarter(wr * WIN_COLS + before, 1), :
        ].astype(out_ref.dtype)
        for sub, col, piece in ((1, wc, 0), (0, before, 1)):
            if wr == 0:
                value = edge_ref[pl.ds(2 * BLOCK * col + BLOCK * piece, BLOCK), :]
            else:
                value = main_ref[quarter((wr - 1) * WIN_COLS + col, 2 + piece), :]
            out_ref[quarter(window, sub), :] = value.astype(out_ref.dtype)


def assemble_ahead(main_ref, edge_ref, out_ref):
    windows = main_ref.shape[0] // CELL
    last = windows // WIN_COLS - 1
    for window in range(windows):
        wr, wc = divmod(window, WIN_COLS)
        after = (wc + 1) % WIN_COLS
        out_ref[quarter(window, 0), :] = main_ref[quarter(window, 3), :].astype(out_ref.dtype)
        out_ref[quarter(window, 1), :] = main_ref[
            quarter(wr * WIN_COLS + after, 2), :
        ].astype(out_ref.dtype)
        for sub, col, piece in ((2, wc, 1), (3, after, 0)):
            if wr == last:
                value = edge_ref[pl.ds(2 * BLOCK * col + BLOCK * piece, BLOCK), :]
            else:
                value = main_ref[quarter((wr + 1) * WIN_COLS + col, piece), :]
            out_ref[quarter(window, sub), :] = value.astype(out_ref.dtype)


def unplace_rows(place, main, edge):
    tokens, width = main.shape
    return pl.pallas_call(
        unplace_kernel,
        grid=(tokens // CHUNK,),
        in_specs=[whole((1, tokens)), whole((tokens, width)), whole(edge.shape)],
        out_specs=rows_of((CHUNK, width)),
        out_shape=jax.ShapeDtypeStruct((tokens, width), bf16),
        scratch_shapes=[pltpu.VMEM((tokens, width), bf16)],
        name="unplace_rows",
    )(place, main, edge)


def forward_kernel(
    layer,
    mask_ref,
    *refs,
):
    if layer == 0:
        place_ref, rows_ref = refs[:2]
    else:
        main_ref, edge_ref = refs[:2]
    (
        qkv_w,
        proj_w,
        fc1_w,
        fc2_w,
        vec_ref,
        qkv_b,
        fc1_b,
        bias_ref,
        heads_ref,
        wide_heads_ref,
        x_out,
        qkv_out,
        prob_out,
        att_out,
        mid_out,
        act_out,
        slope_out,
        y_out,
    ) = refs[2:20]
    step = pl.program_id(0)
    if layer == 0:
        spots = lax.broadcasted_iota(jnp.int32, (CHUNK, rows_ref.shape[0]), 1)
        pick = jnp.where(spots == place_ref[...], 1.0, 0.0).astype(bf16)
        x_out[...] = dot_nn(pick, rows_ref[...])
    else:
        whole_ref = refs[20]

        @pl.when(step == 0)
        def _():
            assemble_ahead(main_ref, edge_ref, whole_ref)

        x_out[...] = whole_ref[pl.ds(pl.multiple_of(step * CHUNK, CHUNK), CHUNK), :]
    x = x_out[...]
    normal, _ = norm_parts(x)
    hidden = (normal * vec_ref[4:5, :] + vec_ref[6:7, :]).astype(bf16)
    qkv_out[...] = (dot_nn(hidden, qkv_w[...]) + qkv_b[...]).astype(bf16)
    if layer == 1:
        apart = lax.broadcasted_iota(jnp.int32, (CELL, GROUP * CELL), 0) ^ lax.broadcasted_iota(
            jnp.int32, (CELL, GROUP * CELL), 1
        )
    for k in range(CHUNK_WINS):
        rows = slice(CELL * k, CELL * (k + 1))
        mixed = []
        for g in range(2):
            q = qkv_out[rows, 128 * g : 128 * g + 256]
            key = qkv_out[rows, D + 128 * g : D + 128 * g + 256]
            val = qkv_out[rows, 2 * D + 128 * g : 2 * D + 128 * g + 256]
            q_wide = jnp.concatenate([q] * GROUP, axis=0) * wide_heads_ref[g]
            lanes = slice(GROUP * CELL * g, GROUP * CELL * (g + 1))
            s = dot_nt(key, q_wide) * SCALE + bias_ref[:, lanes]
            if layer == 1:
                cut = mask_ref[step * CHUNK_WINS + k]
                s = jnp.where((apart & cut) == 0, s, MASKED)
            e = jnp.exp(s - jnp.max(s, axis=0, keepdims=True))
            prob = (e * (1.0 / jnp.sum(e, axis=0, keepdims=True))).astype(bf16)
            prob_out[rows, lanes] = prob
            spread = dot_tn(prob, val)
            mixed.append(gather_heads(spread, heads_ref, g))
        att_out[rows, :] = join_groups(*mixed).astype(bf16)
    mid = x + (dot_nn(att_out[...], proj_w[...]) + vec_ref[2:3, :])
    mid_out[...] = mid
    normal, _ = norm_parts(mid)
    hidden = (normal * vec_ref[5:6, :] + vec_ref[7:8, :]).astype(bf16)
    u = dot_nn(hidden, fc1_w[...]) + fc1_b[...]
    cdf = 0.5 * (1.0 + lax.erf(u * ROOT_HALF))
    act_out[...] = (u * cdf).astype(bf16)
    slope_out[...] = (cdf + u * (jnp.exp(-0.5 * u * u) * INV_ROOT_TAU)).astype(bf16)
    y = mid + (dot_nn(act_out[...], fc2_w[...]) + vec_ref[3:4, :])
    y_out[...] = y.astype(y_out.dtype)


def gather_heads(spread, heads_ref, g):
    total = None
    for h in range(GROUP):
        part = spread[CELL * h : CELL * (h + 1), :] * heads_ref[
            GROUP * g + h : GROUP * g + h + 1, 128 * g : 128 * g + 256
        ]
        total = part if total is None else total + part
    return total


def join_groups(low, high):
    return jnp.concatenate([low[:, :128], low[:, 128:] + high[:, :128], high[:, 128:]], axis=1)


def forward_layer(layer, masks, first, second, weights, bias, y_dtype):
    qkv_w, proj_w, fc1_w, fc2_w, vec, qkv_b, fc1_b = weights
    heads, wide = head_masks()
    tokens = 1024 if layer == 0 else first.shape[0]
    tokens = first.shape[0]
    ff = fc1_w.shape[1]
    if layer == 0:
        leading = [rows_of((CHUNK, 1)), whole(second.shape)]
        scratch = []
    else:
        leading = [whole(first.shape), whole(second.shape)]
        scratch = [pltpu.VMEM((tokens, D), f32)]
    operands = (
        qkv_w,
        proj_w,
        fc1_w,
        fc2_w,
        vec,
        qkv_b,
        fc1_b,
        bias,
        jnp.asarray(heads),
        jnp.asarray(wide, dtype=bf16),
    )
    outs = [
        ((tokens, D), f32),
        ((tokens, 3 * D), bf16),
        ((tokens, HEADS * CELL), bf16),
        ((tokens, D), bf16),
        ((tokens, D), f32),
        ((tokens, ff), bf16),
        ((tokens, ff), bf16),
        ((tokens, D), y_dtype),
    ]
    return pl.pallas_call(
        functools.partial(forward_kernel, layer),
        grid=(tokens // CHUNK,),
        in_specs=[pl.BlockSpec(memory_space=pltpu.SMEM)]
        + leading
        + [whole(operand.shape) for operand in operands],
        out_specs=[rows_of((CHUNK, shape[1])) for shape, _ in outs],
        out_shape=[jax.ShapeDtypeStruct(shape, dtype) for shape, dtype in outs],
        scratch_shapes=scratch,
        compiler_params=pltpu.CompilerParams(vmem_limit_bytes=VMEM_LIMIT),
        name=f"forward_{layer}",
    )(masks, first, second, *operands)


def backward_kernel(
    layer,
    main_ref,
    edge_ref,
    x_ref,
    qkv_ref,
    prob_ref,
    att_ref,
    mid_ref,
    act_ref,
    slope_ref,
    qkv_w,
    proj_w,
    fc1_w,
    fc2_w,
    vec_ref,
    heads_ref,
    wide_heads_ref,
    grad_out,
    qkv_g,
    proj_g,
    fc1_g,
    fc2_g,
    vec_g,
    fc1_bg,
    table_g,
    whole_ref,
    h1_ref,
    dt_ref,
    ga_ref,
    h2_ref,
    du_ref,
    gz_ref,
):
    step = pl.program_id(0)
    here = pl.ds(pl.multiple_of(step * CHUNK, CHUNK), CHUNK)

    @pl.when(step == 0)
    def _():
        if layer == 0:
            assemble_back(main_ref, edge_ref, whole_ref)
        else:
            assemble_ahead(main_ref, edge_ref, whole_ref)
        vec_g[...] = jnp.zeros_like(vec_g)
        fc1_bg[...] = jnp.zeros_like(fc1_bg)
        table_g[...] = jnp.zeros_like(table_g)

    upstream = whole_ref[here, :]
    low = upstream.astype(bf16)
    gz_ref[here, :] = low
    vec_g[3:4, :] += column_sum(low.astype(f32))
    du = (dot_nt(low, fc2_w[...]) * slope_ref[...].astype(f32)).astype(bf16)
    du_ref[here, :] = du
    fc1_bg[...] += column_sum(du.astype(f32))
    dn = dot_nt(du, fc1_w[...])
    normal, inverse = norm_parts(mid_ref[...])
    h2_ref[here, :] = (normal * vec_ref[5:6, :] + vec_ref[7:8, :]).astype(bf16)
    vec_g[5:6, :] += column_sum(dn * normal)
    vec_g[7:8, :] += column_sum(dn)
    mid_grad = upstream + norm_back(dn, normal, inverse, vec_ref[5:6, :])
    low = mid_grad.astype(bf16)
    ga_ref[here, :] = low
    vec_g[2:3, :] += column_sum(low.astype(f32))
    att_grad = dot_nt(low, proj_w[...]).astype(bf16)
    for k in range(CHUNK_WINS):
        rows = slice(CELL * k, CELL * (k + 1))
        there = pl.ds(pl.multiple_of(step * CHUNK + CELL * k, CELL), CELL)
        q_parts, k_parts, v_parts = [], [], []
        for g in range(2):
            q = qkv_ref[rows, 128 * g : 128 * g + 256]
            key = qkv_ref[rows, D + 128 * g : D + 128 * g + 256]
            val = qkv_ref[rows, 2 * D + 128 * g : 2 * D + 128 * g + 256]
            do = att_grad[rows, 128 * g : 128 * g + 256]
            q_wide = jnp.concatenate([q] * GROUP, axis=0) * wide_heads_ref[g]
            do_wide = jnp.concatenate([do] * GROUP, axis=0) * wide_heads_ref[g]
            lanes = slice(GROUP * CELL * g, GROUP * CELL * (g + 1))
            prob_low = prob_ref[rows, lanes]
            prob = prob_low.astype(f32)
            dp = dot_nt(val, do_wide)
            v_parts.append(dot_nn(prob_low, do_wide))
            weighted = prob * dp
            ds = (weighted - prob * column_sum(weighted)).astype(bf16)
            table_g[:, lanes] += ds.astype(f32)
            k_parts.append(dot_nn(ds, q_wide))
            q_parts.append(gather_heads(dot_tn(ds, key), heads_ref, g))
        dt_ref[there, 0:D] = (join_groups(*q_parts) * SCALE).astype(bf16)
        dt_ref[there, D : 2 * D] = (join_groups(*k_parts) * SCALE).astype(bf16)
        dt_ref[there, 2 * D : 3 * D] = join_groups(*v_parts).astype(bf16)
    dt = dt_ref[here, :]
    vec_g[0:1, :] += column_sum(dt[:, 0:D].astype(f32))
    vec_g[1:2, :] += column_sum(dt[:, 2 * D :].astype(f32))
    dn = dot_nt(dt, qkv_w[...])
    normal, inverse = norm_parts(x_ref[...])
    h1_ref[here, :] = (normal * vec_ref[4:5, :] + vec_ref[6:7, :]).astype(bf16)
    vec_g[4:5, :] += column_sum(dn * normal)
    vec_g[6:7, :] += column_sum(dn)
    grad_out[...] = (mid_grad + norm_back(dn, normal, inverse, vec_ref[4:5, :])).astype(
        grad_out.dtype
    )

    @pl.when(step == pl.num_programs(0) - 1)
    def _():
        fc2_g[...] = dot_tn(act_ref[...], gz_ref[...]).astype(bf16)
        fc1_g[...] = dot_tn(h2_ref[...], du_ref[...]).astype(bf16)
        proj_g[...] = dot_tn(att_ref[...], ga_ref[...]).astype(bf16)
        qkv_g[...] = dot_tn(h1_ref[...], dt_ref[...]).astype(bf16)


def backward_layer(layer, main, edge, saved, weights, grad_dtype):
    x, qkv, prob, att, mid, act, slope = saved
    qkv_w, proj_w, fc1_w, fc2_w, vec, _, _ = weights
    heads, wide = head_masks()
    tokens = main.shape[0]
    ff = fc1_w.shape[1]
    specs = [
        whole(main.shape),
        whole(edge.shape),
        rows_of((CHUNK, D)),
        rows_of((CHUNK, 3 * D)),
        rows_of((CHUNK, HEADS * CELL)),
        whole(att.shape),
        rows_of((CHUNK, D)),
        whole(act.shape),
        rows_of((CHUNK, ff)),
    ]
    operands = (
        qkv_w,
        proj_w,
        fc1_w,
        fc2_w,
        vec,
        jnp.asarray(heads),
        jnp.asarray(wide, dtype=bf16),
    )
    outs = [
        ((tokens, D), grad_dtype, rows_of((CHUNK, D))),
        (qkv_w.shape, bf16, whole(qkv_w.shape)),
        (proj_w.shape, bf16, whole(proj_w.shape)),
        (fc1_w.shape, bf16, whole(fc1_w.shape)),
        (fc2_w.shape, bf16, whole(fc2_w.shape)),
        (vec.shape, f32, whole(vec.shape)),
        ((1, ff), f32, whole((1, ff))),
        ((CELL, HEADS * CELL), f32, whole((CELL, HEADS * CELL))),
    ]
    return pl.pallas_call(
        functools.partial(backward_kernel, layer),
        grid=(tokens // CHUNK,),
        in_specs=specs + [whole(operand.shape) for operand in operands],
        out_specs=[spec for _, _, spec in outs],
        out_shape=[jax.ShapeDtypeStruct(shape, dtype) for shape, dtype, _ in outs],
        scratch_shapes=[
            pltpu.VMEM((tokens, D), f32),
            pltpu.VMEM((tokens, D), bf16),
            pltpu.VMEM((tokens, 3 * D), bf16),
            pltpu.VMEM((tokens, D), bf16),
            pltpu.VMEM((tokens, D), bf16),
            pltpu.VMEM((tokens, ff), bf16),
            pltpu.VMEM((tokens, D), bf16),
        ],
        compiler_params=pltpu.CompilerParams(vmem_limit_bytes=VMEM_LIMIT),
        name=f"backward_{layer}",
    )(main, edge, x, qkv, prob, att, mid, act, slope, *operands)


def shifted_rows(value, steps):
    count = lax.axis_size("row")
    pairs = [(source, (source + steps) % count) for source in range(count)]
    return lax.ppermute(value, "row", pairs)


def edge_rows(values, first_window, first_sub):
    shaped = values.reshape(-1, CELL, values.shape[-1])
    part = shaped[first_window : first_window + WIN_COLS, first_sub * BLOCK : (first_sub + 2) * BLOCK]
    return part.reshape(-1, values.shape[-1]).astype(bf16)


def exchange(values):
    return lax.all_to_all(values, ("clip", "row"), split_axis=0, concat_axis=0, tiled=True)


def body(
    inputs,
    cotangent,
    source_of,
    split_row,
    qkv_weight,
    qv_bias,
    proj_weight,
    proj_bias,
    fc1_weight,
    fc1_bias,
    fc2_weight,
    fc2_bias,
    norm_gain,
    norm_bias,
    rel_table,
):
    clip_count = lax.axis_size("clip")
    row_count = lax.axis_size("row")
    tokens = inputs.shape[0]
    block_rows = tokens // (clip_count * row_count)
    grid_rows = tokens // GRID_COLS
    slot_rows = grid_rows * row_count
    window_rows = grid_rows // WIN
    part = D // row_count

    placing = source_of // tokens * block_rows + source_of % block_rows
    placing = placing.reshape(window_rows, 2, SHIFT, WIN_COLS, 2, SHIFT)
    placing = placing.transpose(0, 3, 1, 4, 2, 5).reshape(tokens)
    arrived = exchange(inputs)
    incoming = exchange(cotangent)

    middle = lax.axis_index("row") * grid_rows + WIN * (1 + jnp.arange(window_rows))
    row_cut = ((middle == split_row[0]) | (middle == slot_rows)).astype(jnp.int32)
    col_cut = (jnp.arange(WIN_COLS) == WIN_COLS - 1).astype(jnp.int32)
    cuts = (32 * row_cut[:, None] + 16 * col_cut[None, :]).reshape(-1)

    vectors = jnp.concatenate(
        [
            qv_bias,
            proj_bias[:, None],
            fc2_bias[:, None],
            norm_gain,
            norm_bias,
            fc1_bias.reshape(2, -1, part),
        ],
        axis=1,
    )
    vectors = lax.all_gather(vectors, "row", axis=0)
    ff = fc1_weight.shape[2]
    fc1_row = vectors[:, :, 8:].transpose(1, 0, 2, 3).reshape(2, 1, ff).astype(f32)
    vec_rows = vectors[:, :, :8].transpose(1, 2, 0, 3).reshape(2, 8, D).astype(f32)
    qkv_row = jnp.concatenate(
        [vec_rows[:, 0:1], jnp.zeros((2, 1, D), f32), vec_rows[:, 1:2]], axis=2
    )
    weights = []
    for layer in range(2):
        gathered = [
            lax.all_gather(weight[layer], "row", axis=0, tiled=True)
            for weight in (qkv_weight, proj_weight, fc1_weight, fc2_weight)
        ]
        weights.append((*gathered, vec_rows[layer], qkv_row[layer], fc1_row[layer]))
    bias = bias_tables(rel_table)

    *saved_one, layer_one = forward_layer(
        0, cuts, placing.reshape(tokens, 1), arrived, weights[0], bias[0], f32
    )
    incoming = place_rows(placing.reshape(tokens, 1), incoming)
    ahead = shifted_rows(edge_rows(layer_one, 0, 0), -1)
    ahead_grad = shifted_rows(edge_rows(incoming, 0, 0), -1)
    *saved_two, layer_two = forward_layer(1, cuts, layer_one, ahead, weights[1], bias[1], bf16)
    last = (window_rows - 1) * WIN_COLS
    behind = shifted_rows(edge_rows(layer_two, last, 2), 1)
    out_rows = unplace_rows(placing.reshape(1, tokens), layer_two, behind)
    output = exchange(out_rows)
    grad_two, *grads_two = backward_layer(1, incoming, ahead_grad, saved_two, weights[1], f32)
    behind_grad = shifted_rows(edge_rows(grad_two, last, 2), 1)
    grad_one, *grads_one = backward_layer(0, grad_two, behind_grad, saved_one, weights[0], bf16)
    grad_rows = unplace_plain(placing.reshape(1, tokens), grad_one)
    input_grad = exchange(grad_rows).astype(f32)

    totals = []
    for one, two in zip(grads_one[:4], grads_two[:4]):
        pair = []
        for value in (one, two):
            value = lax.psum_scatter(value, "row", scatter_dimension=0, tiled=True)
            pair.append(lax.psum(value, "clip").astype(f32))
        totals.append(jnp.stack(pair))
    table = table_sums(grads_one[6], grads_two[6])
    small = jnp.concatenate(
        [
            jnp.stack([grads_one[4], grads_two[4]]).reshape(2, -1),
            jnp.stack([grads_one[5], grads_two[5]]).reshape(2, -1),
            table.reshape(2, -1),
        ],
        axis=1,
    )
    small = lax.psum(small, ("clip", "row"))
    at = lax.axis_index("row")
    vec_total = small[:, : 8 * D].reshape(2, 8, D)
    vec_total = lax.dynamic_slice_in_dim(vec_total, at * part, part, axis=2)
    fc1_total = lax.dynamic_slice_in_dim(
        small[:, 8 * D : 8 * D + ff], at * (ff // row_count), ff // row_count, axis=1
    )
    table_total = small[:, 8 * D + ff :].reshape(2, HEADS, TABLE_PAD)[:, :, :TABLE]
    return (
        output,
        input_grad,
        totals[0],
        vec_total[:, 0:2],
        totals[1],
        vec_total[:, 2],
        totals[2],
        fc1_total,
        totals[3],
        vec_total[:, 3],
        vec_total[:, 4:6],
        vec_total[:, 6:8],
        table_total.transpose(0, 2, 1),
    )


def unplace_plain_kernel(place_ref, rows_ref, out_ref):
    tokens = rows_ref.shape[0]
    spots = lax.broadcasted_iota(jnp.int32, (CHUNK, tokens), 0) + pl.program_id(0) * CHUNK
    pick = jnp.where(spots == place_ref[...], 1.0, 0.0).astype(bf16)
    out_ref[...] = dot_nn(pick, rows_ref[...]).astype(out_ref.dtype)


def unplace_plain(place, rows):
    tokens, width = rows.shape
    return pl.pallas_call(
        unplace_plain_kernel,
        grid=(tokens // CHUNK,),
        in_specs=[whole((1, tokens)), whole((tokens, width))],
        out_specs=rows_of((CHUNK, width)),
        out_shape=jax.ShapeDtypeStruct((tokens, width), bf16),
        name="unplace_plain",
    )(place, rows)


def solution(mesh):
    placed = (
        P(("clip", "row"), None),
        P(("clip", "row"), None),
        P(("clip", "row")),
        P("clip"),
        P(None, "row", None),
        P(None, None, "row"),
        P(None, "row", None),
        P(None, "row"),
        P(None, "row", None),
        P(None, "row"),
        P(None, "row", None),
        P(None, "row"),
        P(None, None, "row"),
        P(None, None, "row"),
        P(),
    )
    return jax.shard_map(
        body,
        mesh=mesh,
        in_specs=placed,
        out_specs=(
            P(("clip", "row"), None),
            P(("clip", "row"), None),
            P(None, "row", None),
            P(None, None, "row"),
            P(None, "row", None),
            P(None, "row"),
            P(None, "row", None),
            P(None, "row"),
            P(None, "row", None),
            P(None, "row"),
            P(None, None, "row"),
            P(None, None, "row"),
            P(),
        ),
        check_vma=False,
    )
```

```python
import functools

import jax
import jax.numpy as jnp
import numpy as np
from jax import lax
from jax.experimental import pallas as pl
from jax.experimental.pallas import tpu as pltpu
from jax.sharding import PartitionSpec as P

WIN = 8
SHIFT = 4
GRID_COLS = 64
EPSILON = 1e-05
MASKED = -1000000000.0
ROOT_HALF = 0.7071067811865476
INV_ROOT_TAU = 0.3989422804014327

HEADS = 16
HEAD_DIM = 24
D = HEADS * HEAD_DIM
GROUP = 8
CELL = WIN * WIN
BLOCK = SHIFT * SHIFT
WIN_COLS = GRID_COLS // WIN
SPREAD = 2 * WIN - 1
TABLE = SPREAD * SPREAD
TABLE_PAD = 256
SCALE = HEAD_DIM**-0.5
CHUNK = 256
CHUNK_WINS = CHUNK // CELL
VMEM_LIMIT = 56 * 1024 * 1024

MESH = pl.DeviceIdType.MESH
f32 = jnp.float32
bf16 = jnp.bfloat16


def window_places():
    spot = np.arange(CELL)
    row = (spot // 32) * SHIFT + (spot % BLOCK) // SHIFT
    col = (spot // BLOCK % 2) * SHIFT + spot % SHIFT
    return row, col


def head_masks():
    feature = np.arange(D) // HEAD_DIM
    rows = (feature[None, :] == np.arange(HEADS)[:, None]).astype(np.float32)
    wide = np.stack(
        [
            np.repeat(rows[GROUP * g : GROUP * (g + 1), 128 * g : 128 * g + 256], CELL, axis=0)
            for g in range(2)
        ]
    )
    return rows, wide


def table_constants():
    row, col = window_places()
    natural = row * WIN + col
    lanes = np.zeros((2, TABLE_PAD, 128), np.float32)
    for half in range(2):
        lanes[half, row * SPREAD + col, half * CELL + np.arange(CELL)] = 1.0
    order = np.zeros((CELL, CELL), np.float32)
    order[np.arange(CELL), natural] = 1.0
    back = np.zeros((CELL, CELL), np.float32)
    back[row * WIN + (WIN - 1 - col), np.arange(CELL)] = 1.0
    return lanes, order, back


def dot_nn(a, b):
    return lax.dot_general(a, b, (((1,), (0,)), ((), ())), preferred_element_type=f32)


def dot_nt(a, b):
    return lax.dot_general(a, b, (((1,), (1,)), ((), ())), preferred_element_type=f32)


def dot_tn(a, b):
    return lax.dot_general(a, b, (((0,), (0,)), ((), ())), preferred_element_type=f32)


def dot_exact(a, b, dims):
    return lax.dot_general(
        a, b, (dims, ((), ())), precision=lax.Precision.HIGHEST, preferred_element_type=f32
    )


def whole(shape):
    zeros = (0,) * len(shape)
    return pl.BlockSpec(shape, lambda i: zeros)


def rows_of(shape):
    return pl.BlockSpec(shape, lambda i: (i, 0))


def norm_parts(values):
    centred = values - jnp.mean(values, axis=-1, keepdims=True)
    inverse = lax.rsqrt(jnp.mean(centred * centred, axis=-1, keepdims=True) + EPSILON)
    return centred * inverse, inverse


def norm_back(upstream, normal, inverse, gain):
    scaled = upstream * gain
    centred = scaled - jnp.mean(scaled, axis=-1, keepdims=True)
    return inverse * (centred - normal * jnp.mean(scaled * normal, axis=-1, keepdims=True))


def column_sum(values):
    return jnp.sum(values, axis=0, keepdims=True)


def bias_kernel(table_ref, lanes_ref, order_ref, out_ref, wide_ref):
    for layer in range(2):
        for pair in range(HEADS // 2):
            halves = []
            for half in range(2):
                row = table_ref[layer, 2 * pair + half : 2 * pair + half + 1, :]
                spread = jnp.broadcast_to(row, (WIN, TABLE_PAD))
                for i in range(WIN):
                    wide_ref[WIN * i : WIN * (i + 1), :] = pltpu.roll(
                        spread, (SPREAD * i - 112) % TABLE_PAD, 1, stride=1, stride_axis=0
                    )
                halves.append(dot_exact(wide_ref[...], lanes_ref[half], ((1,), (0,))))
            out_ref[layer, :, 128 * pair : 128 * (pair + 1)] = dot_exact(
                order_ref[...], halves[0] + halves[1], ((1,), (0,))
            )


def bias_tables(rel_table):
    lanes, order, _ = table_constants()
    rows = jnp.pad(rel_table.transpose(0, 2, 1), ((0, 0), (0, 0), (0, TABLE_PAD - TABLE)))
    return pl.pallas_call(
        bias_kernel,
        out_shape=jax.ShapeDtypeStruct((2, CELL, HEADS * CELL), f32),
        scratch_shapes=[pltpu.VMEM((CELL, TABLE_PAD), f32)],
        name="bias_tables",
    )(rows, jnp.asarray(lanes), jnp.asarray(order))


def table_rows(grad_ref, lanes_ref, back_ref, out_ref):
    for pair in range(HEADS // 2):
        turned = dot_exact(back_ref[...], grad_ref[:, 128 * pair : 128 * (pair + 1)], ((1,), (0,)))
        for half in range(2):
            spread = dot_exact(turned, lanes_ref[half], ((1,), (1,)))
            total = jnp.zeros((WIN, TABLE_PAD), f32)
            for i in range(WIN):
                total += pltpu.roll(
                    spread[WIN * i : WIN * (i + 1), :],
                    (112 - SPREAD * i - (WIN - 1)) % TABLE_PAD,
                    1,
                    stride=1,
                    stride_axis=0,
                )
            out_ref[2 * pair + half : 2 * pair + half + 1, :] = column_sum(total)


def place_kernel(place_ref, rows_ref, out_ref):
    spots = lax.broadcasted_iota(jnp.int32, (CHUNK, rows_ref.shape[0]), 1)
    pick = jnp.where(spots == place_ref[...], 1.0, 0.0).astype(bf16)
    out_ref[...] = dot_nn(pick, rows_ref[...]).astype(out_ref.dtype)


def place_rows(place, rows):
    tokens, width = rows.shape
    return pl.pallas_call(
        place_kernel,
        grid=(tokens // CHUNK,),
        in_specs=[rows_of((CHUNK, 1)), whole((tokens, width))],
        out_specs=rows_of((CHUNK, width)),
        out_shape=jax.ShapeDtypeStruct((tokens, width), bf16),
        name="place_rows",
    )(place, rows)


def unplace_kernel(place_ref, main_ref, edge_ref, out_ref, wide_ref):
    step = pl.program_id(0)

    @pl.when(step == 0)
    def _():
        assemble_back(main_ref, edge_ref, wide_ref)

    tokens = main_ref.shape[0]
    spots = lax.broadcasted_iota(jnp.int32, (CHUNK, tokens), 0) + step * CHUNK
    pick = jnp.where(spots == place_ref[...], 1.0, 0.0).astype(bf16)
    out_ref[...] = dot_nn(pick, wide_ref[...]).astype(out_ref.dtype)


def quarter(window, sub):
    return pl.ds(CELL * window + BLOCK * sub, BLOCK)


def assemble_back(main_ref, edge_ref, out_ref):
    windows = main_ref.shape[0] // CELL
    for window in range(windows):
        wr, wc = divmod(window, WIN_COLS)
        before = (wc - 1) % WIN_COLS
        out_ref[quarter(window, 3), :] = main_ref[quarter(window, 0), :].astype(out_ref.dtype)
        out_ref[quarter(window, 2), :] = main_ref[
            quarter(wr * WIN_COLS + before, 1), :
        ].astype(out_ref.dtype)
        for sub, col, piece in ((1, wc, 0), (0, before, 1)):
            if wr == 0:
                value = edge_ref[pl.ds(2 * BLOCK * col + BLOCK * piece, BLOCK), :]
            else:
                value = main_ref[quarter((wr - 1) * WIN_COLS + col, 2 + piece), :]
            out_ref[quarter(window, sub), :] = value.astype(out_ref.dtype)


def assemble_ahead(main_ref, edge_ref, out_ref):
    windows = main_ref.shape[0] // CELL
    last = windows // WIN_COLS - 1
    for window in range(windows):
        wr, wc = divmod(window, WIN_COLS)
        after = (wc + 1) % WIN_COLS
        out_ref[quarter(window, 0), :] = main_ref[quarter(window, 3), :].astype(out_ref.dtype)
        out_ref[quarter(window, 1), :] = main_ref[
            quarter(wr * WIN_COLS + after, 2), :
        ].astype(out_ref.dtype)
        for sub, col, piece in ((2, wc, 1), (3, after, 0)):
            if wr == last:
                value = edge_ref[pl.ds(2 * BLOCK * col + BLOCK * piece, BLOCK), :]
            else:
                value = main_ref[quarter((wr + 1) * WIN_COLS + col, piece), :]
            out_ref[quarter(window, sub), :] = value.astype(out_ref.dtype)


def unplace_rows(place, main, edge):
    tokens, width = main.shape
    return pl.pallas_call(
        unplace_kernel,
        grid=(tokens // CHUNK,),
        in_specs=[whole((1, tokens)), whole((tokens, width)), whole(edge.shape)],
        out_specs=rows_of((CHUNK, width)),
        out_shape=jax.ShapeDtypeStruct((tokens, width), bf16),
        scratch_shapes=[pltpu.VMEM((tokens, width), bf16)],
        name="unplace_rows",
    )(place, main, edge)


def forward_kernel(
    layer,
    mask_ref,
    *refs,
):
    if layer == 0:
        place_ref, rows_ref = refs[:2]
    else:
        main_ref, edge_ref = refs[:2]
    (
        qkv_w,
        proj_w,
        fc1_w,
        fc2_w,
        vec_ref,
        qkv_b,
        fc1_b,
        bias_ref,
        heads_ref,
        wide_heads_ref,
        x_out,
        qkv_out,
        prob_out,
        att_out,
        mid_out,
        act_out,
        slope_out,
        y_out,
    ) = refs[2:20]
    step = pl.program_id(0)
    if layer == 0:
        spots = lax.broadcasted_iota(jnp.int32, (CHUNK, rows_ref.shape[0]), 1)
        pick = jnp.where(spots == place_ref[...], 1.0, 0.0).astype(bf16)
        x_out[...] = dot_nn(pick, rows_ref[...])
    else:
        whole_ref = refs[20]

        @pl.when(step == 0)
        def _():
            assemble_ahead(main_ref, edge_ref, whole_ref)

        x_out[...] = whole_ref[pl.ds(pl.multiple_of(step * CHUNK, CHUNK), CHUNK), :]
    x = x_out[...]
    normal, _ = norm_parts(x)
    hidden = (normal * vec_ref[4:5, :] + vec_ref[6:7, :]).astype(bf16)
    qkv_out[...] = (dot_nn(hidden, qkv_w[...]) + qkv_b[...]).astype(bf16)
    if layer == 1:
        apart = lax.broadcasted_iota(jnp.int32, (CELL, GROUP * CELL), 0) ^ lax.broadcasted_iota(
            jnp.int32, (CELL, GROUP * CELL), 1
        )
    for k in range(CHUNK_WINS):
        rows = slice(CELL * k, CELL * (k + 1))
        mixed = []
        for g in range(2):
            q = qkv_out[rows, 128 * g : 128 * g + 256]
            key = qkv_out[rows, D + 128 * g : D + 128 * g + 256]
            val = qkv_out[rows, 2 * D + 128 * g : 2 * D + 128 * g + 256]
            q_wide = jnp.concatenate([q] * GROUP, axis=0) * wide_heads_ref[g]
            lanes = slice(GROUP * CELL * g, GROUP * CELL * (g + 1))
            s = dot_nt(key, q_wide) * SCALE + bias_ref[:, lanes]
            if layer == 1:
                cut = mask_ref[step * CHUNK_WINS + k]
                s = jnp.where((apart & cut) == 0, s, MASKED)
            e = jnp.exp(s - jnp.max(s, axis=0, keepdims=True))
            prob = (e * (1.0 / jnp.sum(e, axis=0, keepdims=True))).astype(bf16)
            prob_out[rows, lanes] = prob
            spread = dot_tn(prob, val)
            mixed.append(gather_heads(spread, heads_ref, g))
        att_out[rows, :] = join_groups(*mixed).astype(bf16)
    mid = x + (dot_nn(att_out[...], proj_w[...]) + vec_ref[2:3, :])
    mid_out[...] = mid
    normal, _ = norm_parts(mid)
    hidden = (normal * vec_ref[5:6, :] + vec_ref[7:8, :]).astype(bf16)
    u = dot_nn(hidden, fc1_w[...]) + fc1_b[...]
    cdf = 0.5 * (1.0 + lax.erf(u * ROOT_HALF))
    act_out[...] = (u * cdf).astype(bf16)
    slope_out[...] = (cdf + u * (jnp.exp(-0.5 * u * u) * INV_ROOT_TAU)).astype(bf16)
    y = mid + (dot_nn(act_out[...], fc2_w[...]) + vec_ref[3:4, :])
    y_out[...] = y.astype(y_out.dtype)


def gather_heads(spread, heads_ref, g):
    total = None
    for h in range(GROUP):
        part = spread[CELL * h : CELL * (h + 1), :] * heads_ref[
            GROUP * g + h : GROUP * g + h + 1, 128 * g : 128 * g + 256
        ]
        total = part if total is None else total + part
    return total


def join_groups(low, high):
    return jnp.concatenate([low[:, :128], low[:, 128:] + high[:, :128], high[:, 128:]], axis=1)


def forward_layer(layer, masks, first, second, weights, bias, y_dtype):
    qkv_w, proj_w, fc1_w, fc2_w, vec, qkv_b, fc1_b = weights
    heads, wide = head_masks()
    tokens = 1024 if layer == 0 else first.shape[0]
    tokens = first.shape[0]
    ff = fc1_w.shape[1]
    if layer == 0:
        leading = [rows_of((CHUNK, 1)), whole(second.shape)]
        scratch = []
    else:
        leading = [whole(first.shape), whole(second.shape)]
        scratch = [pltpu.VMEM((tokens, D), f32)]
    operands = (
        qkv_w,
        proj_w,
        fc1_w,
        fc2_w,
        vec,
        qkv_b,
        fc1_b,
        bias,
        jnp.asarray(heads),
        jnp.asarray(wide, dtype=bf16),
    )
    outs = [
        ((tokens, D), f32),
        ((tokens, 3 * D), bf16),
        ((tokens, HEADS * CELL), bf16),
        ((tokens, D), bf16),
        ((tokens, D), f32),
        ((tokens, ff), bf16),
        ((tokens, ff), bf16),
        ((tokens, D), y_dtype),
    ]
    return pl.pallas_call(
        functools.partial(forward_kernel, layer),
        grid=(tokens // CHUNK,),
        in_specs=[pl.BlockSpec(memory_space=pltpu.SMEM)]
        + leading
        + [whole(operand.shape) for operand in operands],
        out_specs=[rows_of((CHUNK, shape[1])) for shape, _ in outs],
        out_shape=[jax.ShapeDtypeStruct(shape, dtype) for shape, dtype in outs],
        scratch_shapes=scratch,
        compiler_params=pltpu.CompilerParams(vmem_limit_bytes=VMEM_LIMIT),
        name=f"forward_{layer}",
    )(masks, first, second, *operands)


def backward_kernel(
    layer,
    main_ref,
    edge_ref,
    x_ref,
    qkv_ref,
    prob_ref,
    att_ref,
    mid_ref,
    act_ref,
    slope_ref,
    qkv_w,
    proj_w,
    fc1_w,
    fc2_w,
    vec_ref,
    heads_ref,
    wide_heads_ref,
    lanes_ref,
    back_ref,
    grad_out,
    packed_out,
    vec_g,
    fc1_bg,
    table_g,
    table_t,
    whole_ref,
    h1_ref,
    dt_ref,
    ga_ref,
    h2_ref,
    du_ref,
    gz_ref,
):
    step = pl.program_id(0)
    here = pl.ds(pl.multiple_of(step * CHUNK, CHUNK), CHUNK)

    @pl.when(step == 0)
    def _():
        if layer == 0:
            assemble_back(main_ref, edge_ref, whole_ref)
        else:
            assemble_ahead(main_ref, edge_ref, whole_ref)
        vec_g[...] = jnp.zeros_like(vec_g)
        fc1_bg[...] = jnp.zeros_like(fc1_bg)
        table_g[...] = jnp.zeros_like(table_g)

    upstream = whole_ref[here, :]
    low = upstream.astype(bf16)
    gz_ref[here, :] = low
    vec_g[3:4, :] += column_sum(low.astype(f32))
    du = (dot_nt(low, fc2_w[...]) * slope_ref[...].astype(f32)).astype(bf16)
    du_ref[here, :] = du
    fc1_bg[...] += column_sum(du.astype(f32))
    dn = dot_nt(du, fc1_w[...])
    normal, inverse = norm_parts(mid_ref[...])
    h2_ref[here, :] = (normal * vec_ref[5:6, :] + vec_ref[7:8, :]).astype(bf16)
    vec_g[5:6, :] += column_sum(dn * normal)
    vec_g[7:8, :] += column_sum(dn)
    mid_grad = upstream + norm_back(dn, normal, inverse, vec_ref[5:6, :])
    low = mid_grad.astype(bf16)
    ga_ref[here, :] = low
    vec_g[2:3, :] += column_sum(low.astype(f32))
    att_grad = dot_nt(low, proj_w[...]).astype(bf16)
    for k in range(CHUNK_WINS):
        rows = slice(CELL * k, CELL * (k + 1))
        there = pl.ds(pl.multiple_of(step * CHUNK + CELL * k, CELL), CELL)
        q_parts, k_parts, v_parts = [], [], []
        for g in range(2):
            q = qkv_ref[rows, 128 * g : 128 * g + 256]
            key = qkv_ref[rows, D + 128 * g : D + 128 * g + 256]
            val = qkv_ref[rows, 2 * D + 128 * g : 2 * D + 128 * g + 256]
            do = att_grad[rows, 128 * g : 128 * g + 256]
            q_wide = jnp.concatenate([q] * GROUP, axis=0) * wide_heads_ref[g]
            do_wide = jnp.concatenate([do] * GROUP, axis=0) * wide_heads_ref[g]
            lanes = slice(GROUP * CELL * g, GROUP * CELL * (g + 1))
            prob_low = prob_ref[rows, lanes]
            prob = prob_low.astype(f32)
            dp = dot_nt(val, do_wide)
            v_parts.append(dot_nn(prob_low, do_wide))
            weighted = prob * dp
            ds = (weighted - prob * column_sum(weighted)).astype(bf16)
            table_g[:, lanes] += ds.astype(f32)
            k_parts.append(dot_nn(ds, q_wide))
            q_parts.append(gather_heads(dot_tn(ds, key), heads_ref, g))
        dt_ref[there, 0:D] = (join_groups(*q_parts) * SCALE).astype(bf16)
        dt_ref[there, D : 2 * D] = (join_groups(*k_parts) * SCALE).astype(bf16)
        dt_ref[there, 2 * D : 3 * D] = join_groups(*v_parts).astype(bf16)
    dt = dt_ref[here, :]
    vec_g[0:1, :] += column_sum(dt[:, 0:D].astype(f32))
    vec_g[1:2, :] += column_sum(dt[:, 2 * D :].astype(f32))
    dn = dot_nt(dt, qkv_w[...])
    normal, inverse = norm_parts(x_ref[...])
    h1_ref[here, :] = (normal * vec_ref[4:5, :] + vec_ref[6:7, :]).astype(bf16)
    vec_g[4:5, :] += column_sum(dn * normal)
    vec_g[6:7, :] += column_sum(dn)
    grad_out[...] = (mid_grad + norm_back(dn, normal, inverse, vec_ref[4:5, :])).astype(
        grad_out.dtype
    )

    @pl.when(step == pl.num_programs(0) - 1)
    def _():
        n_row = packed_out.shape[1]
        size = D // n_row

        def put(half, at, value):
            for r in range(n_row):
                packed_out[half, r, at : at + size, :] = value[size * r : size * (r + 1), :]

        for j in range(3):
            put(0, size * j, dot_tn(h1_ref[...], dt_ref[:, D * j : D * (j + 1)]).astype(bf16))
        put(0, size * 3, dot_tn(att_ref[...], ga_ref[...]).astype(bf16))
        for j in range(4):
            put(1, size * j, dot_tn(h2_ref[...], du_ref[:, D * j : D * (j + 1)]).astype(bf16))
        fc2 = dot_tn(act_ref[...], gz_ref[...]).astype(bf16)
        table_rows(table_g, lanes_ref, back_ref, table_t)
        vectors = jnp.concatenate(
            [vec_g[...]]
            + [fc1_bg[:, D * j : D * (j + 1)] for j in range(4)]
            + [jnp.zeros((4, D), f32)],
            axis=0,
        ).astype(bf16)
        table = jnp.concatenate(
            [table_t[...], jnp.zeros((HEADS, D - TABLE_PAD), f32)], axis=1
        ).astype(bf16)
        for r in range(n_row):
            for half in range(2):
                at = (2 * r + half) * 2 * size
                packed_out[half, r, 4 * size : 6 * size, :] = fc2[at : at + 2 * size, :]
            packed_out[0, r, 6 * size :, :] = vectors
            packed_out[1, r, 6 * size :, :] = table


def backward_layer(layer, main, edge, saved, weights, grad_dtype):
    x, qkv, prob, att, mid, act, slope = saved
    qkv_w, proj_w, fc1_w, fc2_w, vec, _, _ = weights
    heads, wide = head_masks()
    lanes, _, back = table_constants()
    n_row = lax.axis_size("row")
    packed = (2, n_row, packed_rows(n_row), D)
    tokens = main.shape[0]
    ff = fc1_w.shape[1]
    specs = [
        whole(main.shape),
        whole(edge.shape),
        rows_of((CHUNK, D)),
        rows_of((CHUNK, 3 * D)),
        rows_of((CHUNK, HEADS * CELL)),
        whole(att.shape),
        rows_of((CHUNK, D)),
        whole(act.shape),
        rows_of((CHUNK, ff)),
    ]
    operands = (
        qkv_w,
        proj_w,
        fc1_w,
        fc2_w,
        vec,
        jnp.asarray(heads),
        jnp.asarray(wide, dtype=bf16),
        jnp.asarray(lanes),
        jnp.asarray(back),
    )
    outs = [
        ((tokens, D), grad_dtype, rows_of((CHUNK, D))),
        (packed, bf16, whole(packed)),
    ]
    return pl.pallas_call(
        functools.partial(backward_kernel, layer),
        grid=(tokens // CHUNK,),
        in_specs=specs + [whole(operand.shape) for operand in operands],
        out_specs=[spec for _, _, spec in outs],
        out_shape=[jax.ShapeDtypeStruct(shape, dtype) for shape, dtype, _ in outs],
        scratch_shapes=[
            pltpu.VMEM(vec.shape, f32),
            pltpu.VMEM((1, ff), f32),
            pltpu.VMEM((CELL, HEADS * CELL), f32),
            pltpu.VMEM((HEADS, TABLE_PAD), f32),
            pltpu.VMEM((tokens, D), f32),
            pltpu.VMEM((tokens, D), bf16),
            pltpu.VMEM((tokens, 3 * D), bf16),
            pltpu.VMEM((tokens, D), bf16),
            pltpu.VMEM((tokens, D), bf16),
            pltpu.VMEM((tokens, ff), bf16),
            pltpu.VMEM((tokens, D), bf16),
        ],
        compiler_params=pltpu.CompilerParams(vmem_limit_bytes=VMEM_LIMIT),
        name=f"backward_{layer}",
    )(main, edge, x, qkv, prob, att, mid, act, slope, *operands)


def packed_rows(n_row):
    return 6 * (D // n_row) + 16


def piece_rows(n_row, n_far):
    return -(-packed_rows(n_row) // (16 * n_far)) * 16


class Place:
    def __init__(self, n_row, n_far):
        clip = lax.axis_index("clip")
        self.n_row, self.n_far = n_row, n_far
        self.core, self.far, self.row = clip % 2, clip // 2, lax.axis_index("row")

    def row_at(self, d):
        return (self.row + d) % self.n_row

    def far_at(self, d):
        return (self.far + d) % self.n_far

    def twin(self):
        return (2 * self.far + 1 - self.core, self.row)

    def in_row(self, d):
        return (2 * self.far + self.core, self.row_at(d))

    def along(self, d):
        return (2 * self.far_at(d) + self.core, self.row)

    def partners(self, far=True):
        found = [self.twin()] + [self.in_row(d) for d in range(1, self.n_row)]
        return found + ([self.along(d) for d in range(1, self.n_far)] if far else [])


def meet(partners):
    barrier = pltpu.get_barrier_semaphore()
    for partner in partners:
        pl.semaphore_signal(barrier, inc=1, device_id=partner, device_id_type=MESH)
    pl.semaphore_wait(barrier, len(partners))


def send(src, dst, send_sem, recv_sem, target):
    copy = pltpu.make_async_remote_copy(
        src_ref=src,
        dst_ref=dst,
        send_sem=send_sem,
        recv_sem=recv_sem,
        device_id=target,
        device_id_type=MESH,
    )
    copy.start()
    return copy


def sum_kernel(
    n_row,
    n_far,
    one_ref,
    two_ref,
    out_ref,
    own,
    got_a,
    out_b,
    got_b,
    out_c,
    got_c,
    final,
    own_sem,
    a_sem,
    b_sem,
    c_sem,
    d_sem,
    e_sem,
    out_sem,
):
    place = Place(n_row, n_far)
    core, row, far = place.core, place.row, place.far
    piece = got_c.shape[2]
    valid = own.shape[2]

    def part(ref, layer, at):
        return ref.at[layer, pl.ds(pl.multiple_of(at * piece, 16), piece), :]

    order = (1, 0)
    refs = (one_ref, two_ref)
    mine = [pltpu.make_async_copy(refs[l].at[core], own.at[l], own_sem.at[l]) for l in range(2)]
    for l in order:
        mine[l].start()
    meet(place.partners())
    copies_a, copies_b, copies_c, copies_d, copies_e = {}, {}, {}, {}, {}
    for l in order:
        copies_a[l] = send(
            refs[l].at[1 - core], got_a.at[l], a_sem.at[0, l], a_sem.at[1, l], place.twin()
        )
    if n_far * piece > valid:
        out_c[:, valid:, :] = jnp.zeros((2, n_far * piece - valid, D), bf16)
    for l in order:
        mine[l].wait()
        copies_a[l].wait_recv()
        for d in range(1, n_row):
            r = place.row_at(d)
            out_b[l, r] = own[l, r] + got_a[l, r]
            copies_b[l, d] = send(
                out_b.at[l, r],
                got_b.at[l, d - 1],
                b_sem.at[0, l, d - 1],
                b_sem.at[1, l, d - 1],
                place.in_row(d),
            )
    for l in order:
        total = own[l, row].astype(f32) + got_a[l, row].astype(f32)
        for d in range(1, n_row):
            copies_b[l, d].wait_recv()
            total += got_b[l, d - 1].astype(f32)
        out_c[l, 0:valid, :] = total.astype(bf16)
        for d in range(1, n_far):
            copies_c[l, d] = send(
                part(out_c, l, place.far_at(d)),
                got_c.at[l, d - 1],
                c_sem.at[0, l, d - 1],
                c_sem.at[1, l, d - 1],
                place.along(d),
            )
    for l in order:
        total = part(out_c, l, far)[...].astype(f32)
        for d in range(1, n_far):
            copies_c[l, d].wait_recv()
            total += got_c[l, d - 1].astype(f32)
        here = part(final.at[core], l, far)
        here[...] = total.astype(bf16)
        for d in range(1, n_far):
            copies_d[l, d] = send(
                here, here, d_sem.at[0, l, d - 1], d_sem.at[1, l, d - 1], place.along(d)
            )
        copies_e[l, 0] = send(here, here, e_sem.at[0, l, 0], e_sem.at[1, l, 0], place.twin())
    for l in order:
        for d in range(1, n_far):
            copies_d[l, d].wait_recv()
            here = part(final.at[core], l, place.far_at(n_far - d))
            copies_e[l, d] = send(here, here, e_sem.at[0, l, d], e_sem.at[1, l, d], place.twin())
    for copies in (copies_a, copies_b, copies_c, copies_d):
        for copy in copies.values():
            copy.wait_send()
    for copy in copies_e.values():
        copy.wait()
    done = pltpu.make_async_copy(final, out_ref, out_sem)
    done.start()
    done.wait()


def sum_gradients(one, two):
    n_row, n_far = lax.axis_size("row"), lax.axis_size("clip") // 2
    valid, piece = packed_rows(n_row), piece_rows(n_row, n_far)
    final = (2, 2, n_far * piece, D)
    dma = pltpu.SemaphoreType.DMA
    return pl.pallas_call(
        functools.partial(sum_kernel, n_row, n_far),
        in_specs=[pl.BlockSpec(memory_space=pl.ANY)] * 2,
        out_specs=pl.BlockSpec(memory_space=pl.ANY),
        out_shape=jax.ShapeDtypeStruct(final, bf16),
        scratch_shapes=[
            pltpu.VMEM((2, n_row, valid, D), bf16),
            pltpu.VMEM((2, n_row, valid, D), bf16),
            pltpu.VMEM((2, n_row, valid, D), bf16),
            pltpu.VMEM((2, n_row - 1, valid, D), bf16),
            pltpu.VMEM((2, n_far * piece, D), bf16),
            pltpu.VMEM((2, n_far - 1, piece, D), bf16),
            pltpu.VMEM(final, bf16),
            dma((2,)),
            dma((2, 2)),
            dma((2, 2, n_row - 1)),
            dma((2, 2, n_far - 1)),
            dma((2, 2, n_far - 1)),
            dma((2, 2, n_far)),
            dma,
        ],
        compiler_params=pltpu.CompilerParams(
            collective_id=1, has_side_effects=True, vmem_limit_bytes=VMEM_LIMIT
        ),
        name="sum_gradients",
    )(one, two)


def unpack_kernel(
    n_row, packed_ref, qkv_o, qvb_o, proj_o, projb_o, fc1_o, fc1b_o, fc2_o, fc2b_o, gain_o, shift_o, table_o
):
    row = lax.axis_index("row")
    size = D // n_row
    lane = lax.broadcasted_iota(jnp.int32, (D, size), 0)
    want = lax.broadcasted_iota(jnp.int32, (D, size), 1)
    pick = jnp.where(lane == want + size * row, 1.0, 0.0).astype(bf16)
    start = 4 * size * row
    lane = lax.broadcasted_iota(jnp.int32, (D, 4 * size), 0)
    want = lax.broadcasted_iota(jnp.int32, (D, 4 * size), 1)
    pick_fc1 = jnp.where(lane == want + start % D, 1.0, 0.0).astype(bf16)
    spot = lax.broadcasted_iota(jnp.int32, (16, 4 * size), 0)
    a = lax.broadcasted_iota(jnp.int32, (HEADS, HEADS), 0)
    b = lax.broadcasted_iota(jnp.int32, (HEADS, HEADS), 1)
    same = jnp.where(a == b, 1.0, 0.0).astype(bf16)
    for layer in range(2):
        for j in range(3):
            qkv_o[layer, :, D * j : D * (j + 1)] = packed_ref[
                0, layer, size * j : size * (j + 1), :
            ].astype(f32)
        proj_o[layer] = packed_ref[0, layer, size * 3 : size * 4, :].astype(f32)
        for j in range(4):
            fc1_o[layer, :, D * j : D * (j + 1)] = packed_ref[
                1, layer, size * j : size * (j + 1), :
            ].astype(f32)
        for half in range(2):
            fc2_o[layer, 2 * size * half : 2 * size * (half + 1), :] = packed_ref[
                half, layer, size * 4 : size * 6, :
            ].astype(f32)
        vectors = packed_ref[0, layer, size * 6 : size * 6 + 16, :]
        mine = dot_nn(vectors, pick)
        qvb_o[layer] = mine[0:2]
        projb_o[layer : layer + 1] = mine[2:3]
        fc2b_o[layer : layer + 1] = mine[3:4]
        gain_o[layer] = mine[4:6]
        shift_o[layer] = mine[6:8]
        mine = dot_nn(vectors, pick_fc1)
        fc1b_o[layer : layer + 1] = column_sum(jnp.where(spot == 8 + start // D, mine, 0.0))
        table = packed_ref[1, layer, size * 6 : size * 6 + 16, 0:TABLE_PAD]
        table_o[layer] = dot_tn(table, same)[0:TABLE, :]


def unpack_gradients(packed):
    n_row = lax.axis_size("row")
    size = D // n_row
    shapes = [
        (2, size, 3 * D),
        (2, 2, size),
        (2, size, D),
        (2, size),
        (2, size, 4 * D),
        (2, 4 * size),
        (2, 4 * size, D),
        (2, size),
        (2, 2, size),
        (2, 2, size),
        (2, TABLE, HEADS),
    ]
    return pl.pallas_call(
        functools.partial(unpack_kernel, n_row),
        out_shape=[jax.ShapeDtypeStruct(shape, f32) for shape in shapes],
        compiler_params=pltpu.CompilerParams(vmem_limit_bytes=VMEM_LIMIT),
        name="unpack_gradients",
    )(packed)


def gather_kernel(n_row, n_far, qkv_i, proj_i, fc1_i, fc2_i, vec_i, *refs):
    outs = (refs[0:4], refs[4:8])
    vec_o, own_sem, row_sem, twin_sem, vec_sem = refs[8:]
    place = Place(n_row, n_far)
    row = place.row
    size = D // n_row
    shards = (qkv_i, proj_i, fc1_i, fc2_i)
    heights = (size, size, size, 4 * size)
    halves = (
        ((0, 0, size), (1, 0, size), (3, 0, 2 * size)),
        ((2, 0, size), (3, 2 * size, 2 * size)),
    )

    def spot(layer, weight, owner, first, count):
        at = pl.multiple_of(owner * heights[weight] + first, 16)
        return outs[layer][weight].at[pl.ds(at, count), :]

    local = [
        pltpu.make_async_copy(
            shards[w].at[l], spot(l, w, row, 0, heights[w]), own_sem.at[l, w]
        )
        for l in range(2)
        for w in range(4)
    ]
    local.append(pltpu.make_async_copy(vec_i, vec_o.at[row], own_sem.at[2, 0]))
    for copy in local:
        copy.start()
    meet(place.partners(far=False))
    vecs = [
        send(vec_i, vec_o.at[row], vec_sem.at[0, d - 1], vec_sem.at[1, d - 1], place.in_row(d))
        for d in range(1, n_row)
    ]
    for core in range(2):

        @pl.when(place.core == core)
        def _():
            pushes, handed = {}, []
            for l in range(2):
                for i, (w, first, count) in enumerate(halves[core]):
                    for d in range(1, n_row):
                        pushes[l, i, d] = send(
                            shards[w].at[l, pl.ds(first, count), :],
                            spot(l, w, row, first, count),
                            row_sem.at[0, l, i, d - 1],
                            row_sem.at[1, l, i, d - 1],
                            place.in_row(d),
                        )
            for l in range(2):
                for i, (w, first, count) in enumerate(halves[core]):
                    for d in range(1, n_row):
                        pushes[l, i, d].wait_recv()
                        here = spot(l, w, place.row_at(n_row - d), first, count)
                        handed.append(
                            send(
                                here,
                                here,
                                twin_sem.at[0, l, i, d - 1],
                                twin_sem.at[1, l, i, d - 1],
                                place.twin(),
                            )
                        )
            for copy in list(pushes.values()) + handed:
                copy.wait_send()
            for l in range(2):
                for i, (w, first, count) in enumerate(halves[1 - core]):
                    for d in range(1, n_row):
                        here = spot(l, w, place.row_at(n_row - d), first, count)
                        pltpu.make_async_remote_copy(
                            src_ref=here,
                            dst_ref=here,
                            send_sem=twin_sem.at[0, l, i, d - 1],
                            recv_sem=twin_sem.at[1, l, i, d - 1],
                            device_id=place.twin(),
                            device_id_type=MESH,
                        ).wait_recv()

    for copy in vecs:
        copy.wait()
    for copy in local:
        copy.wait()


def gather_weights(qkv, proj, fc1, fc2, vectors):
    n_row, n_far = lax.axis_size("row"), lax.axis_size("clip") // 2
    full = [
        jax.ShapeDtypeStruct((shard.shape[1] * n_row, shard.shape[2]), bf16)
        for shard in (qkv, proj, fc1, fc2)
    ]
    dma = pltpu.SemaphoreType.DMA
    *weights, gathered = pl.pallas_call(
        functools.partial(gather_kernel, n_row, n_far),
        in_specs=[pl.BlockSpec(memory_space=pl.ANY)] * 5,
        out_specs=[pl.BlockSpec(memory_space=pl.ANY)] * 9,
        out_shape=full + full + [jax.ShapeDtypeStruct((n_row, *vectors.shape), bf16)],
        scratch_shapes=[
            dma((3, 4)),
            dma((2, 2, 3, n_row - 1)),
            dma((2, 2, 3, n_row - 1)),
            dma((2, n_row - 1)),
        ],
        compiler_params=pltpu.CompilerParams(collective_id=0, has_side_effects=True),
        name="gather_weights",
    )(qkv, proj, fc1, fc2, vectors)
    return weights[:4], weights[4:], gathered


def shifted_rows(value, steps):
    count = lax.axis_size("row")
    pairs = [(source, (source + steps) % count) for source in range(count)]
    return lax.ppermute(value, "row", pairs)


def edge_rows(values, first_window, first_sub):
    shaped = values.reshape(-1, CELL, values.shape[-1])
    part = shaped[first_window : first_window + WIN_COLS, first_sub * BLOCK : (first_sub + 2) * BLOCK]
    return part.reshape(-1, values.shape[-1]).astype(bf16)


def exchange(values):
    return lax.all_to_all(values, ("clip", "row"), split_axis=0, concat_axis=0, tiled=True)


def body(
    inputs,
    cotangent,
    source_of,
    split_row,
    qkv_weight,
    qv_bias,
    proj_weight,
    proj_bias,
    fc1_weight,
    fc1_bias,
    fc2_weight,
    fc2_bias,
    norm_gain,
    norm_bias,
    rel_table,
):
    clip_count = lax.axis_size("clip")
    row_count = lax.axis_size("row")
    tokens = inputs.shape[0]
    block_rows = tokens // (clip_count * row_count)
    grid_rows = tokens // GRID_COLS
    slot_rows = grid_rows * row_count
    window_rows = grid_rows // WIN
    part = D // row_count

    placing = source_of // tokens * block_rows + source_of % block_rows
    placing = placing.reshape(window_rows, 2, SHIFT, WIN_COLS, 2, SHIFT)
    placing = placing.transpose(0, 3, 1, 4, 2, 5).reshape(tokens)
    arrived = exchange(inputs)
    incoming = exchange(cotangent)

    middle = lax.axis_index("row") * grid_rows + WIN * (1 + jnp.arange(window_rows))
    row_cut = ((middle == split_row[0]) | (middle == slot_rows)).astype(jnp.int32)
    col_cut = (jnp.arange(WIN_COLS) == WIN_COLS - 1).astype(jnp.int32)
    cuts = (32 * row_cut[:, None] + 16 * col_cut[None, :]).reshape(-1)

    vectors = jnp.concatenate(
        [
            qv_bias,
            proj_bias[:, None],
            fc2_bias[:, None],
            norm_gain,
            norm_bias,
            fc1_bias.reshape(2, -1, part),
        ],
        axis=1,
    )
    vectors = jnp.pad(vectors, ((0, 0), (0, 4), (0, 128 - part))).reshape(32, 128)
    full_one, full_two, vectors = gather_weights(
        qkv_weight, proj_weight, fc1_weight, fc2_weight, vectors
    )
    vectors = vectors.reshape(row_count, 2, 16, 128)[:, :, :, :part]
    ff = fc1_weight.shape[2]
    fc1_row = vectors[:, :, 8:12].transpose(1, 0, 2, 3).reshape(2, 1, ff).astype(f32)
    vec_rows = vectors[:, :, :8].transpose(1, 2, 0, 3).reshape(2, 8, D).astype(f32)
    qkv_row = jnp.concatenate(
        [vec_rows[:, 0:1], jnp.zeros((2, 1, D), f32), vec_rows[:, 1:2]], axis=2
    )
    weights = [
        (*full, vec_rows[layer], qkv_row[layer], fc1_row[layer])
        for layer, full in enumerate((full_one, full_two))
    ]
    bias = bias_tables(rel_table)

    *saved_one, layer_one = forward_layer(
        0, cuts, placing.reshape(tokens, 1), arrived, weights[0], bias[0], f32
    )
    incoming = place_rows(placing.reshape(tokens, 1), incoming)
    ahead = shifted_rows(edge_rows(layer_one, 0, 0), -1)
    ahead_grad = shifted_rows(edge_rows(incoming, 0, 0), -1)
    *saved_two, layer_two = forward_layer(1, cuts, layer_one, ahead, weights[1], bias[1], bf16)
    last = (window_rows - 1) * WIN_COLS
    behind = shifted_rows(edge_rows(layer_two, last, 2), 1)
    out_rows = unplace_rows(placing.reshape(1, tokens), layer_two, behind)
    output = exchange(out_rows)
    grad_two, packed_two = backward_layer(1, incoming, ahead_grad, saved_two, weights[1], f32)
    behind_grad = shifted_rows(edge_rows(grad_two, last, 2), 1)
    grad_one, packed_one = backward_layer(0, grad_two, behind_grad, saved_one, weights[0], bf16)
    grad_rows = unplace_plain(placing.reshape(1, tokens), grad_one)
    input_grad = exchange(grad_rows).astype(f32)

    totals = unpack_gradients(sum_gradients(packed_one, packed_two))
    return (output, input_grad, *totals)


def unplace_plain_kernel(place_ref, rows_ref, out_ref):
    tokens = rows_ref.shape[0]
    spots = lax.broadcasted_iota(jnp.int32, (CHUNK, tokens), 0) + pl.program_id(0) * CHUNK
    pick = jnp.where(spots == place_ref[...], 1.0, 0.0).astype(bf16)
    out_ref[...] = dot_nn(pick, rows_ref[...]).astype(out_ref.dtype)


def unplace_plain(place, rows):
    tokens, width = rows.shape
    return pl.pallas_call(
        unplace_plain_kernel,
        grid=(tokens // CHUNK,),
        in_specs=[whole((1, tokens)), whole((tokens, width))],
        out_specs=rows_of((CHUNK, width)),
        out_shape=jax.ShapeDtypeStruct((tokens, width), bf16),
        name="unplace_plain",
    )(place, rows)


def solution(mesh):
    placed = (
        P(("clip", "row"), None),
        P(("clip", "row"), None),
        P(("clip", "row")),
        P("clip"),
        P(None, "row", None),
        P(None, None, "row"),
        P(None, "row", None),
        P(None, "row"),
        P(None, "row", None),
        P(None, "row"),
        P(None, "row", None),
        P(None, "row"),
        P(None, None, "row"),
        P(None, None, "row"),
        P(),
    )
    return jax.shard_map(
        body,
        mesh=mesh,
        in_specs=placed,
        out_specs=(
            P(("clip", "row"), None),
            P(("clip", "row"), None),
            P(None, "row", None),
            P(None, None, "row"),
            P(None, "row", None),
            P(None, "row"),
            P(None, "row", None),
            P(None, "row"),
            P(None, "row", None),
            P(None, "row"),
            P(None, None, "row"),
            P(None, None, "row"),
            P(),
        ),
        check_vma=False,
    )
```

```python
import functools

import jax
import jax.numpy as jnp
import numpy as np
from jax import lax
from jax.experimental import pallas as pl
from jax.experimental.pallas import tpu as pltpu
from jax.sharding import PartitionSpec as P

WIN = 8
SHIFT = 4
GRID_COLS = 64
EPSILON = 1e-05
MASKED = -1000000000.0
ROOT_HALF = 0.7071067811865476
INV_ROOT_TAU = 0.3989422804014327

HEADS = 16
HEAD_DIM = 24
D = HEADS * HEAD_DIM
GROUP = 8
CELL = WIN * WIN
BLOCK = SHIFT * SHIFT
WIN_COLS = GRID_COLS // WIN
SPREAD = 2 * WIN - 1
TABLE = SPREAD * SPREAD
TABLE_PAD = 256
SCALE = HEAD_DIM**-0.5
CHUNK = 256
CHUNK_WINS = CHUNK // CELL
VMEM_LIMIT = 56 * 1024 * 1024

MESH = pl.DeviceIdType.MESH
f32 = jnp.float32
bf16 = jnp.bfloat16


def window_places():
    spot = np.arange(CELL)
    row = (spot // 32) * SHIFT + (spot % BLOCK) // SHIFT
    col = (spot // BLOCK % 2) * SHIFT + spot % SHIFT
    return row, col


def head_masks():
    feature = np.arange(D) // HEAD_DIM
    rows = (feature[None, :] == np.arange(HEADS)[:, None]).astype(np.float32)
    wide = np.stack(
        [
            np.repeat(rows[GROUP * g : GROUP * (g + 1), 128 * g : 128 * g + 256], CELL, axis=0)
            for g in range(2)
        ]
    )
    return rows, wide


def table_constants():
    row, col = window_places()
    natural = row * WIN + col
    lanes = np.zeros((2, TABLE_PAD, 128), np.float32)
    for half in range(2):
        lanes[half, row * SPREAD + col, half * CELL + np.arange(CELL)] = 1.0
    order = np.zeros((CELL, CELL), np.float32)
    order[np.arange(CELL), natural] = 1.0
    back = np.zeros((CELL, CELL), np.float32)
    back[row * WIN + (WIN - 1 - col), np.arange(CELL)] = 1.0
    return lanes, order, back


def dot_nn(a, b):
    return lax.dot_general(a, b, (((1,), (0,)), ((), ())), preferred_element_type=f32)


def dot_nt(a, b):
    return lax.dot_general(a, b, (((1,), (1,)), ((), ())), preferred_element_type=f32)


def dot_tn(a, b):
    return lax.dot_general(a, b, (((0,), (0,)), ((), ())), preferred_element_type=f32)


def dot_exact(a, b, dims):
    return lax.dot_general(
        a, b, (dims, ((), ())), precision=lax.Precision.HIGHEST, preferred_element_type=f32
    )


def split(values):
    high = values.astype(bf16)
    rest = values - high.astype(f32)
    middle = rest.astype(bf16)
    return high, middle, (rest - middle.astype(f32)).astype(bf16)


def whole(shape):
    zeros = (0,) * len(shape)
    return pl.BlockSpec(shape, lambda i: zeros)


def rows_of(shape):
    return pl.BlockSpec(shape, lambda i: (i, 0))


def norm_parts(values):
    centred = values - jnp.mean(values, axis=-1, keepdims=True)
    inverse = lax.rsqrt(jnp.mean(centred * centred, axis=-1, keepdims=True) + EPSILON)
    return centred * inverse, inverse


def norm_back(upstream, normal, inverse, gain):
    scaled = upstream * gain
    centred = scaled - jnp.mean(scaled, axis=-1, keepdims=True)
    return inverse * (centred - normal * jnp.mean(scaled * normal, axis=-1, keepdims=True))


def column_sum(values):
    return jnp.sum(values, axis=0, keepdims=True)


def bias_rows(table_ref, lanes_ref, order_ref, out_ref, wide_ref):
    for layer in range(2):
        for head in range(HEADS):
            pair, half = divmod(head, 2)
            spread = jnp.broadcast_to(table_ref[layer, head : head + 1, :], (WIN, TABLE_PAD))
            for i in range(WIN):
                at = CELL * pair + WIN * i
                wide_ref[at : at + WIN, TABLE_PAD * half : TABLE_PAD * (half + 1)] = pltpu.roll(
                    spread, (SPREAD * i - 112) % TABLE_PAD, 1, stride=1, stride_axis=0
                )
        picked = sum(dot_nn(part, lanes_ref[...]) for part in reversed(split(wide_ref[...])))
        joined = jnp.concatenate(
            [picked[CELL * pair : CELL * (pair + 1), :] for pair in range(HEADS // 2)], axis=1
        )
        out_ref[layer] = sum(dot_nn(order_ref[...], part) for part in reversed(split(joined)))


def table_rows(grad_ref, lanes_ref, back_ref, out_ref):
    for pair in range(HEADS // 2):
        turned = dot_exact(back_ref[...], grad_ref[:, 128 * pair : 128 * (pair + 1)], ((1,), (0,)))
        for half in range(2):
            spread = dot_exact(turned, lanes_ref[half], ((1,), (1,)))
            total = jnp.zeros((WIN, TABLE_PAD), f32)
            for i in range(WIN):
                total += pltpu.roll(
                    spread[WIN * i : WIN * (i + 1), :],
                    (112 - SPREAD * i - (WIN - 1)) % TABLE_PAD,
                    1,
                    stride=1,
                    stride_axis=0,
                )
            out_ref[2 * pair + half : 2 * pair + half + 1, :] = column_sum(total)


def quarter(window, sub):
    return pl.ds(CELL * window + BLOCK * sub, BLOCK)


def assemble_back(main_ref, edge_ref, out_ref):
    windows = main_ref.shape[0] // CELL
    for window in range(windows):
        wr, wc = divmod(window, WIN_COLS)
        before = (wc - 1) % WIN_COLS
        out_ref[quarter(window, 3), :] = main_ref[quarter(window, 0), :].astype(out_ref.dtype)
        out_ref[quarter(window, 2), :] = main_ref[
            quarter(wr * WIN_COLS + before, 1), :
        ].astype(out_ref.dtype)
        for sub, col, piece in ((1, wc, 0), (0, before, 1)):
            if wr == 0:
                value = edge_ref[pl.ds(2 * BLOCK * col + BLOCK * piece, BLOCK), :]
            else:
                value = main_ref[quarter((wr - 1) * WIN_COLS + col, 2 + piece), :]
            out_ref[quarter(window, sub), :] = value.astype(out_ref.dtype)


def assemble_ahead(main_ref, edge_ref, out_ref):
    windows = main_ref.shape[0] // CELL
    last = windows // WIN_COLS - 1
    for window in range(windows):
        wr, wc = divmod(window, WIN_COLS)
        after = (wc + 1) % WIN_COLS
        out_ref[quarter(window, 0), :] = main_ref[quarter(window, 3), :].astype(out_ref.dtype)
        out_ref[quarter(window, 1), :] = main_ref[
            quarter(wr * WIN_COLS + after, 2), :
        ].astype(out_ref.dtype)
        for sub, col, piece in ((2, wc, 1), (3, after, 0)):
            if wr == last:
                value = edge_ref[pl.ds(2 * BLOCK * col + BLOCK * piece, BLOCK), :]
            else:
                value = main_ref[quarter((wr + 1) * WIN_COLS + col, piece), :]
            out_ref[quarter(window, sub), :] = value.astype(out_ref.dtype)


def packed_rows(n_row):
    return 6 * (D // n_row) + 16


def piece_rows(n_row, n_far):
    return -(-packed_rows(n_row) // (16 * n_far)) * 16


class Place:
    def __init__(self, n_row, n_far):
        clip = lax.axis_index("clip")
        self.n_row, self.n_far = n_row, n_far
        self.core, self.far, self.row = clip % 2, clip // 2, lax.axis_index("row")
        self.n = 2 * n_far * n_row
        self.index = clip * n_row + self.row

    def index_at(self, d):
        return (self.index + d) % self.n

    def device(self, d):
        at = self.index_at(d)
        return (at // self.n_row, at % self.n_row)

    def row_at(self, d):
        return (self.row + d) % self.n_row

    def far_at(self, d):
        return (self.far + d) % self.n_far

    def twin(self):
        return (2 * self.far + 1 - self.core, self.row)

    def in_row(self, d):
        return (2 * self.far + self.core, self.row_at(d))

    def along(self, d):
        return (2 * self.far_at(d) + self.core, self.row)

    def partners(self, far=True):
        found = [self.twin()] + [self.in_row(d) for d in range(1, self.n_row)]
        return found + ([self.along(d) for d in range(1, self.n_far)] if far else [])


def meet(partners):
    barrier = pltpu.get_barrier_semaphore()
    for partner in partners:
        pl.semaphore_signal(barrier, inc=1, device_id=partner, device_id_type=MESH)
    pl.semaphore_wait(barrier, len(partners))


def send(src, dst, send_sem, recv_sem, target):
    copy = pltpu.make_async_remote_copy(
        src_ref=src,
        dst_ref=dst,
        send_sem=send_sem,
        recv_sem=recv_sem,
        device_id=target,
        device_id_type=MESH,
    )
    copy.start()
    return copy


def remote(src, dst, send_sem, recv_sem, target):
    return pltpu.make_async_remote_copy(
        src_ref=src,
        dst_ref=dst,
        send_sem=send_sem,
        recv_sem=recv_sem,
        device_id=target,
        device_id_type=MESH,
    )


def can_swap(tokens, n):
    return tokens // n % 16 == 0


def meet_all(place):
    barrier = pltpu.get_barrier_semaphore()

    def greet(d, carry):
        pl.semaphore_signal(barrier, inc=1, device_id=place.device(d), device_id_type=MESH)
        return carry

    lax.fori_loop(1, place.n, greet, 0)
    pl.semaphore_wait(barrier, place.n - 1)


def swap_block(place, ref, index):
    count = ref.shape[0] // place.n
    return ref.at[pl.ds(pl.multiple_of(index * count, 16), count), :]


def swap_own(place, src, dst, sem):
    return pltpu.make_async_copy(
        swap_block(place, src, place.index), swap_block(place, dst, place.index), sem.at[0, 0]
    )


def swap_copy(place, src, dst, sem, d, owner):
    return remote(
        swap_block(place, src, place.index_at(d)),
        swap_block(place, dst, owner),
        sem.at[0, d],
        sem.at[1, d],
        place.device(d),
    )


def swap_start(place, src, dst, sem):
    def work(d, carry):
        swap_copy(place, src, dst, sem, d, place.index).start()
        return carry

    lax.fori_loop(1, place.n, work, 0)


def swap_wait(place, src, dst, sem):
    def work(d, carry):
        swap_copy(place, src, dst, sem, d, place.index_at(place.n - d)).wait_recv()
        return carry

    lax.fori_loop(1, place.n, work, 0)


def swap_end(place, src, dst, sem):
    def work(d, carry):
        swap_copy(place, src, dst, sem, d, place.index).wait_send()
        return carry

    lax.fori_loop(1, place.n, work, 0)


def row_share(n_row):
    return D // n_row


HALVES = (((0, 0, 1), (1, 0, 1), (3, 0, 2)), ((2, 0, 1), (3, 2, 2)))
HEIGHTS = (1, 1, 1, 4)


def forward_kernel(
    n_row,
    n_far,
    swap,
    cuts_ref,
    place_col,
    place_row,
    x_in,
    c_in,
    qkv_i,
    proj_i,
    fc1_i,
    fc2_i,
    vec_i,
    table_ref,
    lanes_ref,
    order_ref,
    heads_ref,
    wide_heads_ref,
    x_out,
    qkv_out,
    prob_out,
    att_out,
    mid_out,
    act_out,
    slope_out,
    up_out,
    rows_out,
    qkv_wo,
    proj_wo,
    fc1_wo,
    fc2_wo,
    vec_out,
    x_got,
    c_got,
    qkv_s,
    proj_s,
    fc1_s,
    fc2_s,
    vec_got,
    qkv_b,
    fc1_b,
    bias_s,
    wide_s,
    x_s,
    y_s,
    c_s,
    edge_out,
    edge_in,
    x_sem,
    c_sem,
    own_sem,
    row_sem,
    twin_sem,
    vec_sem,
    edge_sem,
    out_sem,
):
    step = pl.program_id(0)
    tokens = x_s.shape[0]
    chunks = tokens // CHUNK
    layer = step // chunks
    chunk = (step + layer * (chunks // 2)) % chunks
    place = Place(n_row, n_far)
    size = row_share(n_row)
    shards = (qkv_i, proj_i, fc1_i, fc2_i)
    kept = (qkv_s, proj_s, fc1_s, fc2_s)
    outs = (qkv_wo, proj_wo, fc1_wo, fc2_wo)
    last_row = (tokens // CELL // WIN_COLS - 1) * WIN_COLS
    if not swap:
        x_got, c_got = x_in, c_in

    def own(l, w):
        return pltpu.make_async_copy(
            shards[w].at[l], spot(l, w, place.row, 0, HEIGHTS[w]), own_sem.at[l, w]
        )

    def spot(l, w, owner, first, count):
        at = pl.multiple_of((owner * HEIGHTS[w] + first) * size, 16)
        return kept[w].at[l, pl.ds(at, count * size), :]

    def push(l, core, i, d, source=None):
        w, first, count = HALVES[core][i]
        return remote(
            shards[w].at[l, pl.ds(first * size, count * size), :],
            spot(l, w, place.row if source is None else source, first, count),
            row_sem.at[0, l, i, d - 1],
            row_sem.at[1, l, i, d - 1],
            place.in_row(d),
        )

    def hand(l, core, i, d):
        w, first, count = HALVES[core][i]
        here = spot(l, w, place.row_at(n_row - d), first, count)
        return remote(
            here, here, twin_sem.at[0, l, i, d - 1], twin_sem.at[1, l, i, d - 1], place.twin()
        )

    def pieces(core):
        return [(i, d) for i in range(len(HALVES[core])) for d in range(1, n_row)]

    def by_core(work):
        for core in range(2):
            pl.when(place.core == core)(functools.partial(work, core))

    def start_weights(l):
        def work(core):
            for i, d in pieces(core):
                push(l, core, i, d).start()

        by_core(work)

    def pass_weights(l):
        def work(core):
            for i, d in pieces(core):
                push(l, core, i, d, place.row_at(n_row - d)).wait_recv()
                hand(l, core, i, d).start()

        by_core(work)

    def wait_weights(l):
        def work(core):
            for i, d in pieces(1 - core):
                hand(l, 1 - core, i, d).wait_recv()

        by_core(work)
        for w in range(4):
            own(l, w).wait()

    def end_weights(l):
        def work(core):
            for i, d in pieces(core):
                push(l, core, i, d).wait_send()
                hand(l, core, i, d).wait_send()

        by_core(work)

    def vector_copy(d):
        return remote(
            vec_i, vec_got.at[place.row], vec_sem.at[0, d - 1], vec_sem.at[1, d - 1], place.in_row(d)
        )

    def edge_copy(which, d):
        return remote(
            edge_out.at[which],
            edge_in.at[which],
            edge_sem.at[0, which],
            edge_sem.at[1, which],
            place.in_row(d),
        )

    def pack_edge(which, source, first_window, first_sub):
        for col in range(WIN_COLS):
            at = CELL * (first_window + col) + BLOCK * first_sub
            edge_out[which, 2 * BLOCK * col : 2 * BLOCK * (col + 1), :] = source[
                at : at + 2 * BLOCK, :
            ].astype(bf16)

    def pick_rows(source, target):
        for c in range(chunks):
            rows = slice(CHUNK * c, CHUNK * (c + 1))
            spots = lax.broadcasted_iota(jnp.int32, (CHUNK, tokens), 1)
            pick = jnp.where(spots == place_col[rows, :], 1.0, 0.0).astype(bf16)
            target[rows, :] = dot_nn(pick, source[...]).astype(target.dtype)

    @pl.when(step == 0)
    def _():
        for l in range(2):
            for w in range(4):
                own(l, w).start()
        mine = pltpu.make_async_copy(vec_i, vec_got.at[place.row], out_sem.at[4])
        mine.start()
        if swap:
            swap_own(place, x_in, x_got, x_sem).start()
            swap_own(place, c_in, c_got, c_sem).start()
            meet_all(place)
            swap_start(place, x_in, x_got, x_sem)
        else:
            meet(place.partners(far=False))
        for d in range(1, n_row):
            vector_copy(d).start()
        start_weights(0)
        bias_rows(table_ref, lanes_ref, order_ref, bias_s, wide_s)
        mine.wait()
        for d in range(1, n_row):
            vector_copy(d).wait()
        for l in range(2):
            shares = [vec_got[r, 16 * l : 16 * (l + 1), :].astype(f32) for r in range(n_row)]
            rows = jnp.concatenate([share[0:8, 0:size] for share in shares], axis=1)
            vec_out[l] = rows
            qkv_b[l, 0:1, 0:D] = rows[0:1]
            qkv_b[l, 0:1, D : 2 * D] = jnp.zeros((1, D), f32)
            qkv_b[l, 0:1, 2 * D : 3 * D] = rows[1:2]
            fc1_b[l, 0:1, :] = jnp.concatenate(
                [share[8:9, 0 : 4 * size] for share in shares], axis=1
            )
        if swap:
            swap_wait(place, x_in, x_got, x_sem)
            swap_own(place, x_in, x_got, x_sem).wait()
        pick_rows(x_got, x_s)
        pass_weights(0)
        wait_weights(0)

    @pl.when(step == 1)
    def _():
        start_weights(1)
        if swap:
            swap_start(place, c_in, c_got, c_sem)

    @pl.when(step == chunks - 1)
    def _():
        pass_weights(1)

    @pl.when(step == chunks)
    def _():
        wait_weights(1)
        for w in range(4):
            pltpu.make_async_copy(kept[w], outs[w], out_sem.at[w]).start()
        edge_copy(0, n_row - 1).wait_recv()
        assemble_ahead(y_s, edge_in.at[0], x_s)

    @pl.when(step == chunks + 2)
    def _():
        if swap:
            swap_wait(place, c_in, c_got, c_sem)
            swap_own(place, c_in, c_got, c_sem).wait()
        pick_rows(c_got, c_s)
        pack_edge(2, c_s, 0, 0)
        edge_copy(2, n_row - 1).start()

    here = pl.ds(pl.multiple_of(chunk * CHUNK, CHUNK), CHUNK)
    x = x_s[here, :]
    x_out[0] = x
    normal, _ = norm_parts(x)
    hidden = (normal * vec_out[layer, 4:5, :] + vec_out[layer, 6:7, :]).astype(bf16)
    qkv_out[0] = (dot_nn(hidden, qkv_s[layer]) + qkv_b[layer]).astype(bf16)
    wide = (CELL, GROUP * CELL)
    apart = lax.broadcasted_iota(jnp.int32, wide, 0) ^ lax.broadcasted_iota(jnp.int32, wide, 1)
    for k in range(CHUNK_WINS):
        rows = slice(CELL * k, CELL * (k + 1))
        keep = (apart & cuts_ref[(layer * chunks + chunk) * CHUNK_WINS + k]) == 0
        mixed = []
        for g in range(2):
            q = qkv_out[0, rows, 128 * g : 128 * g + 256]
            key = qkv_out[0, rows, D + 128 * g : D + 128 * g + 256]
            val = qkv_out[0, rows, 2 * D + 128 * g : 2 * D + 128 * g + 256]
            q_wide = jnp.concatenate([q] * GROUP, axis=0) * wide_heads_ref[g]
            lanes = slice(GROUP * CELL * g, GROUP * CELL * (g + 1))
            s = dot_nt(key, q_wide) * SCALE + bias_s[layer, :, lanes]
            s = jnp.where(keep, s, MASKED)
            e = jnp.exp(s - jnp.max(s, axis=0, keepdims=True))
            prob = (e * (1.0 / jnp.sum(e, axis=0, keepdims=True))).astype(bf16)
            prob_out[0, rows, lanes] = prob
            mixed.append(gather_heads(dot_tn(prob, val), heads_ref, g))
        att_out[0, rows, :] = join_groups(*mixed).astype(bf16)
    mid = x + (dot_nn(att_out[0], proj_s[layer]) + vec_out[layer, 2:3, :])
    mid_out[0] = mid
    normal, _ = norm_parts(mid)
    hidden = (normal * vec_out[layer, 5:6, :] + vec_out[layer, 7:8, :]).astype(bf16)
    u = dot_nn(hidden, fc1_s[layer]) + fc1_b[layer]
    cdf = 0.5 * (1.0 + lax.erf(u * ROOT_HALF))
    act_out[0] = (u * cdf).astype(bf16)
    slope_out[0] = (cdf + u * (jnp.exp(-0.5 * u * u) * INV_ROOT_TAU)).astype(bf16)
    y_s[here, :] = mid + (dot_nn(act_out[0], fc2_s[layer]) + vec_out[layer, 3:4, :])

    @pl.when(step == chunks // 2 - 1)
    def _():
        pack_edge(0, y_s, 0, 0)
        edge_copy(0, n_row - 1).start()

    @pl.when(step == chunks + chunks // 2 - 1)
    def _():
        pack_edge(1, y_s, last_row, 2)
        edge_copy(1, 1).start()

    @pl.when(step == 2 * chunks - 1)
    def _():
        edge_copy(2, n_row - 1).wait_recv()
        assemble_ahead(c_s, edge_in.at[2], up_out)
        edge_copy(1, 1).wait_recv()
        assemble_back(y_s, edge_in.at[1], c_s)
        for c in range(chunks):
            rows = slice(CHUNK * c, CHUNK * (c + 1))
            spots = lax.broadcasted_iota(jnp.int32, (CHUNK, tokens), 0) + CHUNK * c
            pick = jnp.where(spots == place_row[...], 1.0, 0.0).astype(bf16)
            rows_out[rows, :] = dot_nn(pick, c_s[...]).astype(bf16)
        for l in range(2):
            end_weights(l)
        for which in range(3):
            edge_copy(which, 1 if which == 1 else n_row - 1).wait_send()
        for w in range(4):
            pltpu.make_async_copy(kept[w], outs[w], out_sem.at[w]).wait()
        if swap:
            swap_end(place, x_in, x_got, x_sem)
            swap_end(place, c_in, c_got, c_sem)


def gather_heads(spread, heads_ref, g):
    total = None
    for h in range(GROUP):
        part = spread[CELL * h : CELL * (h + 1), :] * heads_ref[
            GROUP * g + h : GROUP * g + h + 1, 128 * g : 128 * g + 256
        ]
        total = part if total is None else total + part
    return total


def join_groups(low, high):
    return jnp.concatenate([low[:, :128], low[:, 128:] + high[:, :128], high[:, 128:]], axis=1)


def forward_layers(cuts, placing, x_in, c_in, shards, vectors, rel_table):
    n_row, n_far = lax.axis_size("row"), lax.axis_size("clip") // 2
    tokens = x_in.shape[0]
    chunks = tokens // CHUNK
    swap = can_swap(tokens, n_row * n_far * 2)
    heads, wide = head_masks()
    lanes, order, _ = table_constants()
    table = jnp.pad(rel_table.transpose(0, 2, 1), ((0, 0), (0, 0), (0, TABLE_PAD - TABLE)))
    ff = shards[2].shape[2]
    anywhere = pl.BlockSpec(memory_space=pl.ANY)
    patches = anywhere if swap else whole((tokens, D))
    constants = (
        table,
        jnp.asarray(lanes.reshape(2 * TABLE_PAD, 128), dtype=bf16),
        jnp.asarray(order, dtype=bf16),
        jnp.asarray(heads),
        jnp.asarray(wide, dtype=bf16),
    )
    full = [(2, shard.shape[1] * n_row, shard.shape[2]) for shard in shards]

    def block(i):
        layer = i // chunks
        return layer, (i + layer * (chunks // 2)) % chunks, 0

    saved = [(D, f32), (3 * D, bf16), (HEADS * CELL, bf16), (D, bf16), (D, f32), (ff, bf16), (ff, bf16)]
    dma = pltpu.SemaphoreType.DMA
    n = n_row * n_far * 2
    results = pl.pallas_call(
        functools.partial(forward_kernel, n_row, n_far, swap),
        grid=(2 * chunks,),
        in_specs=[
            pl.BlockSpec(memory_space=pltpu.SMEM),
            whole((tokens, 1)),
            whole((1, tokens)),
            patches,
            patches,
        ]
        + [anywhere] * 5
        + [whole(constant.shape) for constant in constants],
        out_specs=[pl.BlockSpec((1, CHUNK, width), block) for width, _ in saved]
        + [whole((tokens, D))] * 2
        + [anywhere] * 4
        + [whole((2, 8, D))],
        out_shape=[jax.ShapeDtypeStruct((2, tokens, width), kind) for width, kind in saved]
        + [jax.ShapeDtypeStruct((tokens, D), bf16)] * 2
        + [jax.ShapeDtypeStruct(shape, bf16) for shape in full]
        + [jax.ShapeDtypeStruct((2, 8, D), f32)],
        scratch_shapes=[
            pltpu.VMEM((tokens if swap else 16, D), bf16),
            pltpu.VMEM((tokens if swap else 16, D), bf16),
            *[pltpu.VMEM(shape, bf16) for shape in full],
            pltpu.VMEM((n_row, *vectors.shape), bf16),
            pltpu.VMEM((2, 1, 3 * D), f32),
            pltpu.VMEM((2, 1, ff), f32),
            pltpu.VMEM((2, CELL, HEADS * CELL), f32),
            pltpu.VMEM((HEADS // 2 * CELL, 2 * TABLE_PAD), f32),
            pltpu.VMEM((tokens, D), f32),
            pltpu.VMEM((tokens, D), f32),
            pltpu.VMEM((tokens, D), bf16),
            pltpu.VMEM((3, WIN_COLS * 2 * BLOCK, D), bf16),
            pltpu.VMEM((3, WIN_COLS * 2 * BLOCK, D), bf16),
            dma((2, n if swap else 1)),
            dma((2, n if swap else 1)),
            dma((2, 4)),
            dma((2, 2, 3, n_row - 1)),
            dma((2, 2, 3, n_row - 1)),
            dma((2, n_row - 1)),
            dma((2, 3)),
            dma((5,)),
        ],
        compiler_params=pltpu.CompilerParams(
            collective_id=0, has_side_effects=True, vmem_limit_bytes=VMEM_LIMIT
        ),
        name="forward_layers",
    )(cuts, placing.reshape(tokens, 1), placing.reshape(1, tokens), x_in, c_in, *shards, vectors, *constants)
    return results[:7], results[7], results[8], results[9:13], results[13]


def backward_kernel(
    layer,
    main_ref,
    edge_ref,
    x_ref,
    qkv_ref,
    prob_ref,
    att_ref,
    mid_ref,
    act_ref,
    slope_ref,
    qkv_w,
    proj_w,
    fc1_w,
    fc2_w,
    vec_ref,
    heads_ref,
    wide_heads_ref,
    lanes_ref,
    back_ref,
    grad_out,
    packed_out,
    vec_g,
    fc1_bg,
    table_g,
    table_t,
    whole_ref,
    h1_ref,
    dt_ref,
    ga_ref,
    h2_ref,
    du_ref,
    gz_ref,
):
    step = pl.program_id(0)
    here = pl.ds(pl.multiple_of(step * CHUNK, CHUNK), CHUNK)

    @pl.when(step == 0)
    def _():
        if layer == 0:
            assemble_back(main_ref, edge_ref, whole_ref)
        else:
            whole_ref[...] = main_ref[...].astype(f32)
        vec_g[...] = jnp.zeros_like(vec_g)
        fc1_bg[...] = jnp.zeros_like(fc1_bg)
        table_g[...] = jnp.zeros_like(table_g)

    upstream = whole_ref[here, :]
    low = upstream.astype(bf16)
    gz_ref[here, :] = low
    vec_g[3:4, :] += column_sum(low.astype(f32))
    du = (dot_nt(low, fc2_w[...]) * slope_ref[...].astype(f32)).astype(bf16)
    du_ref[here, :] = du
    fc1_bg[...] += column_sum(du.astype(f32))
    dn = dot_nt(du, fc1_w[...])
    normal, inverse = norm_parts(mid_ref[...])
    h2_ref[here, :] = (normal * vec_ref[5:6, :] + vec_ref[7:8, :]).astype(bf16)
    vec_g[5:6, :] += column_sum(dn * normal)
    vec_g[7:8, :] += column_sum(dn)
    mid_grad = upstream + norm_back(dn, normal, inverse, vec_ref[5:6, :])
    low = mid_grad.astype(bf16)
    ga_ref[here, :] = low
    vec_g[2:3, :] += column_sum(low.astype(f32))
    att_grad = dot_nt(low, proj_w[...]).astype(bf16)
    for k in range(CHUNK_WINS):
        rows = slice(CELL * k, CELL * (k + 1))
        there = pl.ds(pl.multiple_of(step * CHUNK + CELL * k, CELL), CELL)
        q_parts, k_parts, v_parts = [], [], []
        for g in range(2):
            q = qkv_ref[rows, 128 * g : 128 * g + 256]
            key = qkv_ref[rows, D + 128 * g : D + 128 * g + 256]
            val = qkv_ref[rows, 2 * D + 128 * g : 2 * D + 128 * g + 256]
            do = att_grad[rows, 128 * g : 128 * g + 256]
            q_wide = jnp.concatenate([q] * GROUP, axis=0) * wide_heads_ref[g]
            do_wide = jnp.concatenate([do] * GROUP, axis=0) * wide_heads_ref[g]
            lanes = slice(GROUP * CELL * g, GROUP * CELL * (g + 1))
            prob_low = prob_ref[rows, lanes]
            prob = prob_low.astype(f32)
            dp = dot_nt(val, do_wide)
            v_parts.append(dot_nn(prob_low, do_wide))
            weighted = prob * dp
            ds = (weighted - prob * column_sum(weighted)).astype(bf16)
            table_g[:, lanes] += ds.astype(f32)
            k_parts.append(dot_nn(ds, q_wide))
            q_parts.append(gather_heads(dot_tn(ds, key), heads_ref, g))
        dt_ref[there, 0:D] = (join_groups(*q_parts) * SCALE).astype(bf16)
        dt_ref[there, D : 2 * D] = (join_groups(*k_parts) * SCALE).astype(bf16)
        dt_ref[there, 2 * D : 3 * D] = join_groups(*v_parts).astype(bf16)
    dt = dt_ref[here, :]
    vec_g[0:1, :] += column_sum(dt[:, 0:D].astype(f32))
    vec_g[1:2, :] += column_sum(dt[:, 2 * D :].astype(f32))
    dn = dot_nt(dt, qkv_w[...])
    normal, inverse = norm_parts(x_ref[...])
    h1_ref[here, :] = (normal * vec_ref[4:5, :] + vec_ref[6:7, :]).astype(bf16)
    vec_g[4:5, :] += column_sum(dn * normal)
    vec_g[6:7, :] += column_sum(dn)
    grad_out[...] = (mid_grad + norm_back(dn, normal, inverse, vec_ref[4:5, :])).astype(
        grad_out.dtype
    )

    @pl.when(step == pl.num_programs(0) - 1)
    def _():
        n_row = packed_out.shape[1]
        size = D // n_row

        def put(half, at, value):
            for r in range(n_row):
                packed_out[half, r, at : at + size, :] = value[size * r : size * (r + 1), :]

        for j in range(3):
            put(0, size * j, dot_tn(h1_ref[...], dt_ref[:, D * j : D * (j + 1)]).astype(bf16))
        put(0, size * 3, dot_tn(att_ref[...], ga_ref[...]).astype(bf16))
        for j in range(4):
            put(1, size * j, dot_tn(h2_ref[...], du_ref[:, D * j : D * (j + 1)]).astype(bf16))
        fc2 = dot_tn(act_ref[...], gz_ref[...]).astype(bf16)
        table_rows(table_g, lanes_ref, back_ref, table_t)
        vectors = jnp.concatenate(
            [vec_g[...]]
            + [fc1_bg[:, D * j : D * (j + 1)] for j in range(4)]
            + [jnp.zeros((4, D), f32)],
            axis=0,
        ).astype(bf16)
        table = jnp.concatenate(
            [table_t[...], jnp.zeros((HEADS, D - TABLE_PAD), f32)], axis=1
        ).astype(bf16)
        for r in range(n_row):
            for half in range(2):
                at = (2 * r + half) * 2 * size
                packed_out[half, r, 4 * size : 6 * size, :] = fc2[at : at + 2 * size, :]
            packed_out[0, r, 6 * size :, :] = vectors
            packed_out[1, r, 6 * size :, :] = table


def backward_layer(layer, main, edge, saved, weights, vec, grad_dtype):
    x, qkv, prob, att, mid, act, slope = saved
    qkv_w, proj_w, fc1_w, fc2_w = weights
    heads, wide = head_masks()
    lanes, _, back = table_constants()
    n_row = lax.axis_size("row")
    packed = (2, n_row, packed_rows(n_row), D)
    tokens = main.shape[0]
    ff = fc1_w.shape[1]
    specs = [
        whole(main.shape),
        whole(edge.shape),
        rows_of((CHUNK, D)),
        rows_of((CHUNK, 3 * D)),
        rows_of((CHUNK, HEADS * CELL)),
        whole(att.shape),
        rows_of((CHUNK, D)),
        whole(act.shape),
        rows_of((CHUNK, ff)),
    ]
    operands = (
        qkv_w,
        proj_w,
        fc1_w,
        fc2_w,
        vec,
        jnp.asarray(heads),
        jnp.asarray(wide, dtype=bf16),
        jnp.asarray(lanes),
        jnp.asarray(back),
    )
    outs = [
        ((tokens, D), grad_dtype, rows_of((CHUNK, D))),
        (packed, bf16, whole(packed)),
    ]
    return pl.pallas_call(
        functools.partial(backward_kernel, layer),
        grid=(tokens // CHUNK,),
        in_specs=specs + [whole(operand.shape) for operand in operands],
        out_specs=[spec for _, _, spec in outs],
        out_shape=[jax.ShapeDtypeStruct(shape, dtype) for shape, dtype, _ in outs],
        scratch_shapes=[
            pltpu.VMEM(vec.shape, f32),
            pltpu.VMEM((1, ff), f32),
            pltpu.VMEM((CELL, HEADS * CELL), f32),
            pltpu.VMEM((HEADS, TABLE_PAD), f32),
            pltpu.VMEM((tokens, D), f32),
            pltpu.VMEM((tokens, D), bf16),
            pltpu.VMEM((tokens, 3 * D), bf16),
            pltpu.VMEM((tokens, D), bf16),
            pltpu.VMEM((tokens, D), bf16),
            pltpu.VMEM((tokens, ff), bf16),
            pltpu.VMEM((tokens, D), bf16),
        ],
        compiler_params=pltpu.CompilerParams(vmem_limit_bytes=VMEM_LIMIT),
        name=f"backward_{layer}",
    )(main, edge, x, qkv, prob, att, mid, act, slope, *operands)


def sum_kernel(
    n_row,
    n_far,
    one_ref,
    two_ref,
    out_ref,
    own,
    got_a,
    out_b,
    got_b,
    out_c,
    got_c,
    final,
    own_sem,
    a_sem,
    b_sem,
    c_sem,
    d_sem,
    e_sem,
    out_sem,
):
    place = Place(n_row, n_far)
    core, row, far = place.core, place.row, place.far
    piece = got_c.shape[2]
    valid = own.shape[2]

    def part(ref, layer, at):
        return ref.at[layer, pl.ds(pl.multiple_of(at * piece, 16), piece), :]

    order = (1, 0)
    refs = (one_ref, two_ref)
    mine = [pltpu.make_async_copy(refs[l].at[core], own.at[l], own_sem.at[l]) for l in range(2)]
    for l in order:
        mine[l].start()
    meet(place.partners())
    copies_a, copies_b, copies_c, copies_d, copies_e = {}, {}, {}, {}, {}
    for l in order:
        copies_a[l] = send(
            refs[l].at[1 - core], got_a.at[l], a_sem.at[0, l], a_sem.at[1, l], place.twin()
        )
    if n_far * piece > valid:
        out_c[:, valid:, :] = jnp.zeros((2, n_far * piece - valid, D), bf16)
    for l in order:
        mine[l].wait()
        copies_a[l].wait_recv()
        for d in range(1, n_row):
            r = place.row_at(d)
            out_b[l, r] = own[l, r] + got_a[l, r]
            copies_b[l, d] = send(
                out_b.at[l, r],
                got_b.at[l, d - 1],
                b_sem.at[0, l, d - 1],
                b_sem.at[1, l, d - 1],
                place.in_row(d),
            )
    for l in order:
        total = own[l, row].astype(f32) + got_a[l, row].astype(f32)
        for d in range(1, n_row):
            copies_b[l, d].wait_recv()
            total += got_b[l, d - 1].astype(f32)
        out_c[l, 0:valid, :] = total.astype(bf16)
        for d in range(1, n_far):
            copies_c[l, d] = send(
                part(out_c, l, place.far_at(d)),
                got_c.at[l, d - 1],
                c_sem.at[0, l, d - 1],
                c_sem.at[1, l, d - 1],
                place.along(d),
            )
    for l in order:
        total = part(out_c, l, far)[...].astype(f32)
        for d in range(1, n_far):
            copies_c[l, d].wait_recv()
            total += got_c[l, d - 1].astype(f32)
        here = part(final.at[core], l, far)
        here[...] = total.astype(bf16)
        for d in range(1, n_far):
            copies_d[l, d] = send(
                here, here, d_sem.at[0, l, d - 1], d_sem.at[1, l, d - 1], place.along(d)
            )
        copies_e[l, 0] = send(here, here, e_sem.at[0, l, 0], e_sem.at[1, l, 0], place.twin())
    for l in order:
        for d in range(1, n_far):
            copies_d[l, d].wait_recv()
            here = part(final.at[core], l, place.far_at(n_far - d))
            copies_e[l, d] = send(here, here, e_sem.at[0, l, d], e_sem.at[1, l, d], place.twin())
    for copies in (copies_a, copies_b, copies_c, copies_d):
        for copy in copies.values():
            copy.wait_send()
    for copy in copies_e.values():
        copy.wait()
    done = pltpu.make_async_copy(final, out_ref, out_sem)
    done.start()
    done.wait()


def sum_gradients(one, two):
    n_row, n_far = lax.axis_size("row"), lax.axis_size("clip") // 2
    valid, piece = packed_rows(n_row), piece_rows(n_row, n_far)
    final = (2, 2, n_far * piece, D)
    dma = pltpu.SemaphoreType.DMA
    return pl.pallas_call(
        functools.partial(sum_kernel, n_row, n_far),
        in_specs=[pl.BlockSpec(memory_space=pl.ANY)] * 2,
        out_specs=pl.BlockSpec(memory_space=pl.ANY),
        out_shape=jax.ShapeDtypeStruct(final, bf16),
        scratch_shapes=[
            pltpu.VMEM((2, n_row, valid, D), bf16),
            pltpu.VMEM((2, n_row, valid, D), bf16),
            pltpu.VMEM((2, n_row, valid, D), bf16),
            pltpu.VMEM((2, n_row - 1, valid, D), bf16),
            pltpu.VMEM((2, n_far * piece, D), bf16),
            pltpu.VMEM((2, n_far - 1, piece, D), bf16),
            pltpu.VMEM(final, bf16),
            dma((2,)),
            dma((2, 2)),
            dma((2, 2, n_row - 1)),
            dma((2, 2, n_far - 1)),
            dma((2, 2, n_far - 1)),
            dma((2, 2, n_far)),
            dma,
        ],
        compiler_params=pltpu.CompilerParams(
            collective_id=1, has_side_effects=True, vmem_limit_bytes=VMEM_LIMIT
        ),
        name="sum_gradients",
    )(one, two)


def unpack_kernel(
    n_row, packed_ref, qkv_o, qvb_o, proj_o, projb_o, fc1_o, fc1b_o, fc2_o, fc2b_o, gain_o, shift_o, table_o
):
    row = lax.axis_index("row")
    size = D // n_row
    lane = lax.broadcasted_iota(jnp.int32, (D, size), 0)
    want = lax.broadcasted_iota(jnp.int32, (D, size), 1)
    pick = jnp.where(lane == want + size * row, 1.0, 0.0).astype(bf16)
    start = 4 * size * row
    lane = lax.broadcasted_iota(jnp.int32, (D, 4 * size), 0)
    want = lax.broadcasted_iota(jnp.int32, (D, 4 * size), 1)
    pick_fc1 = jnp.where(lane == want + start % D, 1.0, 0.0).astype(bf16)
    spot = lax.broadcasted_iota(jnp.int32, (16, 4 * size), 0)
    a = lax.broadcasted_iota(jnp.int32, (HEADS, HEADS), 0)
    b = lax.broadcasted_iota(jnp.int32, (HEADS, HEADS), 1)
    same = jnp.where(a == b, 1.0, 0.0).astype(bf16)
    for layer in range(2):
        for j in range(3):
            qkv_o[layer, :, D * j : D * (j + 1)] = packed_ref[
                0, layer, size * j : size * (j + 1), :
            ].astype(f32)
        proj_o[layer] = packed_ref[0, layer, size * 3 : size * 4, :].astype(f32)
        for j in range(4):
            fc1_o[layer, :, D * j : D * (j + 1)] = packed_ref[
                1, layer, size * j : size * (j + 1), :
            ].astype(f32)
        for half in range(2):
            fc2_o[layer, 2 * size * half : 2 * size * (half + 1), :] = packed_ref[
                half, layer, size * 4 : size * 6, :
            ].astype(f32)
        vectors = packed_ref[0, layer, size * 6 : size * 6 + 16, :]
        mine = dot_nn(vectors, pick)
        qvb_o[layer] = mine[0:2]
        projb_o[layer : layer + 1] = mine[2:3]
        fc2b_o[layer : layer + 1] = mine[3:4]
        gain_o[layer] = mine[4:6]
        shift_o[layer] = mine[6:8]
        mine = dot_nn(vectors, pick_fc1)
        fc1b_o[layer : layer + 1] = column_sum(jnp.where(spot == 8 + start // D, mine, 0.0))
        table = packed_ref[1, layer, size * 6 : size * 6 + 16, 0:TABLE_PAD]
        table_o[layer] = dot_tn(table, same)[0:TABLE, :]


def unpack_gradients(packed):
    n_row = lax.axis_size("row")
    size = D // n_row
    shapes = [
        (2, size, 3 * D),
        (2, 2, size),
        (2, size, D),
        (2, size),
        (2, size, 4 * D),
        (2, 4 * size),
        (2, 4 * size, D),
        (2, size),
        (2, 2, size),
        (2, 2, size),
        (2, TABLE, HEADS),
    ]
    return pl.pallas_call(
        functools.partial(unpack_kernel, n_row),
        out_shape=[jax.ShapeDtypeStruct(shape, f32) for shape in shapes],
        compiler_params=pltpu.CompilerParams(vmem_limit_bytes=VMEM_LIMIT),
        name="unpack_gradients",
    )(packed)


def shifted_rows(value, steps):
    count = lax.axis_size("row")
    pairs = [(source, (source + steps) % count) for source in range(count)]
    return lax.ppermute(value, "row", pairs)


def edge_rows(values, first_window, first_sub):
    shaped = values.reshape(-1, CELL, values.shape[-1])
    part = shaped[first_window : first_window + WIN_COLS, first_sub * BLOCK : (first_sub + 2) * BLOCK]
    return part.reshape(-1, values.shape[-1]).astype(bf16)


def exchange(values):
    return lax.all_to_all(values, ("clip", "row"), split_axis=0, concat_axis=0, tiled=True)


def body(
    inputs,
    cotangent,
    source_of,
    split_row,
    qkv_weight,
    qv_bias,
    proj_weight,
    proj_bias,
    fc1_weight,
    fc1_bias,
    fc2_weight,
    fc2_bias,
    norm_gain,
    norm_bias,
    rel_table,
):
    clip_count = lax.axis_size("clip")
    row_count = lax.axis_size("row")
    tokens = inputs.shape[0]
    block_rows = tokens // (clip_count * row_count)
    grid_rows = tokens // GRID_COLS
    slot_rows = grid_rows * row_count
    window_rows = grid_rows // WIN
    part = D // row_count

    placing = source_of // tokens * block_rows + source_of % block_rows
    placing = placing.reshape(window_rows, 2, SHIFT, WIN_COLS, 2, SHIFT)
    placing = placing.transpose(0, 3, 1, 4, 2, 5).reshape(tokens)
    middle = lax.axis_index("row") * grid_rows + WIN * (1 + jnp.arange(window_rows))
    row_cut = ((middle == split_row[0]) | (middle == slot_rows)).astype(jnp.int32)
    col_cut = (jnp.arange(WIN_COLS) == WIN_COLS - 1).astype(jnp.int32)
    cuts = (32 * row_cut[:, None] + 16 * col_cut[None, :]).reshape(-1)

    cuts = jnp.concatenate([jnp.zeros_like(cuts), cuts])

    vectors = jnp.concatenate(
        [qv_bias, proj_bias[:, None], fc2_bias[:, None], norm_gain, norm_bias], axis=1
    )
    vectors = jnp.concatenate(
        [
            jnp.pad(vectors, ((0, 0), (0, 0), (0, D - part))),
            jnp.pad(fc1_bias[:, None], ((0, 0), (0, 7), (0, D - 4 * part))),
        ],
        axis=1,
    ).reshape(32, D)
    if not can_swap(tokens, clip_count * row_count):
        inputs, cotangent = exchange(inputs), exchange(cotangent)
    saved, upstream, out_rows, full, vec_rows = forward_layers(
        cuts,
        placing,
        inputs,
        cotangent,
        (qkv_weight, proj_weight, fc1_weight, fc2_weight),
        vectors,
        rel_table,
    )
    output = exchange(out_rows)
    last = (window_rows - 1) * WIN_COLS
    grad_two, packed_two = backward_layer(
        1, upstream, upstream, [v[1] for v in saved], [w[1] for w in full], vec_rows[1], f32
    )
    behind_grad = shifted_rows(edge_rows(grad_two, last, 2), 1)
    grad_one, packed_one = backward_layer(
        0, grad_two, behind_grad, [v[0] for v in saved], [w[0] for w in full], vec_rows[0], bf16
    )
    grad_rows = unplace_plain(placing.reshape(1, tokens), grad_one)
    input_grad = exchange(grad_rows).astype(f32)
    totals = unpack_gradients(sum_gradients(packed_one, packed_two))
    return (output, input_grad, *totals)


def unplace_plain_kernel(place_ref, rows_ref, out_ref):
    tokens = rows_ref.shape[0]
    spots = lax.broadcasted_iota(jnp.int32, (CHUNK, tokens), 0) + pl.program_id(0) * CHUNK
    pick = jnp.where(spots == place_ref[...], 1.0, 0.0).astype(bf16)
    out_ref[...] = dot_nn(pick, rows_ref[...]).astype(out_ref.dtype)


def unplace_plain(place, rows):
    tokens, width = rows.shape
    return pl.pallas_call(
        unplace_plain_kernel,
        grid=(tokens // CHUNK,),
        in_specs=[whole((1, tokens)), whole((tokens, width))],
        out_specs=rows_of((CHUNK, width)),
        out_shape=jax.ShapeDtypeStruct((tokens, width), bf16),
        name="unplace_plain",
    )(place, rows)


def solution(mesh):
    placed = (
        P(("clip", "row"), None),
        P(("clip", "row"), None),
        P(("clip", "row")),
        P("clip"),
        P(None, "row", None),
        P(None, None, "row"),
        P(None, "row", None),
        P(None, "row"),
        P(None, "row", None),
        P(None, "row"),
        P(None, "row", None),
        P(None, "row"),
        P(None, None, "row"),
        P(None, None, "row"),
        P(),
    )
    return jax.shard_map(
        body,
        mesh=mesh,
        in_specs=placed,
        out_specs=(
            P(("clip", "row"), None),
            P(("clip", "row"), None),
            P(None, "row", None),
            P(None, None, "row"),
            P(None, "row", None),
            P(None, "row"),
            P(None, "row", None),
            P(None, "row"),
            P(None, "row", None),
            P(None, "row"),
            P(None, None, "row"),
            P(None, None, "row"),
            P(),
        ),
        check_vma=False,
    )
```

```python
import functools

import jax
import jax.numpy as jnp
import numpy as np
from jax import lax
from jax.experimental import pallas as pl
from jax.experimental.pallas import tpu as pltpu
from jax.sharding import PartitionSpec as P

WIN = 8
SHIFT = 4
GRID_COLS = 64
EPSILON = 1e-05
MASKED = -1000000000.0
ROOT_HALF = 0.7071067811865476
INV_ROOT_TAU = 0.3989422804014327

HEADS = 16
HEAD_DIM = 24
D = HEADS * HEAD_DIM
GROUP = 8
CELL = WIN * WIN
BLOCK = SHIFT * SHIFT
WIN_COLS = GRID_COLS // WIN
SPREAD = 2 * WIN - 1
TABLE = SPREAD * SPREAD
TABLE_PAD = 256
SCALE = HEAD_DIM**-0.5
CHUNK = 256
CHUNK_WINS = CHUNK // CELL
VMEM_LIMIT = 56 * 1024 * 1024

MESH = pl.DeviceIdType.MESH
f32 = jnp.float32
bf16 = jnp.bfloat16


def window_places():
    spot = np.arange(CELL)
    row = (spot // 32) * SHIFT + (spot % BLOCK) // SHIFT
    col = (spot // BLOCK % 2) * SHIFT + spot % SHIFT
    return row, col


def head_masks():
    feature = np.arange(D) // HEAD_DIM
    rows = (feature[None, :] == np.arange(HEADS)[:, None]).astype(np.float32)
    wide = np.stack(
        [
            np.repeat(rows[GROUP * g : GROUP * (g + 1), 128 * g : 128 * g + 256], CELL, axis=0)
            for g in range(2)
        ]
    )
    return rows, wide


def table_constants():
    row, col = window_places()
    natural = row * WIN + col
    lanes = np.zeros((2, TABLE_PAD, 128), np.float32)
    for half in range(2):
        lanes[half, row * SPREAD + col, half * CELL + np.arange(CELL)] = 1.0
    order = np.zeros((CELL, CELL), np.float32)
    order[np.arange(CELL), natural] = 1.0
    back = np.zeros((CELL, CELL), np.float32)
    back[row * WIN + (WIN - 1 - col), np.arange(CELL)] = 1.0
    return lanes, order, back


def dot_nn(a, b):
    return lax.dot_general(a, b, (((1,), (0,)), ((), ())), preferred_element_type=f32)


def dot_nt(a, b):
    return lax.dot_general(a, b, (((1,), (1,)), ((), ())), preferred_element_type=f32)


def dot_tn(a, b):
    return lax.dot_general(a, b, (((0,), (0,)), ((), ())), preferred_element_type=f32)


def dot_exact(a, b, dims):
    return lax.dot_general(
        a, b, (dims, ((), ())), precision=lax.Precision.HIGHEST, preferred_element_type=f32
    )


def split(values):
    high = values.astype(bf16)
    rest = values - high.astype(f32)
    middle = rest.astype(bf16)
    return high, middle, (rest - middle.astype(f32)).astype(bf16)


def whole(shape):
    zeros = (0,) * len(shape)
    return pl.BlockSpec(shape, lambda i: zeros)


def rows_of(shape):
    return pl.BlockSpec(shape, lambda i: (i, 0))


def norm_parts(values):
    centred = values - jnp.mean(values, axis=-1, keepdims=True)
    inverse = lax.rsqrt(jnp.mean(centred * centred, axis=-1, keepdims=True) + EPSILON)
    return centred * inverse, inverse


def norm_back(upstream, normal, inverse, gain):
    scaled = upstream * gain
    centred = scaled - jnp.mean(scaled, axis=-1, keepdims=True)
    return inverse * (centred - normal * jnp.mean(scaled * normal, axis=-1, keepdims=True))


def column_sum(values):
    return jnp.sum(values, axis=0, keepdims=True)


def bias_rows(table_ref, lanes_ref, order_ref, out_ref, wide_ref):
    for layer in range(2):
        for head in range(HEADS):
            pair, half = divmod(head, 2)
            spread = jnp.broadcast_to(table_ref[layer, head : head + 1, :], (WIN, TABLE_PAD))
            for i in range(WIN):
                at = CELL * pair + WIN * i
                wide_ref[at : at + WIN, TABLE_PAD * half : TABLE_PAD * (half + 1)] = pltpu.roll(
                    spread, (SPREAD * i - 112) % TABLE_PAD, 1, stride=1, stride_axis=0
                )
        picked = sum(dot_nn(part, lanes_ref[...]) for part in reversed(split(wide_ref[...])))
        joined = jnp.concatenate(
            [picked[CELL * pair : CELL * (pair + 1), :] for pair in range(HEADS // 2)], axis=1
        )
        out_ref[layer] = sum(dot_nn(order_ref[...], part) for part in reversed(split(joined)))


def table_rows(grads, lanes_ref, back_ref):
    turned = sum(dot_nn(back_ref[...], part) for part in reversed(split(grads)))
    stacked = jnp.concatenate([turned[:, 128 * i : 128 * (i + 1)] for i in range(HEADS // 2)], axis=0)
    spread = sum(dot_nt(part, lanes_ref[...]) for part in reversed(split(stacked)))
    rows = []
    for head in range(HEADS):
        pair, half = divmod(head, 2)
        total = jnp.zeros((WIN, TABLE_PAD), f32)
        for i in range(WIN):
            at = CELL * pair + WIN * i
            total += pltpu.roll(
                spread[at : at + WIN, TABLE_PAD * half : TABLE_PAD * (half + 1)],
                (112 - SPREAD * i - (WIN - 1)) % TABLE_PAD,
                1,
                stride=1,
                stride_axis=0,
            )
        rows.append(column_sum(total))
    return jnp.concatenate(rows, axis=0)


def quarter(window, sub):
    return pl.ds(CELL * window + BLOCK * sub, BLOCK)


def assemble_back(main_ref, edge_ref, out_ref):
    windows = main_ref.shape[0] // CELL
    for window in range(windows):
        wr, wc = divmod(window, WIN_COLS)
        before = (wc - 1) % WIN_COLS
        out_ref[quarter(window, 3), :] = main_ref[quarter(window, 0), :].astype(out_ref.dtype)
        out_ref[quarter(window, 2), :] = main_ref[
            quarter(wr * WIN_COLS + before, 1), :
        ].astype(out_ref.dtype)
        for sub, col, piece in ((1, wc, 0), (0, before, 1)):
            if wr == 0:
                value = edge_ref[pl.ds(2 * BLOCK * col + BLOCK * piece, BLOCK), :]
            else:
                value = main_ref[quarter((wr - 1) * WIN_COLS + col, 2 + piece), :]
            out_ref[quarter(window, sub), :] = value.astype(out_ref.dtype)


def assemble_ahead(main_ref, edge_ref, out_ref):
    windows = main_ref.shape[0] // CELL
    last = windows // WIN_COLS - 1
    for window in range(windows):
        wr, wc = divmod(window, WIN_COLS)
        after = (wc + 1) % WIN_COLS
        out_ref[quarter(window, 0), :] = main_ref[quarter(window, 3), :].astype(out_ref.dtype)
        out_ref[quarter(window, 1), :] = main_ref[
            quarter(wr * WIN_COLS + after, 2), :
        ].astype(out_ref.dtype)
        for sub, col, piece in ((2, wc, 1), (3, after, 0)):
            if wr == last:
                value = edge_ref[pl.ds(2 * BLOCK * col + BLOCK * piece, BLOCK), :]
            else:
                value = main_ref[quarter((wr + 1) * WIN_COLS + col, piece), :]
            out_ref[quarter(window, sub), :] = value.astype(out_ref.dtype)


class Place:
    def __init__(self, n_row, n_far):
        clip = lax.axis_index("clip")
        self.n_row, self.n_far = n_row, n_far
        self.core, self.far, self.row = clip % 2, clip // 2, lax.axis_index("row")
        self.n = 2 * n_far * n_row
        self.index = clip * n_row + self.row

    def index_at(self, d):
        return (self.index + d) % self.n

    def device(self, d):
        at = self.index_at(d)
        return (at // self.n_row, at % self.n_row)

    def row_at(self, d):
        return (self.row + d) % self.n_row

    def far_at(self, d):
        return (self.far + d) % self.n_far

    def twin(self):
        return (2 * self.far + 1 - self.core, self.row)

    def in_row(self, d):
        return (2 * self.far + self.core, self.row_at(d))

    def along(self, d):
        return (2 * self.far_at(d) + self.core, self.row)

    def partners(self, far=True):
        found = [self.twin()] + [self.in_row(d) for d in range(1, self.n_row)]
        return found + ([self.along(d) for d in range(1, self.n_far)] if far else [])


def meet(partners):
    barrier = pltpu.get_barrier_semaphore()
    for partner in partners:
        pl.semaphore_signal(barrier, inc=1, device_id=partner, device_id_type=MESH)
    pl.semaphore_wait(barrier, len(partners))


def send(src, dst, send_sem, recv_sem, target):
    copy = pltpu.make_async_remote_copy(
        src_ref=src,
        dst_ref=dst,
        send_sem=send_sem,
        recv_sem=recv_sem,
        device_id=target,
        device_id_type=MESH,
    )
    copy.start()
    return copy


def remote(src, dst, send_sem, recv_sem, target):
    return pltpu.make_async_remote_copy(
        src_ref=src,
        dst_ref=dst,
        send_sem=send_sem,
        recv_sem=recv_sem,
        device_id=target,
        device_id_type=MESH,
    )


def can_swap(tokens, n):
    return tokens // n % 16 == 0


def meet_all(place):
    barrier = pltpu.get_barrier_semaphore()

    def greet(d, carry):
        pl.semaphore_signal(barrier, inc=1, device_id=place.device(d), device_id_type=MESH)
        return carry

    lax.fori_loop(1, place.n, greet, 0)
    pl.semaphore_wait(barrier, place.n - 1)


def swap_block(place, ref, index):
    count = ref.shape[0] // place.n
    return ref.at[pl.ds(pl.multiple_of(index * count, 16), count), :]


def swap_own(place, src, dst, sem):
    return pltpu.make_async_copy(
        swap_block(place, src, place.index), swap_block(place, dst, place.index), sem.at[0, 0]
    )


def swap_copy(place, src, dst, sem, d, owner):
    return remote(
        swap_block(place, src, place.index_at(d)),
        swap_block(place, dst, owner),
        sem.at[0, d],
        sem.at[1, d],
        place.device(d),
    )


def swap_start(place, src, dst, sem):
    def work(d, carry):
        swap_copy(place, src, dst, sem, d, place.index).start()
        return carry

    lax.fori_loop(1, place.n, work, 0)


def swap_wait(place, src, dst, sem):
    def work(d, carry):
        swap_copy(place, src, dst, sem, d, place.index_at(place.n - d)).wait_recv()
        return carry

    lax.fori_loop(1, place.n, work, 0)


def swap_end(place, src, dst, sem):
    def work(d, carry):
        swap_copy(place, src, dst, sem, d, place.index).wait_send()
        return carry

    lax.fori_loop(1, place.n, work, 0)


def row_share(n_row):
    return D // n_row


HALVES = (((0, 0, 1), (1, 0, 1), (3, 0, 2)), ((2, 0, 1), (3, 2, 2)))
HEIGHTS = (1, 1, 1, 4)


def forward_kernel(
    n_row,
    n_far,
    swap,
    cuts_ref,
    place_col,
    place_row,
    x_in,
    c_in,
    qkv_i,
    proj_i,
    fc1_i,
    fc2_i,
    vec_i,
    table_ref,
    lanes_ref,
    order_ref,
    heads_ref,
    wide_heads_ref,
    x_out,
    qkv_out,
    prob_out,
    att_out,
    mid_out,
    act_out,
    slope_out,
    up_out,
    rows_out,
    qkv_wo,
    proj_wo,
    fc1_wo,
    fc2_wo,
    vec_out,
    x_got,
    c_got,
    qkv_s,
    proj_s,
    fc1_s,
    fc2_s,
    vec_got,
    qkv_b,
    fc1_b,
    bias_s,
    wide_s,
    x_s,
    y_s,
    c_s,
    edge_out,
    edge_in,
    x_sem,
    c_sem,
    own_sem,
    row_sem,
    twin_sem,
    vec_sem,
    edge_sem,
    out_sem,
):
    step = pl.program_id(0)
    tokens = x_s.shape[0]
    chunks = tokens // CHUNK
    layer = step // chunks
    chunk = (step + layer * (chunks // 2)) % chunks
    place = Place(n_row, n_far)
    size = row_share(n_row)
    shards = (qkv_i, proj_i, fc1_i, fc2_i)
    kept = (qkv_s, proj_s, fc1_s, fc2_s)
    outs = (qkv_wo, proj_wo, fc1_wo, fc2_wo)
    last_row = (tokens // CELL // WIN_COLS - 1) * WIN_COLS
    if not swap:
        x_got, c_got = x_in, c_in

    def own(l, w):
        return pltpu.make_async_copy(
            shards[w].at[l], spot(l, w, place.row, 0, HEIGHTS[w]), own_sem.at[l, w]
        )

    def spot(l, w, owner, first, count):
        at = pl.multiple_of((owner * HEIGHTS[w] + first) * size, 16)
        return kept[w].at[l, pl.ds(at, count * size), :]

    def push(l, core, i, d, source=None):
        w, first, count = HALVES[core][i]
        return remote(
            shards[w].at[l, pl.ds(first * size, count * size), :],
            spot(l, w, place.row if source is None else source, first, count),
            row_sem.at[0, l, i, d - 1],
            row_sem.at[1, l, i, d - 1],
            place.in_row(d),
        )

    def hand(l, core, i, d):
        w, first, count = HALVES[core][i]
        here = spot(l, w, place.row_at(n_row - d), first, count)
        return remote(
            here, here, twin_sem.at[0, l, i, d - 1], twin_sem.at[1, l, i, d - 1], place.twin()
        )

    def pieces(core):
        return [(i, d) for i in range(len(HALVES[core])) for d in range(1, n_row)]

    def by_core(work):
        for core in range(2):
            pl.when(place.core == core)(functools.partial(work, core))

    def start_weights(l):
        def work(core):
            for i, d in pieces(core):
                push(l, core, i, d).start()

        by_core(work)

    def pass_weights(l):
        def work(core):
            for i, d in pieces(core):
                push(l, core, i, d, place.row_at(n_row - d)).wait_recv()
                hand(l, core, i, d).start()

        by_core(work)

    def wait_weights(l):
        def work(core):
            for i, d in pieces(1 - core):
                hand(l, 1 - core, i, d).wait_recv()

        by_core(work)
        for w in range(4):
            own(l, w).wait()

    def end_weights(l):
        def work(core):
            for i, d in pieces(core):
                push(l, core, i, d).wait_send()
                hand(l, core, i, d).wait_send()

        by_core(work)

    def vector_copy(d):
        return remote(
            vec_i, vec_got.at[place.row], vec_sem.at[0, d - 1], vec_sem.at[1, d - 1], place.in_row(d)
        )

    def edge_copy(which, d):
        return remote(
            edge_out.at[which],
            edge_in.at[which],
            edge_sem.at[0, which],
            edge_sem.at[1, which],
            place.in_row(d),
        )

    def pack_edge(which, source, first_window, first_sub):
        for col in range(WIN_COLS):
            at = CELL * (first_window + col) + BLOCK * first_sub
            edge_out[which, 2 * BLOCK * col : 2 * BLOCK * (col + 1), :] = source[
                at : at + 2 * BLOCK, :
            ].astype(bf16)

    def pick_rows(source, target):
        for c in range(chunks):
            rows = slice(CHUNK * c, CHUNK * (c + 1))
            spots = lax.broadcasted_iota(jnp.int32, (CHUNK, tokens), 1)
            pick = jnp.where(spots == place_col[rows, :], 1.0, 0.0).astype(bf16)
            target[rows, :] = dot_nn(pick, source[...]).astype(target.dtype)

    @pl.when(step == 0)
    def _():
        for l in range(2):
            for w in range(4):
                own(l, w).start()
        mine = pltpu.make_async_copy(vec_i, vec_got.at[place.row], out_sem.at[4])
        mine.start()
        if swap:
            swap_own(place, x_in, x_got, x_sem).start()
            swap_own(place, c_in, c_got, c_sem).start()
            meet_all(place)
            swap_start(place, x_in, x_got, x_sem)
        else:
            meet(place.partners(far=False))
        for d in range(1, n_row):
            vector_copy(d).start()
        start_weights(0)
        bias_rows(table_ref, lanes_ref, order_ref, bias_s, wide_s)
        mine.wait()
        for d in range(1, n_row):
            vector_copy(d).wait()
        for l in range(2):
            shares = [vec_got[r, 16 * l : 16 * (l + 1), :].astype(f32) for r in range(n_row)]
            rows = jnp.concatenate([share[0:8, 0:size] for share in shares], axis=1)
            vec_out[l] = rows
            qkv_b[l, 0:1, 0:D] = rows[0:1]
            qkv_b[l, 0:1, D : 2 * D] = jnp.zeros((1, D), f32)
            qkv_b[l, 0:1, 2 * D : 3 * D] = rows[1:2]
            fc1_b[l, 0:1, :] = jnp.concatenate(
                [share[8:9, 0 : 4 * size] for share in shares], axis=1
            )
        if swap:
            swap_wait(place, x_in, x_got, x_sem)
            swap_own(place, x_in, x_got, x_sem).wait()
        pick_rows(x_got, x_s)
        pass_weights(0)
        wait_weights(0)

    @pl.when(step == 1)
    def _():
        start_weights(1)
        if swap:
            swap_start(place, c_in, c_got, c_sem)

    @pl.when(step == chunks - 1)
    def _():
        pass_weights(1)

    @pl.when(step == chunks)
    def _():
        wait_weights(1)
        for w in range(4):
            pltpu.make_async_copy(kept[w], outs[w], out_sem.at[w]).start()
        edge_copy(0, n_row - 1).wait_recv()
        assemble_ahead(y_s, edge_in.at[0], x_s)

    @pl.when(step == chunks + 2)
    def _():
        if swap:
            swap_wait(place, c_in, c_got, c_sem)
            swap_own(place, c_in, c_got, c_sem).wait()
        pick_rows(c_got, c_s)
        pack_edge(2, c_s, 0, 0)
        edge_copy(2, n_row - 1).start()

    here = pl.ds(pl.multiple_of(chunk * CHUNK, CHUNK), CHUNK)
    x = x_s[here, :]
    x_out[0] = x
    normal, _ = norm_parts(x)
    hidden = (normal * vec_out[layer, 4:5, :] + vec_out[layer, 6:7, :]).astype(bf16)
    qkv_out[0] = (dot_nn(hidden, qkv_s[layer]) + qkv_b[layer]).astype(bf16)
    wide = (CELL, GROUP * CELL)
    apart = lax.broadcasted_iota(jnp.int32, wide, 0) ^ lax.broadcasted_iota(jnp.int32, wide, 1)
    for k in range(CHUNK_WINS):
        rows = slice(CELL * k, CELL * (k + 1))
        keep = (apart & cuts_ref[(layer * chunks + chunk) * CHUNK_WINS + k]) == 0
        mixed = []
        for g in range(2):
            q = qkv_out[0, rows, 128 * g : 128 * g + 256]
            key = qkv_out[0, rows, D + 128 * g : D + 128 * g + 256]
            val = qkv_out[0, rows, 2 * D + 128 * g : 2 * D + 128 * g + 256]
            q_wide = jnp.concatenate([q] * GROUP, axis=0) * wide_heads_ref[g]
            lanes = slice(GROUP * CELL * g, GROUP * CELL * (g + 1))
            s = dot_nt(key, q_wide) * SCALE + bias_s[layer, :, lanes]
            s = jnp.where(keep, s, MASKED)
            e = jnp.exp(s - jnp.max(s, axis=0, keepdims=True))
            prob = (e * (1.0 / jnp.sum(e, axis=0, keepdims=True))).astype(bf16)
            prob_out[0, rows, lanes] = prob
            mixed.append(gather_heads(dot_tn(prob, val), heads_ref, g))
        att_out[0, rows, :] = join_groups(*mixed).astype(bf16)
    mid = x + (dot_nn(att_out[0], proj_s[layer]) + vec_out[layer, 2:3, :])
    mid_out[0] = mid
    normal, _ = norm_parts(mid)
    hidden = (normal * vec_out[layer, 5:6, :] + vec_out[layer, 7:8, :]).astype(bf16)
    u = dot_nn(hidden, fc1_s[layer]) + fc1_b[layer]
    cdf = 0.5 * (1.0 + lax.erf(u * ROOT_HALF))
    act_out[0] = (u * cdf).astype(bf16)
    slope_out[0] = (cdf + u * (jnp.exp(-0.5 * u * u) * INV_ROOT_TAU)).astype(bf16)
    y_s[here, :] = mid + (dot_nn(act_out[0], fc2_s[layer]) + vec_out[layer, 3:4, :])

    @pl.when(step == chunks // 2 - 1)
    def _():
        pack_edge(0, y_s, 0, 0)
        edge_copy(0, n_row - 1).start()

    @pl.when(step == chunks + chunks // 2 - 1)
    def _():
        pack_edge(1, y_s, last_row, 2)
        edge_copy(1, 1).start()

    @pl.when(step == 2 * chunks - 1)
    def _():
        edge_copy(2, n_row - 1).wait_recv()
        assemble_ahead(c_s, edge_in.at[2], up_out)
        edge_copy(1, 1).wait_recv()
        assemble_back(y_s, edge_in.at[1], c_s)
        for c in range(chunks):
            rows = slice(CHUNK * c, CHUNK * (c + 1))
            spots = lax.broadcasted_iota(jnp.int32, (CHUNK, tokens), 0) + CHUNK * c
            pick = jnp.where(spots == place_row[...], 1.0, 0.0).astype(bf16)
            rows_out[rows, :] = dot_nn(pick, c_s[...]).astype(bf16)
        for l in range(2):
            end_weights(l)
        for which in range(3):
            edge_copy(which, 1 if which == 1 else n_row - 1).wait_send()
        for w in range(4):
            pltpu.make_async_copy(kept[w], outs[w], out_sem.at[w]).wait()
        if swap:
            swap_end(place, x_in, x_got, x_sem)
            swap_end(place, c_in, c_got, c_sem)


def gather_heads(spread, heads_ref, g):
    total = None
    for h in range(GROUP):
        part = spread[CELL * h : CELL * (h + 1), :] * heads_ref[
            GROUP * g + h : GROUP * g + h + 1, 128 * g : 128 * g + 256
        ]
        total = part if total is None else total + part
    return total


def join_groups(low, high):
    return jnp.concatenate([low[:, :128], low[:, 128:] + high[:, :128], high[:, 128:]], axis=1)


def forward_layers(cuts, placing, x_in, c_in, shards, vectors, rel_table):
    n_row, n_far = lax.axis_size("row"), lax.axis_size("clip") // 2
    tokens = x_in.shape[0]
    chunks = tokens // CHUNK
    swap = can_swap(tokens, n_row * n_far * 2)
    heads, wide = head_masks()
    lanes, order, _ = table_constants()
    table = jnp.pad(rel_table.transpose(0, 2, 1), ((0, 0), (0, 0), (0, TABLE_PAD - TABLE)))
    ff = shards[2].shape[2]
    anywhere = pl.BlockSpec(memory_space=pl.ANY)
    patches = anywhere if swap else whole((tokens, D))
    constants = (
        table,
        jnp.asarray(lanes.reshape(2 * TABLE_PAD, 128), dtype=bf16),
        jnp.asarray(order, dtype=bf16),
        jnp.asarray(heads),
        jnp.asarray(wide, dtype=bf16),
    )
    full = [(2, shard.shape[1] * n_row, shard.shape[2]) for shard in shards]

    def block(i):
        layer = i // chunks
        return layer, (i + layer * (chunks // 2)) % chunks, 0

    saved = [(D, f32), (3 * D, bf16), (HEADS * CELL, bf16), (D, bf16), (D, f32), (ff, bf16), (ff, bf16)]
    dma = pltpu.SemaphoreType.DMA
    n = n_row * n_far * 2
    results = pl.pallas_call(
        functools.partial(forward_kernel, n_row, n_far, swap),
        grid=(2 * chunks,),
        in_specs=[
            pl.BlockSpec(memory_space=pltpu.SMEM),
            whole((tokens, 1)),
            whole((1, tokens)),
            patches,
            patches,
        ]
        + [anywhere] * 5
        + [whole(constant.shape) for constant in constants],
        out_specs=[pl.BlockSpec((1, CHUNK, width), block) for width, _ in saved]
        + [whole((tokens, D))] * 2
        + [anywhere] * 4
        + [whole((2, 8, D))],
        out_shape=[jax.ShapeDtypeStruct((2, tokens, width), kind) for width, kind in saved]
        + [jax.ShapeDtypeStruct((tokens, D), bf16)] * 2
        + [jax.ShapeDtypeStruct(shape, bf16) for shape in full]
        + [jax.ShapeDtypeStruct((2, 8, D), f32)],
        scratch_shapes=[
            pltpu.VMEM((tokens if swap else 16, D), bf16),
            pltpu.VMEM((tokens if swap else 16, D), bf16),
            *[pltpu.VMEM(shape, bf16) for shape in full],
            pltpu.VMEM((n_row, *vectors.shape), bf16),
            pltpu.VMEM((2, 1, 3 * D), f32),
            pltpu.VMEM((2, 1, ff), f32),
            pltpu.VMEM((2, CELL, HEADS * CELL), f32),
            pltpu.VMEM((HEADS // 2 * CELL, 2 * TABLE_PAD), f32),
            pltpu.VMEM((tokens, D), f32),
            pltpu.VMEM((tokens, D), f32),
            pltpu.VMEM((tokens, D), bf16),
            pltpu.VMEM((3, WIN_COLS * 2 * BLOCK, D), bf16),
            pltpu.VMEM((3, WIN_COLS * 2 * BLOCK, D), bf16),
            dma((2, n if swap else 1)),
            dma((2, n if swap else 1)),
            dma((2, 4)),
            dma((2, 2, 3, n_row - 1)),
            dma((2, 2, 3, n_row - 1)),
            dma((2, n_row - 1)),
            dma((2, 3)),
            dma((5,)),
        ],
        compiler_params=pltpu.CompilerParams(
            collective_id=0, has_side_effects=True, vmem_limit_bytes=VMEM_LIMIT
        ),
        name="forward_layers",
    )(cuts, placing.reshape(tokens, 1), placing.reshape(1, tokens), x_in, c_in, *shards, vectors, *constants)
    return results[:7], results[7], results[8], results[9:13], results[13]


BATCHES = ((1, 0), (1, 1), (0, 0), (0, 1))


def batch_rows(n_row, kind):
    return 4 * row_share(n_row) if kind == 0 else 2 * row_share(n_row) + 16


def piece_rows(n_row, n_far, kind):
    return -(-batch_rows(n_row, kind) // (16 * n_far)) * 16


def backward_kernel(
    n_row,
    n_far,
    swap,
    place_row,
    up_ref,
    rows_in,
    x_ref,
    qkv_ref,
    prob_ref,
    att_ref,
    mid_ref,
    act_ref,
    slope_ref,
    qkv_w,
    proj_w,
    fc1_w,
    fc2_w,
    vec_ref,
    heads_ref,
    wide_heads_ref,
    lanes_ref,
    back_ref,
    rows_out,
    grad_out,
    final_m_out,
    final_a_out,
    vec_g,
    fc1_bg,
    table_g,
    g_s,
    h1_s,
    dt_s,
    ga_s,
    h2_s,
    du_s,
    gz_s,
    grad_rows,
    edge_out,
    edge_in,
    pack_m,
    pack_a,
    got_am,
    got_aa,
    got_bm,
    got_ba,
    out_cm,
    out_ca,
    got_cm,
    got_ca,
    final_m,
    final_a,
    rows_sem,
    grad_sem,
    edge_sem,
    a_sem,
    b_sem,
    c_sem,
    d_sem,
    e_sem,
    done_sem,
):
    step = pl.program_id(0)
    tokens = g_s.shape[1]
    chunks = tokens // CHUNK
    layer = 1 - step // (2 * chunks)
    kind = step // chunks % 2
    chunk = (step + chunks // 2) % chunks
    place = Place(n_row, n_far)
    core, row, far = place.core, place.row, place.far
    size = row_share(n_row)
    last_row = (tokens // CELL // WIN_COLS - 1) * WIN_COLS
    packs, got_as, got_bs = (pack_m, pack_a), (got_am, got_aa), (got_bm, got_ba)
    out_cs, got_cs, finals = (out_cm, out_ca), (got_cm, got_ca), (final_m, final_a)
    here = pl.ds(pl.multiple_of(chunk * CHUNK, CHUNK), CHUNK)

    def edge_copy():
        return remote(
            edge_out, edge_in, edge_sem.at[0], edge_sem.at[1], place.in_row(1)
        )

    def part(ref, b, at):
        rows = got_cs[BATCHES[b][1]].shape[2]
        return ref.at[BATCHES[b][0], pl.ds(pl.multiple_of(at * rows, 16), rows), :]

    def copy_a(b):
        l, k = BATCHES[b]
        return remote(
            packs[k].at[l, 1 - core], got_as[k].at[l], a_sem.at[0, b], a_sem.at[1, b], place.twin()
        )

    def copy_b(b, d):
        l, k = BATCHES[b]
        return remote(
            packs[k].at[l, core, place.row_at(d)],
            got_bs[k].at[l, d - 1],
            b_sem.at[0, b, d - 1],
            b_sem.at[1, b, d - 1],
            place.in_row(d),
        )

    def copy_c(b, d):
        l, k = BATCHES[b]
        return remote(
            part(out_cs[k], b, place.far_at(d)),
            got_cs[k].at[l, d - 1],
            c_sem.at[0, b, d - 1],
            c_sem.at[1, b, d - 1],
            place.along(d),
        )

    def copy_d(b, d, owner):
        spot = part(finals[BATCHES[b][1]].at[core], b, owner)
        return remote(
            spot, spot, d_sem.at[0, b, d - 1], d_sem.at[1, b, d - 1], place.along(d)
        )

    def copy_e(b, d, half):
        spot = part(finals[BATCHES[b][1]].at[half], b, place.far_at((n_far - d) % n_far))
        return remote(spot, spot, e_sem.at[0, b, d], e_sem.at[1, b, d], place.twin())

    def sum_cores(b):
        l, k = BATCHES[b]
        copy_a(b).wait_recv()
        for d in range(1, n_row):
            r = place.row_at(d)
            packs[k][l, core, r] = packs[k][l, core, r] + got_as[k][l, r]
            copy_b(b, d).start()
        packs[k][l, core, row] = packs[k][l, core, row] + got_as[k][l, row]

    def sum_row(b):
        l, k = BATCHES[b]
        total = packs[k][l, core, row].astype(f32)
        for d in range(1, n_row):
            copy_b(b, d).wait_recv()
            total += got_bs[k][l, d - 1].astype(f32)
        out_cs[k][l, 0 : batch_rows(n_row, k), :] = total.astype(bf16)
        for d in range(1, n_far):
            copy_c(b, d).start()

    def sum_far(b):
        l, k = BATCHES[b]
        total = part(out_cs[k], b, far)[...].astype(f32)
        for d in range(1, n_far):
            copy_c(b, d).wait_recv()
            total += got_cs[k][l, d - 1].astype(f32)
        part(finals[k].at[core], b, far)[...] = total.astype(bf16)
        for d in range(1, n_far):
            copy_d(b, d, far).start()
        copy_e(b, 0, core).start()

    def pass_on(b):
        for d in range(1, n_far):
            copy_d(b, d, place.far_at(n_far - d)).wait_recv()
            copy_e(b, d, core).start()

    def finish(b):
        copy_a(b).wait_send()
        for d in range(1, n_row):
            copy_b(b, d).wait_send()
        for d in range(1, n_far):
            copy_c(b, d).wait_send()
            copy_d(b, d, far).wait_send()
        for d in range(n_far):
            copy_e(b, d, core).wait_send()
            copy_e(b, d, 1 - core).wait_recv()

    @pl.when(step == 0)
    def _():
        if swap:
            swap_own(place, rows_in, rows_out, rows_sem).start()
            meet_all(place)
            swap_start(place, rows_in, rows_out, rows_sem)
        else:
            pltpu.make_async_copy(rows_in, rows_out, rows_sem.at[0, 0]).start()
            meet(place.partners())
        g_s[1] = up_ref[...].astype(f32)
        for k in range(2):
            valid, padded = batch_rows(n_row, k), out_cs[k].shape[1]
            if padded > valid:
                out_cs[k][:, valid:, :] = jnp.zeros((2, padded - valid, D), bf16)

    @pl.when(step == chunks + 1)
    def _():
        sum_cores(0)

    @pl.when(step == 2 * chunks)
    def _():
        edge_copy().wait_recv()
        assemble_back(g_s.at[1], edge_in, g_s.at[0])
        sum_row(0)

    @pl.when(step == 2 * chunks + 1)
    def _():
        sum_cores(1)

    @pl.when(step == 2 * chunks + 2)
    def _():
        sum_far(0)

    @pl.when(step == 3 * chunks - 1)
    def _():
        sum_row(1)
        pass_on(0)

    @pl.when(step == 3 * chunks)
    def _():
        sum_far(1)

    @pl.when(step == 3 * chunks + 1)
    def _():
        sum_cores(2)
        pass_on(1)

    @pl.when(step % (2 * chunks) == 0)
    def _():
        vec_g[...] = jnp.zeros_like(vec_g)
        fc1_bg[...] = jnp.zeros_like(fc1_bg)
        table_g[...] = jnp.zeros_like(table_g)

    @pl.when(kind == 0)
    def _():
        upstream = g_s[layer, here, :]
        low = upstream.astype(bf16)
        gz_s[here, :] = low
        vec_g[3:4, :] += column_sum(low.astype(f32))
        du = (dot_nt(low, fc2_w[0]) * slope_ref[0].astype(f32)).astype(bf16)
        du_s[here, :] = du
        fc1_bg[...] += column_sum(du.astype(f32))
        dn = dot_nt(du, fc1_w[0])
        normal, inverse = norm_parts(mid_ref[0])
        gain = vec_ref[layer, 5:6, :]
        h2_s[here, :] = (normal * gain + vec_ref[layer, 7:8, :]).astype(bf16)
        vec_g[5:6, :] += column_sum(dn * normal)
        vec_g[7:8, :] += column_sum(dn)
        mid_grad = upstream + norm_back(dn, normal, inverse, gain)
        g_s[layer, here, :] = mid_grad
        low = mid_grad.astype(bf16)
        ga_s[here, :] = low
        vec_g[2:3, :] += column_sum(low.astype(f32))

    @pl.when(step % (2 * chunks) == chunks - 1)
    def _():
        for j in range(4):
            lanes = slice(D * j, D * (j + 1))
            value = dot_tn(h2_s[...], du_s[:, lanes]).astype(bf16)
            for r in range(n_row):
                pack_m[layer, 0, r, size * j : size * (j + 1), :] = value[
                    size * r : size * (r + 1), :
                ]
            value = dot_tn(act_ref[0, :, lanes], gz_s[...]).astype(bf16)
            count = D // (4 * size)
            for t in range(count):
                pack_m[layer, 1, j * count + t] = value[4 * size * t : 4 * size * (t + 1), :]

    @pl.when(step == chunks - 1)
    def _():
        copy_a(0).start()

    @pl.when(step == 3 * chunks - 1)
    def _():
        copy_a(2).start()

    @pl.when(kind == 1)
    def _():
        att_grad = dot_nt(ga_s[here, :], proj_w[0]).astype(bf16)
        for k in range(CHUNK_WINS):
            rows = slice(CELL * k, CELL * (k + 1))
            there = pl.ds(pl.multiple_of(chunk * CHUNK + CELL * k, CELL), CELL)
            q_parts, k_parts, v_parts = [], [], []
            for g in range(2):
                q = qkv_ref[0, rows, 128 * g : 128 * g + 256]
                key = qkv_ref[0, rows, D + 128 * g : D + 128 * g + 256]
                val = qkv_ref[0, rows, 2 * D + 128 * g : 2 * D + 128 * g + 256]
                do = att_grad[rows, 128 * g : 128 * g + 256]
                q_wide = jnp.concatenate([q] * GROUP, axis=0) * wide_heads_ref[g]
                do_wide = jnp.concatenate([do] * GROUP, axis=0) * wide_heads_ref[g]
                lanes = slice(GROUP * CELL * g, GROUP * CELL * (g + 1))
                prob_low = prob_ref[0, rows, lanes]
                prob = prob_low.astype(f32)
                dp = dot_nt(val, do_wide)
                v_parts.append(dot_nn(prob_low, do_wide))
                weighted = prob * dp
                ds = (weighted - prob * column_sum(weighted)).astype(bf16)
                table_g[:, lanes] += ds.astype(f32)
                k_parts.append(dot_nn(ds, q_wide))
                q_parts.append(gather_heads(dot_tn(ds, key), heads_ref, g))
            dt_s[there, 0:D] = (join_groups(*q_parts) * SCALE).astype(bf16)
            dt_s[there, D : 2 * D] = (join_groups(*k_parts) * SCALE).astype(bf16)
            dt_s[there, 2 * D : 3 * D] = join_groups(*v_parts).astype(bf16)
        dt = dt_s[here, :]
        vec_g[0:1, :] += column_sum(dt[:, 0:D].astype(f32))
        vec_g[1:2, :] += column_sum(dt[:, 2 * D :].astype(f32))
        dn = dot_nt(dt, qkv_w[0])
        normal, inverse = norm_parts(x_ref[0])
        gain = vec_ref[layer, 4:5, :]
        h1_s[here, :] = (normal * gain + vec_ref[layer, 6:7, :]).astype(bf16)
        vec_g[4:5, :] += column_sum(dn * normal)
        vec_g[6:7, :] += column_sum(dn)
        g_s[layer, here, :] += norm_back(dn, normal, inverse, gain)

    @pl.when(step == chunks + chunks // 2 - 1)
    def _():
        for col in range(WIN_COLS):
            at = CELL * (last_row + col) + 2 * BLOCK
            edge_out[2 * BLOCK * col : 2 * BLOCK * (col + 1), :] = g_s[
                1, at : at + 2 * BLOCK, :
            ].astype(bf16)
        edge_copy().start()

    @pl.when(step == 4 * chunks - 1)
    def _():
        source = g_s[0].astype(bf16)
        for c in range(chunks):
            rows = slice(CHUNK * c, CHUNK * (c + 1))
            spots = lax.broadcasted_iota(jnp.int32, (CHUNK, tokens), 0) + CHUNK * c
            pick = jnp.where(spots == place_row[...], 1.0, 0.0).astype(bf16)
            grad_rows[rows, :] = dot_nn(pick, source).astype(bf16)
        if swap:
            swap_own(place, grad_rows, grad_out, grad_sem).start()
            swap_start(place, grad_rows, grad_out, grad_sem)
        else:
            pltpu.make_async_copy(grad_rows, grad_out, grad_sem.at[0, 0]).start()

    @pl.when(step % (2 * chunks) == 2 * chunks - 1)
    def _():
        def put(half, at, value):
            for r in range(n_row):
                pack_a[layer, half, r, at : at + size, :] = value[size * r : size * (r + 1), :]

        for j in range(3):
            value = dot_tn(h1_s[...], dt_s[:, D * j : D * (j + 1)]).astype(bf16)
            put(j // 2, size * (j % 2), value)
        put(1, size, dot_tn(att_ref[0], ga_s[...]).astype(bf16))
        table = table_rows(table_g[...], lanes_ref, back_ref)
        table = jnp.concatenate([table, jnp.zeros((HEADS, D - TABLE_PAD), f32)], axis=1)
        vectors = jnp.concatenate(
            [vec_g[...]]
            + [fc1_bg[:, D * j : D * (j + 1)] for j in range(4)]
            + [jnp.zeros((4, D), f32)],
            axis=0,
        )
        for r in range(n_row):
            pack_a[layer, 0, r, 2 * size :, :] = vectors.astype(bf16)
            pack_a[layer, 1, r, 2 * size :, :] = table.astype(bf16)

    @pl.when(step == 2 * chunks - 1)
    def _():
        copy_a(1).start()

    @pl.when(step == 4 * chunks - 1)
    def _():
        copy_a(3).start()
        sum_row(2)
        sum_cores(3)
        sum_far(2)
        sum_row(3)
        pass_on(2)
        sum_far(3)
        pass_on(3)
        for b in range(4):
            finish(b)
        edge_copy().wait_send()
        copies = [
            pltpu.make_async_copy(final_m, final_m_out, done_sem.at[0]),
            pltpu.make_async_copy(final_a, final_a_out, done_sem.at[1]),
        ]
        for copy in copies:
            copy.start()
        for copy in copies:
            copy.wait()
        for source, target, sem in (
            (rows_in, rows_out, rows_sem),
            (grad_rows, grad_out, grad_sem),
        ):
            if swap:
                swap_wait(place, source, target, sem)
                swap_end(place, source, target, sem)
                swap_own(place, source, target, sem).wait()
            else:
                pltpu.make_async_copy(source, target, sem.at[0, 0]).wait()


def backward_layers(placing, upstream, rows, saved, full, vec):
    n_row, n_far = lax.axis_size("row"), lax.axis_size("clip") // 2
    n = 2 * n_row * n_far
    tokens = upstream.shape[0]
    chunks = tokens // CHUNK
    swap = can_swap(tokens, n)
    heads, wide = head_masks()
    lanes, _, back = table_constants()
    ff = full[2].shape[2]
    size = row_share(n_row)
    anywhere = pl.BlockSpec(memory_space=pl.ANY)

    def at(i):
        return 1 - i // (2 * chunks), i // chunks % 2, (i + chunks // 2) % chunks

    def layer_block(i):
        return 1 - i // (2 * chunks), 0, 0

    def forward_block(i):
        layer, kind, chunk = at(i)
        return (1 - kind) * layer, (1 - kind) * chunk + kind * (chunks // 2 - 1 + layer), 0

    def attention_block(i):
        layer, kind, chunk = at(i)
        return layer, kind * chunk + (1 - kind) * (chunks // 2), 0

    def chunked(value, block):
        return pl.BlockSpec((1, CHUNK, value.shape[2]), block)

    def layered(value):
        return pl.BlockSpec((1, *value.shape[1:]), layer_block)

    x, qkv, prob, att, mid, act, slope = saved
    constants = (
        vec,
        jnp.asarray(heads),
        jnp.asarray(wide, dtype=bf16),
        jnp.asarray(lanes.reshape(2 * TABLE_PAD, 128), dtype=bf16),
        jnp.asarray(back, dtype=bf16),
    )
    valid = [batch_rows(n_row, k) for k in range(2)]
    piece = [piece_rows(n_row, n_far, k) for k in range(2)]
    final = [(2, 2, n_far * piece[k], D) for k in range(2)]
    dma = pltpu.SemaphoreType.DMA

    def pair(shape_of):
        return [pltpu.VMEM(shape_of(k), bf16) for k in range(2)]

    return pl.pallas_call(
        functools.partial(backward_kernel, n_row, n_far, swap),
        grid=(4 * chunks,),
        in_specs=[
            whole((1, tokens)),
            whole((tokens, D)),
            anywhere,
            chunked(x, attention_block),
            chunked(qkv, attention_block),
            chunked(prob, attention_block),
            layered(att),
            chunked(mid, forward_block),
            layered(act),
            chunked(slope, forward_block),
        ]
        + [layered(weight) for weight in full]
        + [whole(constant.shape) for constant in constants],
        out_specs=[anywhere] * 4,
        out_shape=[jax.ShapeDtypeStruct((tokens, D), bf16)] * 2
        + [jax.ShapeDtypeStruct(shape, bf16) for shape in final],
        scratch_shapes=[
            pltpu.VMEM((8, D), f32),
            pltpu.VMEM((1, ff), f32),
            pltpu.VMEM((CELL, HEADS * CELL), f32),
            pltpu.VMEM((2, tokens, D), f32),
            pltpu.VMEM((tokens, D), bf16),
            pltpu.VMEM((tokens, 3 * D), bf16),
            pltpu.VMEM((tokens, D), bf16),
            pltpu.VMEM((tokens, D), bf16),
            pltpu.VMEM((tokens, ff), bf16),
            pltpu.VMEM((tokens, D), bf16),
            pltpu.VMEM((tokens, D), bf16),
            pltpu.VMEM((WIN_COLS * 2 * BLOCK, D), bf16),
            pltpu.VMEM((WIN_COLS * 2 * BLOCK, D), bf16),
            *pair(lambda k: (2, 2, n_row, valid[k], D)),
            *pair(lambda k: (2, n_row, valid[k], D)),
            *pair(lambda k: (2, n_row - 1, valid[k], D)),
            *pair(lambda k: (2, n_far * piece[k], D)),
            *pair(lambda k: (2, n_far - 1, piece[k], D)),
            *pair(lambda k: final[k]),
            dma((2, n if swap else 1)),
            dma((2, n if swap else 1)),
            dma((2,)),
            dma((2, 4)),
            dma((2, 4, n_row - 1)),
            dma((2, 4, n_far - 1)),
            dma((2, 4, n_far - 1)),
            dma((2, 4, n_far)),
            dma((2,)),
        ],
        compiler_params=pltpu.CompilerParams(
            collective_id=1, has_side_effects=True, vmem_limit_bytes=VMEM_LIMIT
        ),
        name="backward_layers",
    )(placing.reshape(1, tokens), upstream, rows, x, qkv, prob, att, mid, act, slope, *full, *constants)


def unpack_kernel(
    n_row, m_ref, a_ref, qkv_o, qvb_o, proj_o, projb_o, fc1_o, fc1b_o, fc2_o, fc2b_o, gain_o, shift_o, table_o
):
    row = lax.axis_index("row")
    size = D // n_row
    lane = lax.broadcasted_iota(jnp.int32, (D, size), 0)
    want = lax.broadcasted_iota(jnp.int32, (D, size), 1)
    pick = jnp.where(lane == want + size * row, 1.0, 0.0).astype(bf16)
    start = 4 * size * row
    lane = lax.broadcasted_iota(jnp.int32, (D, 4 * size), 0)
    want = lax.broadcasted_iota(jnp.int32, (D, 4 * size), 1)
    pick_fc1 = jnp.where(lane == want + start % D, 1.0, 0.0).astype(bf16)
    spot = lax.broadcasted_iota(jnp.int32, (16, 4 * size), 0)
    a = lax.broadcasted_iota(jnp.int32, (HEADS, HEADS), 0)
    b = lax.broadcasted_iota(jnp.int32, (HEADS, HEADS), 1)
    same = jnp.where(a == b, 1.0, 0.0).astype(bf16)
    for layer in range(2):
        for j in range(3):
            at = size * (j % 2)
            qkv_o[layer, :, D * j : D * (j + 1)] = a_ref[j // 2, layer, at : at + size, :].astype(f32)
        proj_o[layer] = a_ref[1, layer, size : 2 * size, :].astype(f32)
        for j in range(4):
            fc1_o[layer, :, D * j : D * (j + 1)] = m_ref[
                0, layer, size * j : size * (j + 1), :
            ].astype(f32)
        fc2_o[layer] = m_ref[1, layer, 0 : 4 * size, :].astype(f32)
        vectors = a_ref[0, layer, 2 * size : 2 * size + 16, :]
        mine = dot_nn(vectors, pick)
        qvb_o[layer] = mine[0:2]
        projb_o[layer : layer + 1] = mine[2:3]
        fc2b_o[layer : layer + 1] = mine[3:4]
        gain_o[layer] = mine[4:6]
        shift_o[layer] = mine[6:8]
        mine = dot_nn(vectors, pick_fc1)
        fc1b_o[layer : layer + 1] = column_sum(jnp.where(spot == 8 + start // D, mine, 0.0))
        table = a_ref[1, layer, 2 * size : 2 * size + 16, 0:TABLE_PAD]
        table_o[layer] = dot_tn(table, same)[0:TABLE, :]


def unpack_gradients(final_m, final_a):
    n_row = lax.axis_size("row")
    size = D // n_row
    shapes = [
        (2, size, 3 * D),
        (2, 2, size),
        (2, size, D),
        (2, size),
        (2, size, 4 * D),
        (2, 4 * size),
        (2, 4 * size, D),
        (2, size),
        (2, 2, size),
        (2, 2, size),
        (2, TABLE, HEADS),
    ]
    return pl.pallas_call(
        functools.partial(unpack_kernel, n_row),
        out_shape=[jax.ShapeDtypeStruct(shape, f32) for shape in shapes],
        compiler_params=pltpu.CompilerParams(vmem_limit_bytes=VMEM_LIMIT),
        name="unpack_gradients",
    )(final_m, final_a)


def exchange(values):
    return lax.all_to_all(values, ("clip", "row"), split_axis=0, concat_axis=0, tiled=True)


def body(
    inputs,
    cotangent,
    source_of,
    split_row,
    qkv_weight,
    qv_bias,
    proj_weight,
    proj_bias,
    fc1_weight,
    fc1_bias,
    fc2_weight,
    fc2_bias,
    norm_gain,
    norm_bias,
    rel_table,
):
    clip_count = lax.axis_size("clip")
    row_count = lax.axis_size("row")
    tokens = inputs.shape[0]
    block_rows = tokens // (clip_count * row_count)
    grid_rows = tokens // GRID_COLS
    slot_rows = grid_rows * row_count
    window_rows = grid_rows // WIN
    part = D // row_count

    placing = source_of // tokens * block_rows + source_of % block_rows
    placing = placing.reshape(window_rows, 2, SHIFT, WIN_COLS, 2, SHIFT)
    placing = placing.transpose(0, 3, 1, 4, 2, 5).reshape(tokens)
    middle = lax.axis_index("row") * grid_rows + WIN * (1 + jnp.arange(window_rows))
    row_cut = ((middle == split_row[0]) | (middle == slot_rows)).astype(jnp.int32)
    col_cut = (jnp.arange(WIN_COLS) == WIN_COLS - 1).astype(jnp.int32)
    cuts = (32 * row_cut[:, None] + 16 * col_cut[None, :]).reshape(-1)

    cuts = jnp.concatenate([jnp.zeros_like(cuts), cuts])

    vectors = jnp.concatenate(
        [qv_bias, proj_bias[:, None], fc2_bias[:, None], norm_gain, norm_bias], axis=1
    )
    vectors = jnp.concatenate(
        [
            jnp.pad(vectors, ((0, 0), (0, 0), (0, D - part))),
            jnp.pad(fc1_bias[:, None], ((0, 0), (0, 7), (0, D - 4 * part))),
        ],
        axis=1,
    ).reshape(32, D)
    if not can_swap(tokens, clip_count * row_count):
        inputs, cotangent = exchange(inputs), exchange(cotangent)
    saved, upstream, out_rows, full, vec_rows = forward_layers(
        cuts,
        placing,
        inputs,
        cotangent,
        (qkv_weight, proj_weight, fc1_weight, fc2_weight),
        vectors,
        rel_table,
    )
    output, input_grad, *finals = backward_layers(placing, upstream, out_rows, saved, full, vec_rows)
    if not can_swap(tokens, clip_count * row_count):
        output, input_grad = exchange(output), exchange(input_grad)
    input_grad = input_grad.astype(f32)
    totals = unpack_gradients(*finals)
    return (output, input_grad, *totals)


def solution(mesh):
    placed = (
        P(("clip", "row"), None),
        P(("clip", "row"), None),
        P(("clip", "row")),
        P("clip"),
        P(None, "row", None),
        P(None, None, "row"),
        P(None, "row", None),
        P(None, "row"),
        P(None, "row", None),
        P(None, "row"),
        P(None, "row", None),
        P(None, "row"),
        P(None, None, "row"),
        P(None, None, "row"),
        P(),
    )
    return jax.shard_map(
        body,
        mesh=mesh,
        in_specs=placed,
        out_specs=(
            P(("clip", "row"), None),
            P(("clip", "row"), None),
            P(None, "row", None),
            P(None, None, "row"),
            P(None, "row", None),
            P(None, "row"),
            P(None, "row", None),
            P(None, "row"),
            P(None, "row", None),
            P(None, "row"),
            P(None, None, "row"),
            P(None, None, "row"),
            P(),
        ),
        check_vma=False,
    )
```

```python
import functools

import jax
import jax.numpy as jnp
import numpy as np
from jax import lax
from jax.experimental import pallas as pl
from jax.experimental.pallas import tpu as pltpu
from jax.sharding import PartitionSpec as P

WIN = 8
SHIFT = 4
GRID_COLS = 64
EPSILON = 1e-05
MASKED = -1000000000.0
ROOT_HALF = 0.7071067811865476
INV_ROOT_TAU = 0.3989422804014327

HEADS = 16
HEAD_DIM = 24
D = HEADS * HEAD_DIM
GROUP = 8
CELL = WIN * WIN
BLOCK = SHIFT * SHIFT
WIN_COLS = GRID_COLS // WIN
SPREAD = 2 * WIN - 1
TABLE = SPREAD * SPREAD
TABLE_PAD = 256
SCALE = HEAD_DIM**-0.5
CHUNK = 256
CHUNK_WINS = CHUNK // CELL
VMEM_LIMIT = 56 * 1024 * 1024

MESH = pl.DeviceIdType.MESH
f32 = jnp.float32
bf16 = jnp.bfloat16


def window_places():
    spot = np.arange(CELL)
    row = (spot // 32) * SHIFT + (spot % BLOCK) // SHIFT
    col = (spot // BLOCK % 2) * SHIFT + spot % SHIFT
    return row, col


def head_masks():
    feature = np.arange(D) // HEAD_DIM
    rows = (feature[None, :] == np.arange(HEADS)[:, None]).astype(np.float32)
    wide = np.stack(
        [
            np.repeat(rows[GROUP * g : GROUP * (g + 1), 128 * g : 128 * g + 256], CELL, axis=0)
            for g in range(2)
        ]
    )
    return rows, wide


def table_constants():
    row, col = window_places()
    natural = row * WIN + col
    lanes = np.zeros((2, TABLE_PAD, 128), np.float32)
    for half in range(2):
        lanes[half, row * SPREAD + col, half * CELL + np.arange(CELL)] = 1.0
    order = np.zeros((CELL, CELL), np.float32)
    order[np.arange(CELL), natural] = 1.0
    back = np.zeros((CELL, CELL), np.float32)
    back[row * WIN + (WIN - 1 - col), np.arange(CELL)] = 1.0
    return lanes, order, back


def dot_nn(a, b):
    return lax.dot_general(a, b, (((1,), (0,)), ((), ())), preferred_element_type=f32)


def dot_nt(a, b):
    return lax.dot_general(a, b, (((1,), (1,)), ((), ())), preferred_element_type=f32)


def dot_tn(a, b):
    return lax.dot_general(a, b, (((0,), (0,)), ((), ())), preferred_element_type=f32)


def dot_exact(a, b, dims):
    return lax.dot_general(
        a, b, (dims, ((), ())), precision=lax.Precision.HIGHEST, preferred_element_type=f32
    )


def split(values):
    high = values.astype(bf16)
    rest = values - high.astype(f32)
    middle = rest.astype(bf16)
    return high, middle, (rest - middle.astype(f32)).astype(bf16)


def whole(shape):
    zeros = (0,) * len(shape)
    return pl.BlockSpec(shape, lambda i: zeros)


def rows_of(shape):
    return pl.BlockSpec(shape, lambda i: (i, 0))


def norm_parts(values):
    centred = values - jnp.mean(values, axis=-1, keepdims=True)
    inverse = lax.rsqrt(jnp.mean(centred * centred, axis=-1, keepdims=True) + EPSILON)
    return centred * inverse, inverse


def norm_back(upstream, normal, inverse, gain):
    scaled = upstream * gain
    centred = scaled - jnp.mean(scaled, axis=-1, keepdims=True)
    return inverse * (centred - normal * jnp.mean(scaled * normal, axis=-1, keepdims=True))


def column_sum(values):
    return jnp.sum(values, axis=0, keepdims=True)


def bias_rows(table_ref, lanes_ref, order_ref, out_ref, wide_ref):
    for layer in range(2):
        for head in range(HEADS):
            pair, half = divmod(head, 2)
            spread = jnp.broadcast_to(table_ref[layer, head : head + 1, :], (WIN, TABLE_PAD))
            for i in range(WIN):
                at = CELL * pair + WIN * i
                wide_ref[at : at + WIN, TABLE_PAD * half : TABLE_PAD * (half + 1)] = pltpu.roll(
                    spread, (SPREAD * i - 112) % TABLE_PAD, 1, stride=1, stride_axis=0
                )
        picked = sum(dot_nn(part, lanes_ref[...]) for part in reversed(split(wide_ref[...])))
        joined = jnp.concatenate(
            [picked[CELL * pair : CELL * (pair + 1), :] for pair in range(HEADS // 2)], axis=1
        )
        out_ref[layer] = sum(dot_nn(order_ref[...], part) for part in reversed(split(joined)))


def table_rows(grads, lanes_ref, back_ref):
    turned = sum(dot_nn(back_ref[...], part) for part in reversed(split(grads)))
    stacked = jnp.concatenate([turned[:, 128 * i : 128 * (i + 1)] for i in range(HEADS // 2)], axis=0)
    spread = sum(dot_nt(part, lanes_ref[...]) for part in reversed(split(stacked)))
    rows = []
    for head in range(HEADS):
        pair, half = divmod(head, 2)
        total = jnp.zeros((WIN, TABLE_PAD), f32)
        for i in range(WIN):
            at = CELL * pair + WIN * i
            total += pltpu.roll(
                spread[at : at + WIN, TABLE_PAD * half : TABLE_PAD * (half + 1)],
                (112 - SPREAD * i - (WIN - 1)) % TABLE_PAD,
                1,
                stride=1,
                stride_axis=0,
            )
        rows.append(column_sum(total))
    return jnp.concatenate(rows, axis=0)


def quarter(window, sub):
    return pl.ds(CELL * window + BLOCK * sub, BLOCK)


def assemble_back(main_ref, edge_ref, out_ref):
    windows = main_ref.shape[0] // CELL
    for window in range(windows):
        wr, wc = divmod(window, WIN_COLS)
        before = (wc - 1) % WIN_COLS
        out_ref[quarter(window, 3), :] = main_ref[quarter(window, 0), :].astype(out_ref.dtype)
        out_ref[quarter(window, 2), :] = main_ref[
            quarter(wr * WIN_COLS + before, 1), :
        ].astype(out_ref.dtype)
        for sub, col, piece in ((1, wc, 0), (0, before, 1)):
            if wr == 0:
                value = edge_ref[pl.ds(2 * BLOCK * col + BLOCK * piece, BLOCK), :]
            else:
                value = main_ref[quarter((wr - 1) * WIN_COLS + col, 2 + piece), :]
            out_ref[quarter(window, sub), :] = value.astype(out_ref.dtype)


def assemble_ahead(main_ref, edge_ref, out_ref, window_rows):
    last = main_ref.shape[0] // CELL // WIN_COLS - 1
    for wr in window_rows:
        for wc in range(WIN_COLS):
            window = wr * WIN_COLS + wc
            after = (wc + 1) % WIN_COLS
            out_ref[quarter(window, 0), :] = main_ref[quarter(window, 3), :].astype(out_ref.dtype)
            out_ref[quarter(window, 1), :] = main_ref[
                quarter(wr * WIN_COLS + after, 2), :
            ].astype(out_ref.dtype)
            for sub, col, piece in ((2, wc, 1), (3, after, 0)):
                if wr == last:
                    value = edge_ref[pl.ds(2 * BLOCK * col + BLOCK * piece, BLOCK), :]
                else:
                    value = main_ref[quarter((wr + 1) * WIN_COLS + col, piece), :]
                out_ref[quarter(window, sub), :] = value.astype(out_ref.dtype)


class Place:
    def __init__(self, n_row, n_far):
        clip = lax.axis_index("clip")
        self.n_row, self.n_far = n_row, n_far
        self.core, self.far, self.row = clip % 2, clip // 2, lax.axis_index("row")
        self.n = 2 * n_far * n_row
        self.index = clip * n_row + self.row

    def index_at(self, d):
        return (self.index + d) % self.n

    def device(self, d):
        at = self.index_at(d)
        return (at // self.n_row, at % self.n_row)

    def row_at(self, d):
        return (self.row + d) % self.n_row

    def far_at(self, d):
        return (self.far + d) % self.n_far

    def twin(self):
        return (2 * self.far + 1 - self.core, self.row)

    def at_row(self, row):
        return (2 * self.far + self.core, row)

    def in_row(self, d):
        return self.at_row(self.row_at(d))

    def at_far(self, far):
        return (2 * far + self.core, self.row)

    def along(self, d):
        return self.at_far(self.far_at(d))

    def partners(self, far=True):
        found = [self.twin()] + [self.in_row(d) for d in range(1, self.n_row)]
        return found + ([self.along(d) for d in range(1, self.n_far)] if far else [])


def meet(partners):
    barrier = pltpu.get_barrier_semaphore()
    for partner in partners:
        pl.semaphore_signal(barrier, inc=1, device_id=partner, device_id_type=MESH)
    pl.semaphore_wait(barrier, len(partners))


def send(src, dst, send_sem, recv_sem, target):
    copy = pltpu.make_async_remote_copy(
        src_ref=src,
        dst_ref=dst,
        send_sem=send_sem,
        recv_sem=recv_sem,
        device_id=target,
        device_id_type=MESH,
    )
    copy.start()
    return copy


def remote(src, dst, send_sem, recv_sem, target):
    return pltpu.make_async_remote_copy(
        src_ref=src,
        dst_ref=dst,
        send_sem=send_sem,
        recv_sem=recv_sem,
        device_id=target,
        device_id_type=MESH,
    )


def can_swap(tokens, n):
    return tokens // n % 16 == 0


def meet_all(place):
    barrier = pltpu.get_barrier_semaphore()

    def greet(d, carry):
        pl.semaphore_signal(barrier, inc=1, device_id=place.device(d), device_id_type=MESH)
        return carry

    lax.fori_loop(1, place.n, greet, 0)
    pl.semaphore_wait(barrier, place.n - 1)


def swap_block(place, ref, index):
    count = ref.shape[0] // place.n
    return ref.at[pl.ds(pl.multiple_of(index * count, 16), count), :]


def swap_own(place, src, dst, sem):
    return pltpu.make_async_copy(
        swap_block(place, src, place.index), swap_block(place, dst, place.index), sem.at[0, 0]
    )


def swap_copy(place, src, dst, sem, d, owner):
    return remote(
        swap_block(place, src, place.index_at(d)),
        swap_block(place, dst, owner),
        sem.at[0, d],
        sem.at[1, d],
        place.device(d),
    )


def swap_start(place, src, dst, sem):
    def work(d, carry):
        swap_copy(place, src, dst, sem, d, place.index).start()
        return carry

    lax.fori_loop(1, place.n, work, 0)


def swap_wait(place, src, dst, sem):
    def work(d, carry):
        swap_copy(place, src, dst, sem, d, place.index_at(place.n - d)).wait_recv()
        return carry

    lax.fori_loop(1, place.n, work, 0)


def swap_end(place, src, dst, sem):
    def work(d, carry):
        swap_copy(place, src, dst, sem, d, place.index).wait_send()
        return carry

    lax.fori_loop(1, place.n, work, 0)


def row_share(n_row):
    return D // n_row


HEIGHTS = (1, 1, 1, 4)
KINDS = ((0, 1), (2, 3))


def shard_half(height, core):
    low = -(-height // 32) * 16
    return (0, low) if core == 0 else (low, height - low)


def forward_kernel(
    n_row,
    n_far,
    swap,
    split_ref,
    place_col,
    place_row,
    x_in,
    c_in,
    qkv_i,
    proj_i,
    fc1_i,
    fc2_i,
    qv_bias,
    proj_bias,
    fc1_bias,
    fc2_bias,
    gain_ref,
    shift_ref,
    table_ref,
    lanes_ref,
    order_ref,
    heads_ref,
    wide_heads_ref,
    x_out,
    qkv_out,
    prob_out,
    att_out,
    mid_out,
    act_out,
    slope_out,
    up_out,
    y_out,
    qkv_wo,
    proj_wo,
    fc1_wo,
    fc2_wo,
    vec_out,
    x_got,
    c_got,
    qkv_s,
    proj_s,
    fc1_s,
    fc2_s,
    vec_wide,
    vec_mine,
    vec_got,
    qkv_b,
    fc1_b,
    table_s,
    bias_s,
    wide_s,
    x_s,
    y_s,
    c_s,
    order_s,
    edge_out,
    edge_in,
    x_sem,
    c_sem,
    own_sem,
    row_sem,
    twin_sem,
    vec_sem,
    edge_sem,
    out_sem,
):
    step = pl.program_id(0)
    tokens = x_s.shape[0]
    chunks = tokens // CHUNK
    layer = step // (2 * chunks)
    kind = step // chunks % 2
    chunk = (step + layer * kind * (chunks // 2)) % chunks
    place = Place(n_row, n_far)
    size = row_share(n_row)
    shards = (qkv_i, proj_i, fc1_i, fc2_i)
    kept = (qkv_s, proj_s, fc1_s, fc2_s)
    outs = (qkv_wo, proj_wo, fc1_wo, fc2_wo)
    window_rows = tokens // CELL // WIN_COLS
    last_row = (window_rows - 1) * WIN_COLS
    square = n_row == 4
    direct = range(2 if square else n_row - 1)
    slots = range(n_row - 1)
    if not swap:
        x_got, c_got = x_in, c_in

    def own(l, w):
        return pltpu.make_async_copy(
            shards[w].at[l], spot(l, w, place.row, 0, HEIGHTS[w] * size), own_sem.at[l, w]
        )

    def spot(l, w, owner, first, count):
        at = pl.multiple_of(owner * HEIGHTS[w] * size + first, 16)
        return kept[w].at[l, pl.ds(at, count), :]

    def neighbour(slot):
        row = place.row
        return (row + 1 - 2 * (row % 2), (row + 2) % 4, 3 - row)[slot]

    def source(slot):
        return neighbour(slot) if square else place.row_at(n_row - 1 - slot)

    def target(slot):
        return place.at_row(neighbour(slot) if square else place.row_at(slot + 1))

    def push(l, core, w, slot, owner=None):
        first, count = shard_half(HEIGHTS[w] * size, core)
        return remote(
            shards[w].at[l, pl.ds(first, count), :],
            spot(l, w, place.row if owner is None else owner, first, count),
            row_sem.at[0, l, w, slot],
            row_sem.at[1, l, w, slot],
            target(slot),
        )

    def relay(l, core, w):
        axis = (w + core) % 2
        here = spot(l, w, source(axis), *shard_half(HEIGHTS[w] * size, core))
        return remote(
            here, here, row_sem.at[0, l, w, 2], row_sem.at[1, l, w, 2], target(1 - axis)
        )

    def hand(l, core, w, slot):
        here = spot(l, w, source(slot), *shard_half(HEIGHTS[w] * size, core))
        return remote(
            here, here, twin_sem.at[0, l, w, slot], twin_sem.at[1, l, w, slot], place.twin()
        )

    def by_core(work):
        for core in range(2):
            pl.when(place.core == core)(functools.partial(work, core))

    def start_weights(l, k):
        def work(core):
            for w in KINDS[k]:
                for slot in direct:
                    push(l, core, w, slot).start()

        by_core(work)

    def pass_weights(l, k):
        def work(core):
            for w in KINDS[k]:
                for slot in direct:
                    push(l, core, w, slot, source(slot)).wait_recv()
                    if square and slot == (w + core) % 2:
                        relay(l, core, w).start()
                    hand(l, core, w, slot).start()

        by_core(work)

    def pass_relayed(l, k):
        def work(core):
            for w in KINDS[k]:
                push(l, core, w, 2, source(2)).wait_recv()
                hand(l, core, w, 2).start()

        if square:
            by_core(work)

    def wait_weights(l, k):
        def work(core):
            for w in KINDS[k]:
                for slot in slots:
                    hand(l, 1 - core, w, slot).wait_recv()

        by_core(work)
        for w in KINDS[k]:
            own(l, w).wait()

    def end_weights():
        def work(core):
            for l in range(2):
                for w in range(4):
                    for slot in direct:
                        push(l, core, w, slot).wait_send()
                    if square:
                        relay(l, core, w).wait_send()
                    for slot in slots:
                        hand(l, core, w, slot).wait_send()

        by_core(work)

    def vector_copy(d):
        return remote(
            vec_mine,
            vec_got.at[place.row],
            vec_sem.at[0, d - 1],
            vec_sem.at[1, d - 1],
            place.in_row(d),
        )

    def edge_copy(which):
        return remote(
            edge_out.at[which],
            edge_in.at[which],
            edge_sem.at[0, which],
            edge_sem.at[1, which],
            place.in_row(1 if which == 2 else n_row - 1),
        )

    def pack_edge(which, values, first_window, first_sub):
        for col in range(WIN_COLS):
            at = CELL * (first_window + col) + BLOCK * first_sub
            edge_out[which, 2 * BLOCK * col : 2 * BLOCK * (col + 1), :] = values[
                at : at + 2 * BLOCK, :
            ].astype(bf16)

    def pick_rows(values, out):
        for c in range(chunks):
            rows = slice(CHUNK * c, CHUNK * (c + 1))
            spots = lax.broadcasted_iota(jnp.int32, (CHUNK, tokens), 1)
            pick = jnp.where(spots == place_col[rows, :], 1.0, 0.0).astype(bf16)
            out[rows, :] = dot_nn(pick, values[...]).astype(out.dtype)

    @pl.when(step == 0)
    def _():
        for l in range(2):
            for w in range(4):
                own(l, w).start()
        if swap:
            swap_own(place, x_in, x_got, x_sem).start()
            swap_own(place, c_in, c_got, c_sem).start()
            meet_all(place)
            swap_start(place, x_in, x_got, x_sem)
        else:
            meet(place.partners(far=False))
        start_weights(0, 0)
        vec_wide[...] = jnp.zeros_like(vec_wide)
        for l in range(2):
            parts = (
                qv_bias[l],
                proj_bias[l : l + 1],
                fc2_bias[l : l + 1],
                gain_ref[l],
                shift_ref[l],
            )
            vec_wide[16 * l : 16 * l + 8, 0:size] = jnp.concatenate(
                [part.astype(f32) for part in parts], axis=0
            )
            vec_wide[16 * l + 8 : 16 * l + 9, 0 : 4 * size] = fc1_bias[l : l + 1].astype(f32)
        vec_mine[...] = vec_wide[...].astype(bf16)
        for d in range(1, n_row):
            vector_copy(d).start()
        mine = pltpu.make_async_copy(vec_mine, vec_got.at[place.row], out_sem.at[4])
        mine.start()
        eye = lax.broadcasted_iota(jnp.int32, (TABLE, TABLE_PAD), 0) == lax.broadcasted_iota(
            jnp.int32, (TABLE, TABLE_PAD), 1
        )
        eye = jnp.where(eye, 1.0, 0.0).astype(bf16)
        for l in range(2):
            table_s[l] = sum(dot_tn(part, eye) for part in reversed(split(table_ref[l])))
        bias_rows(table_s, lanes_ref, order_ref, bias_s, wide_s)
        mine.wait()
        for d in range(1, n_row):
            vector_copy(d).wait()
        for l in range(2):
            shares = [vec_got[r, 16 * l : 16 * (l + 1), :].astype(f32) for r in range(n_row)]
            rows = jnp.concatenate([share[0:8, 0:size] for share in shares], axis=1)
            vec_out[l] = rows
            qkv_b[l, 0:1, 0:D] = rows[0:1]
            qkv_b[l, 0:1, D : 2 * D] = jnp.zeros((1, D), f32)
            qkv_b[l, 0:1, 2 * D : 3 * D] = rows[1:2]
            fc1_b[l, 0:1, :] = jnp.concatenate(
                [share[8:9, 0 : 4 * size] for share in shares], axis=1
            )
        pass_weights(0, 0)
        start_weights(0, 1)
        if swap:
            swap_wait(place, x_in, x_got, x_sem)
            swap_own(place, x_in, x_got, x_sem).wait()
        pick_rows(x_got, x_s)
        pass_relayed(0, 0)
        wait_weights(0, 0)
        start_weights(1, 0)

    @pl.when(step == 1)
    def _():
        pass_weights(0, 1)

    @pl.when(step == chunks - 1)
    def _():
        pass_relayed(0, 1)
        start_weights(1, 1)

    @pl.when(step == chunks)
    def _():
        wait_weights(0, 1)
        pass_weights(1, 0)
        if swap:
            swap_start(place, c_in, c_got, c_sem)

    @pl.when(step == chunks + 2)
    def _():
        pass_relayed(1, 0)

    @pl.when(step == 2 * chunks - 1)
    def _():
        pass_weights(1, 1)

    @pl.when(step == 2 * chunks)
    def _():
        wait_weights(1, 0)
        assemble_ahead(y_s, edge_in.at[0], x_s, range(window_rows - 1))

    @pl.when(step == 2 * chunks + chunks // 2)
    def _():
        pass_relayed(1, 1)
        edge_copy(0).wait_recv()
        assemble_ahead(y_s, edge_in.at[0], x_s, range(window_rows - 1, window_rows))

    @pl.when(step == 3 * chunks)
    def _():
        wait_weights(1, 1)
        for w in range(4):
            pltpu.make_async_copy(kept[w], outs[w], out_sem.at[w]).start()
        if swap:
            swap_wait(place, c_in, c_got, c_sem)
            swap_own(place, c_in, c_got, c_sem).wait()
        pick_rows(c_got, c_s)
        pack_edge(1, c_s, 0, 0)
        edge_copy(1).start()

    here = pl.ds(pl.multiple_of(chunk * CHUNK, CHUNK), CHUNK)

    @pl.when(kind == 0)
    def _():
        x = x_s[here, :]
        x_out[0] = x
        normal, _ = norm_parts(x)
        hidden = (normal * vec_out[layer, 4:5, :] + vec_out[layer, 6:7, :]).astype(bf16)
        qkv_out[0] = (dot_nn(hidden, qkv_s[layer]) + qkv_b[layer]).astype(bf16)
        wide = (CELL, GROUP * CELL)
        apart = lax.broadcasted_iota(jnp.int32, wide, 0) ^ lax.broadcasted_iota(jnp.int32, wide, 1)
        for k in range(CHUNK_WINS):
            rows = slice(CELL * k, CELL * (k + 1))
            window = chunk * CHUNK_WINS + k
            middle = (place.row * window_rows + window // WIN_COLS + 1) * WIN
            row_cut = (middle == split_ref[0]) | (middle == n_row * window_rows * WIN)
            col_cut = window % WIN_COLS == WIN_COLS - 1
            cut = layer * (jnp.where(row_cut, 32, 0) + jnp.where(col_cut, 16, 0))
            keep = (apart & cut) == 0
            mixed = []
            for g in range(2):
                q = qkv_out[0, rows, 128 * g : 128 * g + 256]
                key = qkv_out[0, rows, D + 128 * g : D + 128 * g + 256]
                val = qkv_out[0, rows, 2 * D + 128 * g : 2 * D + 128 * g + 256]
                q_wide = jnp.concatenate([q] * GROUP, axis=0) * wide_heads_ref[g]
                lanes = slice(GROUP * CELL * g, GROUP * CELL * (g + 1))
                scores = dot_nt(key, q_wide) * SCALE + bias_s[layer, :, lanes]
                scores = jnp.where(keep, scores, MASKED)
                e = jnp.exp(scores - jnp.max(scores, axis=0, keepdims=True))
                prob = (e * (1.0 / jnp.sum(e, axis=0, keepdims=True))).astype(bf16)
                prob_out[0, rows, lanes] = prob
                mixed.append(gather_heads(dot_tn(prob, val), heads_ref, g))
            att_out[0, rows, :] = join_groups(*mixed).astype(bf16)
        mid = x + (dot_nn(att_out[0], proj_s[layer]) + vec_out[layer, 2:3, :])
        x_s[here, :] = mid
        mid_out[0] = mid

    @pl.when(kind == 1)
    def _():
        mid = x_s[here, :]
        normal, _ = norm_parts(mid)
        hidden = (normal * vec_out[layer, 5:6, :] + vec_out[layer, 7:8, :]).astype(bf16)
        u = dot_nn(hidden, fc1_s[layer]) + fc1_b[layer]
        cdf = 0.5 * (1.0 + lax.erf(u * ROOT_HALF))
        act_out[0] = (u * cdf).astype(bf16)
        slope_out[0] = (cdf + u * (jnp.exp(-0.5 * u * u) * INV_ROOT_TAU)).astype(bf16)
        y_s[here, :] = mid + (dot_nn(act_out[0], fc2_s[layer]) + vec_out[layer, 3:4, :])

    @pl.when(step == chunks + chunks // 2 - 1)
    def _():
        pack_edge(0, y_s, 0, 0)
        edge_copy(0).start()

    @pl.when(step == 3 * chunks + chunks // 2 - 1)
    def _():
        pack_edge(2, y_s, last_row, 2)
        edge_copy(2).start()

    @pl.when(step == 4 * chunks - 1)
    def _():
        edge_copy(2).wait_recv()
        assemble_back(y_s, edge_in.at[2], order_s)
        for c in range(chunks):
            rows = slice(CHUNK * c, CHUNK * (c + 1))
            spots = lax.broadcasted_iota(jnp.int32, (CHUNK, tokens), 0) + CHUNK * c
            pick = jnp.where(spots == place_row[...], 1.0, 0.0).astype(bf16)
            y_out[rows, :] = dot_nn(pick, order_s[...]).astype(bf16)
        edge_copy(1).wait_recv()
        assemble_ahead(c_s, edge_in.at[1], up_out, range(window_rows))
        end_weights()
        for which in range(3):
            edge_copy(which).wait_send()
        for w in range(4):
            pltpu.make_async_copy(kept[w], outs[w], out_sem.at[w]).wait()
        if swap:
            swap_end(place, x_in, x_got, x_sem)
            swap_end(place, c_in, c_got, c_sem)


def gather_heads(spread, heads_ref, g):
    total = None
    for h in range(GROUP):
        part = spread[CELL * h : CELL * (h + 1), :] * heads_ref[
            GROUP * g + h : GROUP * g + h + 1, 128 * g : 128 * g + 256
        ]
        total = part if total is None else total + part
    return total


def join_groups(low, high):
    return jnp.concatenate([low[:, :128], low[:, 128:] + high[:, :128], high[:, 128:]], axis=1)


def forward_layers(split_row, placing, x_in, c_in, shards, vectors, rel_table):
    n_row, n_far = lax.axis_size("row"), lax.axis_size("clip") // 2
    n = 2 * n_row * n_far
    tokens = x_in.shape[0]
    chunks = tokens // CHUNK
    swap = can_swap(tokens, n)
    heads, wide = head_masks()
    lanes, order, _ = table_constants()
    ff = shards[2].shape[2]
    anywhere = pl.BlockSpec(memory_space=pl.ANY)
    patches = anywhere if swap else whole((tokens, D))
    small = (
        *vectors,
        rel_table,
        jnp.asarray(lanes.reshape(2 * TABLE_PAD, 128), dtype=bf16),
        jnp.asarray(order, dtype=bf16),
        jnp.asarray(heads),
        jnp.asarray(wide, dtype=bf16),
    )
    full = [(2, shard.shape[1] * n_row, shard.shape[2]) for shard in shards]

    def attention_block(i):
        kind = i // chunks % 2
        return i // (2 * chunks), (1 - kind) * (i % chunks) + kind * (chunks - 1), 0

    def forward_block(i):
        layer, kind = i // (2 * chunks), i // chunks % 2
        half = layer * (chunks // 2)
        return layer, kind * ((i + half) % chunks) + (1 - kind) * half, 0

    saved = [
        (D, f32, attention_block),
        (3 * D, bf16, attention_block),
        (HEADS * CELL, bf16, attention_block),
        (D, bf16, attention_block),
        (D, f32, attention_block),
        (ff, bf16, forward_block),
        (ff, bf16, forward_block),
    ]
    dma = pltpu.SemaphoreType.DMA
    results = pl.pallas_call(
        functools.partial(forward_kernel, n_row, n_far, swap),
        grid=(4 * chunks,),
        in_specs=[
            pl.BlockSpec(memory_space=pltpu.SMEM),
            whole((tokens, 1)),
            whole((1, tokens)),
            patches,
            patches,
        ]
        + [anywhere] * 4
        + [whole(value.shape) for value in small],
        out_specs=[pl.BlockSpec((1, CHUNK, width), block) for width, _, block in saved]
        + [whole((tokens, D))] * 2
        + [anywhere] * 4
        + [whole((2, 8, D))],
        out_shape=[jax.ShapeDtypeStruct((2, tokens, width), kind) for width, kind, _ in saved]
        + [jax.ShapeDtypeStruct((tokens, D), bf16)] * 2
        + [jax.ShapeDtypeStruct(shape, bf16) for shape in full]
        + [jax.ShapeDtypeStruct((2, 8, D), f32)],
        scratch_shapes=[
            pltpu.VMEM((tokens if swap else 16, D), bf16),
            pltpu.VMEM((tokens if swap else 16, D), bf16),
            *[pltpu.VMEM(shape, bf16) for shape in full],
            pltpu.VMEM((32, D), f32),
            pltpu.VMEM((32, D), bf16),
            pltpu.VMEM((n_row, 32, D), bf16),
            pltpu.VMEM((2, 1, 3 * D), f32),
            pltpu.VMEM((2, 1, ff), f32),
            pltpu.VMEM((2, HEADS, TABLE_PAD), f32),
            pltpu.VMEM((2, CELL, HEADS * CELL), f32),
            pltpu.VMEM((HEADS // 2 * CELL, 2 * TABLE_PAD), f32),
            pltpu.VMEM((tokens, D), f32),
            pltpu.VMEM((tokens, D), f32),
            pltpu.VMEM((tokens, D), bf16),
            pltpu.VMEM((tokens, D), bf16),
            pltpu.VMEM((3, WIN_COLS * 2 * BLOCK, D), bf16),
            pltpu.VMEM((3, WIN_COLS * 2 * BLOCK, D), bf16),
            dma((2, n if swap else 1)),
            dma((2, n if swap else 1)),
            dma((2, 4)),
            dma((2, 2, 4, n_row - 1)),
            dma((2, 2, 4, n_row - 1)),
            dma((2, n_row - 1)),
            dma((2, 3)),
            dma((5,)),
        ],
        compiler_params=pltpu.CompilerParams(
            collective_id=0, has_side_effects=True, vmem_limit_bytes=VMEM_LIMIT
        ),
        name="forward_layers",
    )(
        split_row,
        placing.reshape(tokens, 1),
        placing.reshape(1, tokens),
        x_in,
        c_in,
        *shards,
        *small,
    )
    return results[:7], results[7], results[8], results[9:13], results[13]


BATCHES = ((1, 0), (1, 1), (1, 2), (0, 0), (0, 1), (0, 2))


def batch_rows(n_row, kind):
    size = row_share(n_row)
    low = shard_half(size, 0)[1]
    return (2 * size, 2 * size + low, size + low + 16)[kind]


def piece_rows(n_row, n_far, kind):
    return -(-batch_rows(n_row, kind) // (16 * n_far)) * 16


def backward_kernel(
    n_row,
    n_far,
    swap,
    place_row,
    up_ref,
    rows_in,
    x_ref,
    qkv_ref,
    prob_ref,
    att_ref,
    mid_ref,
    act_ref,
    slope_ref,
    qkv_w,
    proj_w,
    fc1_w,
    fc2_w,
    vec_ref,
    heads_ref,
    wide_heads_ref,
    lanes_ref,
    back_ref,
    rows_out,
    grad_out,
    final_0,
    final_1,
    final_2,
    vec_g,
    fc1_bg,
    table_g,
    g_s,
    h1_s,
    dt_s,
    ga_s,
    h2_s,
    du_s,
    gz_s,
    grad_rows,
    edge_out,
    edge_in,
    *refs,
):
    packs, got_as, got_bs, out_cs, got_cs, finals = (refs[3 * i : 3 * i + 3] for i in range(6))
    rows_sem, grad_sem, edge_sem, a_sem, b_sem, c_sem, d_sem, e_sem, done_sem = refs[18:]
    step = pl.program_id(0)
    tokens = g_s.shape[1]
    chunks = tokens // CHUNK
    layer = 1 - step // (2 * chunks)
    kind = step // chunks % 2
    chunk = (step + chunks // 2) % chunks
    place = Place(n_row, n_far)
    core, row, far = place.core, place.row, place.far
    size = row_share(n_row)
    low = shard_half(size, 0)[1]
    last_row = (tokens // CELL // WIN_COLS - 1) * WIN_COLS
    here = pl.ds(pl.multiple_of(chunk * CHUNK, CHUNK), CHUNK)

    def edge_copy():
        return remote(edge_out, edge_in, edge_sem.at[0], edge_sem.at[1], place.in_row(1))

    def start_rows(source, target, sem):
        if swap:
            swap_own(place, source, target, sem).start()
            swap_start(place, source, target, sem)
        else:
            pltpu.make_async_copy(source, target, sem.at[0, 0]).start()

    def unpick_rows(values, out):
        for c in range(chunks):
            rows = slice(CHUNK * c, CHUNK * (c + 1))
            spots = lax.broadcasted_iota(jnp.int32, (CHUNK, tokens), 0) + CHUNK * c
            pick = jnp.where(spots == place_row[...], 1.0, 0.0).astype(bf16)
            out[rows, :] = dot_nn(pick, values).astype(bf16)

    def part(ref, b, at):
        rows = got_cs[BATCHES[b][1]].shape[2]
        return ref.at[BATCHES[b][0], pl.ds(pl.multiple_of(at * rows, 16), rows), :]

    def copy_a(b):
        l, k = BATCHES[b]
        return remote(
            packs[k].at[l, 1 - core], got_as[k].at[l], a_sem.at[0, b], a_sem.at[1, b], place.twin()
        )

    def copy_b(b, d):
        l, k = BATCHES[b]
        return remote(
            packs[k].at[l, core, place.row_at(d)],
            got_bs[k].at[l, d - 1],
            b_sem.at[0, b, d - 1],
            b_sem.at[1, b, d - 1],
            place.in_row(d),
        )

    def copy_c(b, d):
        l, k = BATCHES[b]
        return remote(
            part(out_cs[k], b, place.far_at(d)),
            got_cs[k].at[l, d - 1],
            c_sem.at[0, b, d - 1],
            c_sem.at[1, b, d - 1],
            place.along(d),
        )

    def copy_d(b, d, owner):
        spot = part(finals[BATCHES[b][1]].at[core], b, owner)
        return remote(spot, spot, d_sem.at[0, b, d - 1], d_sem.at[1, b, d - 1], place.along(d))

    def copy_e(b, d, half):
        spot = part(finals[BATCHES[b][1]].at[half], b, place.far_at((n_far - d) % n_far))
        return remote(spot, spot, e_sem.at[0, b, d], e_sem.at[1, b, d], place.twin())

    def sum_cores(b):
        l, k = BATCHES[b]
        copy_a(b).wait_recv()
        for d in range(1, n_row):
            r = place.row_at(d)
            packs[k][l, core, r] = packs[k][l, core, r] + got_as[k][l, r]
            copy_b(b, d).start()
        packs[k][l, core, row] = packs[k][l, core, row] + got_as[k][l, row]

    def sum_row(b):
        l, k = BATCHES[b]
        total = packs[k][l, core, row].astype(f32)
        for d in range(1, n_row):
            copy_b(b, d).wait_recv()
            total += got_bs[k][l, d - 1].astype(f32)
        out_cs[k][l, 0 : batch_rows(n_row, k), :] = total.astype(bf16)
        for d in range(1, n_far):
            copy_c(b, d).start()

    def sum_far(b):
        l, k = BATCHES[b]
        total = part(out_cs[k], b, far)[...].astype(f32)
        for d in range(1, n_far):
            copy_c(b, d).wait_recv()
            total += got_cs[k][l, d - 1].astype(f32)
        part(finals[k].at[core], b, far)[...] = total.astype(bf16)
        for d in range(1, n_far):
            copy_d(b, d, far).start()
        copy_e(b, 0, core).start()

    def pass_on(b):
        for d in range(1, n_far):
            copy_d(b, d, place.far_at(n_far - d)).wait_recv()
            copy_e(b, d, core).start()

    def finish(b):
        copy_a(b).wait_send()
        for d in range(1, n_row):
            copy_b(b, d).wait_send()
        for d in range(1, n_far):
            copy_c(b, d).wait_send()
            copy_d(b, d, far).wait_send()
        for d in range(n_far):
            copy_e(b, d, core).wait_send()
            copy_e(b, d, 1 - core).wait_recv()

    stages = [sum_cores, sum_row, sum_far, pass_on]

    visits = {
        2: (0,),
        chunks + 1: (0, 1),
        2 * chunks - 1: (0,),
        2 * chunks: (1,),
        2 * chunks + 1: (0, 2, 3),
        2 * chunks + 2: (1,),
        3 * chunks: (2,),
        3 * chunks + 1: (1, 4),
        3 * chunks + 2: (2, 3),
    }
    reached = [0] * len(BATCHES)

    def advance(b):
        for stage in stages[reached[b] : reached[b] + 1]:
            stage(b)
        reached[b] += 1

    @pl.when(step == 0)
    def _():
        if swap:
            meet_all(place)
        else:
            meet(place.partners())
        start_rows(rows_in, rows_out, rows_sem)
        g_s[1] = up_ref[...].astype(f32)
        for k in range(3):
            valid, padded = batch_rows(n_row, k), out_cs[k].shape[1]
            if padded > valid:
                out_cs[k][:, valid:, :] = jnp.zeros((2, padded - valid, D), bf16)
        if 2 * low > size:
            spare = (2, n_row, 2 * low - size, D)
            packs[1][:, 1, :, 3 * size - low :, :] = jnp.zeros(spare, bf16)
            packs[2][:, 1, :, 2 * size - low : size + low, :] = jnp.zeros(spare, bf16)

    @pl.when(step == 2 * chunks)
    def _():
        edge_copy().wait_recv()
        assemble_back(g_s.at[1], edge_in, g_s.at[0])

    for at, due in visits.items():

        @pl.when(step == at)
        def _():
            for b in due:
                advance(b)

    @pl.when(step % (2 * chunks) == 0)
    def _():
        vec_g[...] = jnp.zeros_like(vec_g)
        fc1_bg[...] = jnp.zeros_like(fc1_bg)
        table_g[...] = jnp.zeros_like(table_g)
        gz_s[...] = g_s[layer].astype(bf16)
        vec_g[3:4, :] = column_sum(gz_s[...].astype(f32))
        count = D // (4 * size)
        for j in range(4):
            value = dot_tn(act_ref[0, :, D * j : D * (j + 1)], gz_s[...]).astype(bf16)
            for t in range(count):
                for half in range(2):
                    at = (2 * t + half) * 2 * size
                    packs[0][layer, half, j * count + t] = value[at : at + 2 * size, :]

    for b in (0, 3):

        @pl.when(step == 2 * chunks * (b // 3))
        def _():
            copy_a(b).start()

    @pl.when(kind == 0)
    def _():
        upstream = g_s[layer, here, :]
        du = (dot_nt(gz_s[here, :], fc2_w[0]) * slope_ref[0].astype(f32)).astype(bf16)
        du_s[here, :] = du
        fc1_bg[...] += column_sum(du.astype(f32))
        dn = dot_nt(du, fc1_w[0])
        normal, inverse = norm_parts(mid_ref[0])
        gain = vec_ref[layer, 5:6, :]
        h2_s[here, :] = (normal * gain + vec_ref[layer, 7:8, :]).astype(bf16)
        vec_g[5:6, :] += column_sum(dn * normal)
        vec_g[7:8, :] += column_sum(dn)
        mid_grad = upstream + norm_back(dn, normal, inverse, gain)
        g_s[layer, here, :] = mid_grad
        branch = mid_grad.astype(bf16)
        ga_s[here, :] = branch
        vec_g[2:3, :] += column_sum(branch.astype(f32))

    def put(k, half, at, value, first, count):
        for r in range(n_row):
            packs[k][layer, half, r, at : at + count, :] = value[
                size * r + first : size * r + first + count, :
            ]

    @pl.when(step % (2 * chunks) == chunks - 1)
    def _():
        for j in range(4):
            value = dot_tn(h2_s[...], du_s[:, D * j : D * (j + 1)]).astype(bf16)
            put(1, j // 2, size * (j % 2), value, 0, size)
        value = dot_tn(att_ref[0], ga_s[...]).astype(bf16)
        put(1, 0, 2 * size, value, 0, low)
        put(1, 1, 2 * size, value, low, size - low)

    for b in (1, 4):

        @pl.when(step == 2 * chunks * (b // 3) + chunks - 1)
        def _():
            copy_a(b).start()

    @pl.when(kind == 1)
    def _():
        att_grad = dot_nt(ga_s[here, :], proj_w[0]).astype(bf16)
        for k in range(CHUNK_WINS):
            rows = slice(CELL * k, CELL * (k + 1))
            there = pl.ds(pl.multiple_of(chunk * CHUNK + CELL * k, CELL), CELL)
            q_parts, k_parts, v_parts = [], [], []
            for g in range(2):
                q = qkv_ref[0, rows, 128 * g : 128 * g + 256]
                key = qkv_ref[0, rows, D + 128 * g : D + 128 * g + 256]
                val = qkv_ref[0, rows, 2 * D + 128 * g : 2 * D + 128 * g + 256]
                do = att_grad[rows, 128 * g : 128 * g + 256]
                q_wide = jnp.concatenate([q] * GROUP, axis=0) * wide_heads_ref[g]
                do_wide = jnp.concatenate([do] * GROUP, axis=0) * wide_heads_ref[g]
                lanes = slice(GROUP * CELL * g, GROUP * CELL * (g + 1))
                prob_low = prob_ref[0, rows, lanes]
                prob = prob_low.astype(f32)
                dp = dot_nt(val, do_wide)
                v_parts.append(dot_nn(prob_low, do_wide))
                weighted = prob * dp
                ds = (weighted - prob * column_sum(weighted)).astype(bf16)
                table_g[:, lanes] += ds.astype(f32)
                k_parts.append(dot_nn(ds, q_wide))
                q_parts.append(gather_heads(dot_tn(ds, key), heads_ref, g))
            dt_s[there, 0:D] = (join_groups(*q_parts) * SCALE).astype(bf16)
            dt_s[there, D : 2 * D] = (join_groups(*k_parts) * SCALE).astype(bf16)
            dt_s[there, 2 * D : 3 * D] = join_groups(*v_parts).astype(bf16)
        dt = dt_s[here, :]
        vec_g[0:1, :] += column_sum(dt[:, 0:D].astype(f32))
        vec_g[1:2, :] += column_sum(dt[:, 2 * D :].astype(f32))
        dn = dot_nt(dt, qkv_w[0])
        normal, inverse = norm_parts(x_ref[0])
        gain = vec_ref[layer, 4:5, :]
        h1_s[here, :] = (normal * gain + vec_ref[layer, 6:7, :]).astype(bf16)
        vec_g[4:5, :] += column_sum(dn * normal)
        vec_g[6:7, :] += column_sum(dn)
        g_s[layer, here, :] += norm_back(dn, normal, inverse, gain)

    @pl.when(step == chunks + chunks // 2 - 1)
    def _():
        for col in range(WIN_COLS):
            at = CELL * (last_row + col) + 2 * BLOCK
            edge_out[2 * BLOCK * col : 2 * BLOCK * (col + 1), :] = g_s[
                1, at : at + 2 * BLOCK, :
            ].astype(bf16)
        edge_copy().start()

    @pl.when(step == 4 * chunks - 1)
    def _():
        for b in (4, 3, 2):
            advance(b)

    @pl.when(step % (2 * chunks) == 2 * chunks - 1)
    def _():
        values = [dot_tn(h1_s[...], dt_s[:, D * j : D * (j + 1)]).astype(bf16) for j in range(3)]
        put(2, 0, 0, values[0], 0, size)
        put(2, 0, size, values[1], 0, low)
        put(2, 1, 0, values[2], 0, size)
        put(2, 1, size, values[1], low, size - low)
        table = table_rows(table_g[...], lanes_ref, back_ref)
        table = jnp.concatenate([table, jnp.zeros((HEADS, D - TABLE_PAD), f32)], axis=1)
        vectors = jnp.concatenate(
            [vec_g[...]]
            + [fc1_bg[:, D * j : D * (j + 1)] for j in range(4)]
            + [jnp.zeros((4, D), f32)],
            axis=0,
        )
        for r in range(n_row):
            packs[2][layer, 0, r, size + low :, :] = vectors.astype(bf16)
            packs[2][layer, 1, r, size + low :, :] = table.astype(bf16)

    @pl.when(step == 2 * chunks - 1)
    def _():
        copy_a(2).start()

    @pl.when(step == 4 * chunks - 1)
    def _():
        copy_a(5).start()
        unpick_rows(g_s[0].astype(bf16), grad_rows)
        start_rows(grad_rows, grad_out, grad_sem)
        while min(reached) < len(stages):
            for b in (5, 4, 3, 2, 1, 0):
                advance(b)
        for b in range(len(BATCHES)):
            finish(b)
        edge_copy().wait_send()
        copies = [
            pltpu.make_async_copy(finals[k], out, done_sem.at[k])
            for k, out in enumerate((final_0, final_1, final_2))
        ]
        for copy in copies:
            copy.start()
        for copy in copies:
            copy.wait()
        for source, target, sem in (
            (rows_in, rows_out, rows_sem),
            (grad_rows, grad_out, grad_sem),
        ):
            if swap:
                swap_wait(place, source, target, sem)
                swap_end(place, source, target, sem)
                swap_own(place, source, target, sem).wait()
            else:
                pltpu.make_async_copy(source, target, sem.at[0, 0]).wait()


def backward_layers(placing, upstream, y, saved, full, vec):
    n_row, n_far = lax.axis_size("row"), lax.axis_size("clip") // 2
    n = 2 * n_row * n_far
    tokens = upstream.shape[0]
    chunks = tokens // CHUNK
    swap = can_swap(tokens, n)
    heads, wide = head_masks()
    lanes, _, back = table_constants()
    ff = full[2].shape[2]
    size = row_share(n_row)
    anywhere = pl.BlockSpec(memory_space=pl.ANY)

    def at(i):
        return 1 - i // (2 * chunks), i // chunks % 2, (i + chunks // 2) % chunks

    def layer_block(i):
        return 1 - i // (2 * chunks), 0, 0

    def forward_block(i):
        layer, kind, chunk = at(i)
        return (1 - kind) * layer, (1 - kind) * chunk + kind * (chunks // 2 - 1 + layer), 0

    def attention_block(i):
        layer, kind, chunk = at(i)
        return layer, kind * chunk + (1 - kind) * (chunks // 2), 0

    def chunked(value, block):
        return pl.BlockSpec((1, CHUNK, value.shape[2]), block)

    def layered(value):
        return pl.BlockSpec((1, *value.shape[1:]), layer_block)

    x, qkv, prob, att, mid, act, slope = saved
    constants = (
        vec,
        jnp.asarray(heads),
        jnp.asarray(wide, dtype=bf16),
        jnp.asarray(lanes.reshape(2 * TABLE_PAD, 128), dtype=bf16),
        jnp.asarray(back, dtype=bf16),
    )
    valid = [batch_rows(n_row, k) for k in range(3)]
    piece = [piece_rows(n_row, n_far, k) for k in range(3)]
    final = [(2, 2, n_far * piece[k], D) for k in range(3)]
    dma = pltpu.SemaphoreType.DMA

    def each(shape_of):
        return [pltpu.VMEM(shape_of(k), bf16) for k in range(3)]

    return pl.pallas_call(
        functools.partial(backward_kernel, n_row, n_far, swap),
        grid=(4 * chunks,),
        in_specs=[
            whole((1, tokens)),
            whole((tokens, D)),
            whole((tokens, D)),
            chunked(x, attention_block),
            chunked(qkv, attention_block),
            chunked(prob, attention_block),
            layered(att),
            chunked(mid, forward_block),
            layered(act),
            chunked(slope, forward_block),
        ]
        + [layered(weight) for weight in full]
        + [whole(constant.shape) for constant in constants],
        out_specs=[anywhere] * 5,
        out_shape=[jax.ShapeDtypeStruct((tokens, D), bf16)] * 2
        + [jax.ShapeDtypeStruct(shape, bf16) for shape in final],
        scratch_shapes=[
            pltpu.VMEM((8, D), f32),
            pltpu.VMEM((1, ff), f32),
            pltpu.VMEM((CELL, HEADS * CELL), f32),
            pltpu.VMEM((2, tokens, D), f32),
            pltpu.VMEM((tokens, D), bf16),
            pltpu.VMEM((tokens, 3 * D), bf16),
            pltpu.VMEM((tokens, D), bf16),
            pltpu.VMEM((tokens, D), bf16),
            pltpu.VMEM((tokens, ff), bf16),
            *[pltpu.VMEM((tokens, D), bf16)] * 2,
            pltpu.VMEM((WIN_COLS * 2 * BLOCK, D), bf16),
            pltpu.VMEM((WIN_COLS * 2 * BLOCK, D), bf16),
            *each(lambda k: (2, 2, n_row, valid[k], D)),
            *each(lambda k: (2, n_row, valid[k], D)),
            *each(lambda k: (2, n_row - 1, valid[k], D)),
            *each(lambda k: (2, n_far * piece[k], D)),
            *each(lambda k: (2, n_far - 1, piece[k], D)),
            *each(lambda k: final[k]),
            dma((2, n if swap else 1)),
            dma((2, n if swap else 1)),
            dma((2,)),
            dma((2, len(BATCHES))),
            dma((2, len(BATCHES), n_row - 1)),
            dma((2, len(BATCHES), n_far - 1)),
            dma((2, len(BATCHES), n_far - 1)),
            dma((2, len(BATCHES), n_far)),
            dma((3,)),
        ],
        compiler_params=pltpu.CompilerParams(
            collective_id=1, has_side_effects=True, vmem_limit_bytes=VMEM_LIMIT
        ),
        name="backward_layers",
    )(placing.reshape(1, tokens), upstream, y, x, qkv, prob, att, mid, act, slope, *full, *constants)


def unpack_kernel(
    n_row, fc2_ref, fc1_ref, qkv_ref, qkv_o, qvb_o, proj_o, projb_o, fc1_o, fc1b_o, fc2_o, fc2b_o, gain_o, shift_o, table_o
):
    row = lax.axis_index("row")
    size = D // n_row
    lane = lax.broadcasted_iota(jnp.int32, (D, size), 0)
    want = lax.broadcasted_iota(jnp.int32, (D, size), 1)
    pick = jnp.where(lane == want + size * row, 1.0, 0.0).astype(bf16)
    start = 4 * size * row
    lane = lax.broadcasted_iota(jnp.int32, (D, 4 * size), 0)
    want = lax.broadcasted_iota(jnp.int32, (D, 4 * size), 1)
    pick_fc1 = jnp.where(lane == want + start % D, 1.0, 0.0).astype(bf16)
    spot = lax.broadcasted_iota(jnp.int32, (16, 4 * size), 0)
    a = lax.broadcasted_iota(jnp.int32, (HEADS, HEADS), 0)
    b = lax.broadcasted_iota(jnp.int32, (HEADS, HEADS), 1)
    same = jnp.where(a == b, 1.0, 0.0).astype(bf16)
    low = shard_half(size, 0)[1]
    for layer in range(2):
        for j in range(2):
            qkv_o[layer, :, 2 * D * j : 2 * D * j + D] = qkv_ref[j, layer, 0:size, :].astype(f32)
        qkv_o[layer, 0:low, D : 2 * D] = qkv_ref[0, layer, size : size + low, :].astype(f32)
        qkv_o[layer, low:size, D : 2 * D] = qkv_ref[1, layer, size : 2 * size - low, :].astype(f32)
        proj_o[layer, 0:low, :] = fc1_ref[0, layer, 2 * size : 2 * size + low, :].astype(f32)
        proj_o[layer, low:size, :] = fc1_ref[1, layer, 2 * size : 3 * size - low, :].astype(f32)
        for j in range(4):
            at = size * (j % 2)
            fc1_o[layer, :, D * j : D * (j + 1)] = fc1_ref[
                j // 2, layer, at : at + size, :
            ].astype(f32)
        for j in range(2):
            fc2_o[layer, 2 * size * j : 2 * size * (j + 1), :] = fc2_ref[
                j, layer, 0 : 2 * size, :
            ].astype(f32)
        vectors = qkv_ref[0, layer, size + low : size + low + 16, :]
        mine = dot_nn(vectors, pick)
        qvb_o[layer] = mine[0:2]
        projb_o[layer : layer + 1] = mine[2:3]
        fc2b_o[layer : layer + 1] = mine[3:4]
        gain_o[layer] = mine[4:6]
        shift_o[layer] = mine[6:8]
        mine = dot_nn(vectors, pick_fc1)
        fc1b_o[layer : layer + 1] = column_sum(jnp.where(spot == 8 + start // D, mine, 0.0))
        table = qkv_ref[1, layer, size + low : size + low + 16, 0:TABLE_PAD]
        table_o[layer] = dot_tn(table, same)[0:TABLE, :]


def unpack_gradients(*finals):
    n_row = lax.axis_size("row")
    size = D // n_row
    shapes = [
        (2, size, 3 * D),
        (2, 2, size),
        (2, size, D),
        (2, size),
        (2, size, 4 * D),
        (2, 4 * size),
        (2, 4 * size, D),
        (2, size),
        (2, 2, size),
        (2, 2, size),
        (2, TABLE, HEADS),
    ]
    return pl.pallas_call(
        functools.partial(unpack_kernel, n_row),
        out_shape=[jax.ShapeDtypeStruct(shape, f32) for shape in shapes],
        compiler_params=pltpu.CompilerParams(vmem_limit_bytes=VMEM_LIMIT),
        name="unpack_gradients",
    )(*finals)


def exchange(values):
    return lax.all_to_all(values, ("clip", "row"), split_axis=0, concat_axis=0, tiled=True)


def body(
    inputs,
    cotangent,
    source_of,
    split_row,
    qkv_weight,
    qv_bias,
    proj_weight,
    proj_bias,
    fc1_weight,
    fc1_bias,
    fc2_weight,
    fc2_bias,
    norm_gain,
    norm_bias,
    rel_table,
):
    clip_count = lax.axis_size("clip")
    row_count = lax.axis_size("row")
    tokens = inputs.shape[0]
    block_rows = tokens // (clip_count * row_count)
    grid_rows = tokens // GRID_COLS
    window_rows = grid_rows // WIN

    placing = source_of // tokens * block_rows + source_of % block_rows
    placing = placing.reshape(window_rows, 2, SHIFT, WIN_COLS, 2, SHIFT)
    placing = placing.transpose(0, 3, 1, 4, 2, 5).reshape(tokens)
    if not can_swap(tokens, clip_count * row_count):
        inputs, cotangent = exchange(inputs), exchange(cotangent)
    saved, upstream, layer_two, full, vec_rows = forward_layers(
        split_row,
        placing,
        inputs,
        cotangent,
        (qkv_weight, proj_weight, fc1_weight, fc2_weight),
        (qv_bias, proj_bias, fc1_bias, fc2_bias, norm_gain, norm_bias),
        rel_table,
    )
    output, input_grad, *finals = backward_layers(placing, upstream, layer_two, saved, full, vec_rows)
    if not can_swap(tokens, clip_count * row_count):
        output, input_grad = exchange(output), exchange(input_grad)
    input_grad = input_grad.astype(f32)
    totals = unpack_gradients(*finals)
    return (output, input_grad, *totals)


def solution(mesh):
    placed = (
        P(("clip", "row"), None),
        P(("clip", "row"), None),
        P(("clip", "row")),
        P("clip"),
        P(None, "row", None),
        P(None, None, "row"),
        P(None, "row", None),
        P(None, "row"),
        P(None, "row", None),
        P(None, "row"),
        P(None, "row", None),
        P(None, "row"),
        P(None, None, "row"),
        P(None, None, "row"),
        P(),
    )
    return jax.shard_map(
        body,
        mesh=mesh,
        in_specs=placed,
        out_specs=(
            P(("clip", "row"), None),
            P(("clip", "row"), None),
            P(None, "row", None),
            P(None, None, "row"),
            P(None, "row", None),
            P(None, "row"),
            P(None, "row", None),
            P(None, "row"),
            P(None, "row", None),
            P(None, "row"),
            P(None, None, "row"),
            P(None, None, "row"),
            P(),
        ),
        check_vma=False,
    )
```

```python
import functools

import jax
import jax.numpy as jnp
import numpy as np
from jax import lax
from jax.experimental import pallas as pl
from jax.experimental.pallas import tpu as pltpu
from jax.sharding import PartitionSpec as P

WIN = 8
SHIFT = 4
GRID_COLS = 64
EPSILON = 1e-05
MASKED = -1000000000.0
ROOT_HALF = 0.7071067811865476
INV_ROOT_TAU = 0.3989422804014327

HEADS = 16
HEAD_DIM = 24
D = HEADS * HEAD_DIM
GROUP = 8
CELL = WIN * WIN
BLOCK = SHIFT * SHIFT
WIN_COLS = GRID_COLS // WIN
SPREAD = 2 * WIN - 1
TABLE = SPREAD * SPREAD
TABLE_PAD = 256
SCALE = HEAD_DIM**-0.5
CHUNK = 256
CHUNK_WINS = CHUNK // CELL
VMEM_LIMIT = 56 * 1024 * 1024

MESH = pl.DeviceIdType.MESH
f32 = jnp.float32
bf16 = jnp.bfloat16


def window_places():
    spot = np.arange(CELL)
    row = (spot // 32) * SHIFT + (spot % BLOCK) // SHIFT
    col = (spot // BLOCK % 2) * SHIFT + spot % SHIFT
    return row, col


def head_masks():
    feature = np.arange(D) // HEAD_DIM
    rows = (feature[None, :] == np.arange(HEADS)[:, None]).astype(np.float32)
    wide = np.stack(
        [
            np.repeat(rows[GROUP * g : GROUP * (g + 1), 128 * g : 128 * g + 256], CELL, axis=0)
            for g in range(2)
        ]
    )
    return rows, wide


def table_constants():
    row, col = window_places()
    natural = row * WIN + col
    lanes = np.zeros((2, TABLE_PAD, 128), np.float32)
    for half in range(2):
        lanes[half, row * SPREAD + col, half * CELL + np.arange(CELL)] = 1.0
    order = np.zeros((CELL, CELL), np.float32)
    order[np.arange(CELL), natural] = 1.0
    back = np.zeros((CELL, CELL), np.float32)
    back[row * WIN + (WIN - 1 - col), np.arange(CELL)] = 1.0
    return lanes, order, back


def dot_nn(a, b):
    return lax.dot_general(a, b, (((1,), (0,)), ((), ())), preferred_element_type=f32)


def dot_nt(a, b):
    return lax.dot_general(a, b, (((1,), (1,)), ((), ())), preferred_element_type=f32)


def dot_tn(a, b):
    return lax.dot_general(a, b, (((0,), (0,)), ((), ())), preferred_element_type=f32)


def dot_exact(a, b, dims):
    return lax.dot_general(
        a, b, (dims, ((), ())), precision=lax.Precision.HIGHEST, preferred_element_type=f32
    )


def split(values):
    high = values.astype(bf16)
    rest = values - high.astype(f32)
    middle = rest.astype(bf16)
    return high, middle, (rest - middle.astype(f32)).astype(bf16)


def whole(shape):
    zeros = (0,) * len(shape)
    return pl.BlockSpec(shape, lambda i: zeros)


def rows_of(shape):
    return pl.BlockSpec(shape, lambda i: (i, 0))


def norm_parts(values):
    centred = values - jnp.mean(values, axis=-1, keepdims=True)
    inverse = lax.rsqrt(jnp.mean(centred * centred, axis=-1, keepdims=True) + EPSILON)
    return centred * inverse, inverse


def norm_back(upstream, normal, inverse, gain):
    scaled = upstream * gain
    centred = scaled - jnp.mean(scaled, axis=-1, keepdims=True)
    return inverse * (centred - normal * jnp.mean(scaled * normal, axis=-1, keepdims=True))


def column_sum(values):
    return jnp.sum(values, axis=0, keepdims=True)


def bias_rows(table_ref, lanes_ref, order_ref, out_ref, wide_ref):
    for layer in range(2):
        for head in range(HEADS):
            pair, half = divmod(head, 2)
            spread = jnp.broadcast_to(table_ref[layer, head : head + 1, :], (WIN, TABLE_PAD))
            for i in range(WIN):
                at = CELL * pair + WIN * i
                wide_ref[at : at + WIN, TABLE_PAD * half : TABLE_PAD * (half + 1)] = pltpu.roll(
                    spread, (SPREAD * i - 112) % TABLE_PAD, 1, stride=1, stride_axis=0
                )
        picked = sum(dot_nn(part, lanes_ref[...]) for part in reversed(split(wide_ref[...])))
        joined = jnp.concatenate(
            [picked[CELL * pair : CELL * (pair + 1), :] for pair in range(HEADS // 2)], axis=1
        )
        out_ref[layer] = sum(dot_nn(order_ref[...], part) for part in reversed(split(joined)))


def table_rows(grads, lanes_ref, back_ref):
    turned = sum(dot_nn(back_ref[...], part) for part in reversed(split(grads)))
    stacked = jnp.concatenate([turned[:, 128 * i : 128 * (i + 1)] for i in range(HEADS // 2)], axis=0)
    spread = sum(dot_nt(part, lanes_ref[...]) for part in reversed(split(stacked)))
    rows = []
    for head in range(HEADS):
        pair, half = divmod(head, 2)
        total = jnp.zeros((WIN, TABLE_PAD), f32)
        for i in range(WIN):
            at = CELL * pair + WIN * i
            total += pltpu.roll(
                spread[at : at + WIN, TABLE_PAD * half : TABLE_PAD * (half + 1)],
                (112 - SPREAD * i - (WIN - 1)) % TABLE_PAD,
                1,
                stride=1,
                stride_axis=0,
            )
        rows.append(column_sum(total))
    return jnp.concatenate(rows, axis=0)


def quarter(window, sub):
    return pl.ds(CELL * window + BLOCK * sub, BLOCK)


def assemble_back(main_ref, edge_ref, out_ref):
    windows = main_ref.shape[0] // CELL
    for window in range(windows):
        wr, wc = divmod(window, WIN_COLS)
        before = (wc - 1) % WIN_COLS
        out_ref[quarter(window, 3), :] = main_ref[quarter(window, 0), :].astype(out_ref.dtype)
        out_ref[quarter(window, 2), :] = main_ref[
            quarter(wr * WIN_COLS + before, 1), :
        ].astype(out_ref.dtype)
        for sub, col, piece in ((1, wc, 0), (0, before, 1)):
            if wr == 0:
                value = edge_ref[pl.ds(2 * BLOCK * col + BLOCK * piece, BLOCK), :]
            else:
                value = main_ref[quarter((wr - 1) * WIN_COLS + col, 2 + piece), :]
            out_ref[quarter(window, sub), :] = value.astype(out_ref.dtype)


def assemble_ahead(main_ref, edge_ref, out_ref, window_rows):
    last = main_ref.shape[0] // CELL // WIN_COLS - 1
    for wr in window_rows:
        for wc in range(WIN_COLS):
            window = wr * WIN_COLS + wc
            after = (wc + 1) % WIN_COLS
            out_ref[quarter(window, 0), :] = main_ref[quarter(window, 3), :].astype(out_ref.dtype)
            out_ref[quarter(window, 1), :] = main_ref[
                quarter(wr * WIN_COLS + after, 2), :
            ].astype(out_ref.dtype)
            for sub, col, piece in ((2, wc, 1), (3, after, 0)):
                if wr == last:
                    value = edge_ref[pl.ds(2 * BLOCK * col + BLOCK * piece, BLOCK), :]
                else:
                    value = main_ref[quarter((wr + 1) * WIN_COLS + col, piece), :]
                out_ref[quarter(window, sub), :] = value.astype(out_ref.dtype)


class Place:
    def __init__(self, n_row, n_far):
        clip = lax.axis_index("clip")
        self.n_row, self.n_far = n_row, n_far
        self.core, self.far, self.row = clip % 2, clip // 2, lax.axis_index("row")
        self.n = 2 * n_far * n_row
        self.index = clip * n_row + self.row

    def index_at(self, d):
        return (self.index + d) % self.n

    def device(self, d):
        at = self.index_at(d)
        return (at // self.n_row, at % self.n_row)

    def row_at(self, d):
        return (self.row + d) % self.n_row

    def far_at(self, d):
        return (self.far + d) % self.n_far

    def twin(self):
        return (2 * self.far + 1 - self.core, self.row)

    def at_row(self, row):
        return (2 * self.far + self.core, row)

    def in_row(self, d):
        return self.at_row(self.row_at(d))

    def at_far(self, far):
        return (2 * far + self.core, self.row)

    def along(self, d):
        return self.at_far(self.far_at(d))

    def partners(self, far=True):
        found = [self.twin()] + [self.in_row(d) for d in range(1, self.n_row)]
        return found + ([self.along(d) for d in range(1, self.n_far)] if far else [])


def meet(partners):
    barrier = pltpu.get_barrier_semaphore()
    for partner in partners:
        pl.semaphore_signal(barrier, inc=1, device_id=partner, device_id_type=MESH)
    pl.semaphore_wait(barrier, len(partners))


def send(src, dst, send_sem, recv_sem, target):
    copy = pltpu.make_async_remote_copy(
        src_ref=src,
        dst_ref=dst,
        send_sem=send_sem,
        recv_sem=recv_sem,
        device_id=target,
        device_id_type=MESH,
    )
    copy.start()
    return copy


def remote(src, dst, send_sem, recv_sem, target):
    return pltpu.make_async_remote_copy(
        src_ref=src,
        dst_ref=dst,
        send_sem=send_sem,
        recv_sem=recv_sem,
        device_id=target,
        device_id_type=MESH,
    )


def can_swap(tokens, n):
    return tokens // n % 16 == 0


def meet_all(place):
    barrier = pltpu.get_barrier_semaphore()

    def greet(d, carry):
        pl.semaphore_signal(barrier, inc=1, device_id=place.device(d), device_id_type=MESH)
        return carry

    lax.fori_loop(1, place.n, greet, 0)
    pl.semaphore_wait(barrier, place.n - 1)


def swap_block(place, ref, index):
    count = ref.shape[0] // place.n
    return ref.at[pl.ds(pl.multiple_of(index * count, 16), count), :]


def swap_own(place, src, dst, sem):
    return pltpu.make_async_copy(
        swap_block(place, src, place.index), swap_block(place, dst, place.index), sem.at[0, 0]
    )


def swap_copy(place, src, dst, sem, d, owner):
    return remote(
        swap_block(place, src, place.index_at(d)),
        swap_block(place, dst, owner),
        sem.at[0, d],
        sem.at[1, d],
        place.device(d),
    )


def swap_start(place, src, dst, sem):
    def work(d, carry):
        swap_copy(place, src, dst, sem, d, place.index).start()
        return carry

    lax.fori_loop(1, place.n, work, 0)


def swap_wait(place, src, dst, sem):
    def work(d, carry):
        swap_copy(place, src, dst, sem, d, place.index_at(place.n - d)).wait_recv()
        return carry

    lax.fori_loop(1, place.n, work, 0)


def swap_end(place, src, dst, sem):
    def work(d, carry):
        swap_copy(place, src, dst, sem, d, place.index).wait_send()
        return carry

    lax.fori_loop(1, place.n, work, 0)


def row_share(n_row):
    return D // n_row


HEIGHTS = (1, 1, 1, 4)
KINDS = ((0, 1), (2, 3))


def shard_half(height, core):
    low = -(-height // 32) * 16
    return (0, low) if core == 0 else (low, height - low)


def forward_kernel(
    n_row,
    n_far,
    swap,
    split_ref,
    place_col,
    place_row,
    x_in,
    c_in,
    qkv_i,
    proj_i,
    fc1_i,
    fc2_i,
    qv_bias,
    proj_bias,
    fc1_bias,
    fc2_bias,
    gain_ref,
    shift_ref,
    table_ref,
    lanes_ref,
    order_ref,
    heads_ref,
    wide_heads_ref,
    x_out,
    qkv_out,
    prob_out,
    att_out,
    mid_out,
    act_out,
    slope_out,
    up_out,
    y_out,
    qkv_wo,
    proj_wo,
    fc1_wo,
    fc2_wo,
    vec_out,
    x_got,
    c_got,
    qkv_s,
    proj_s,
    fc1_s,
    fc2_s,
    vec_wide,
    vec_mine,
    vec_got,
    qkv_b,
    fc1_b,
    table_s,
    bias_s,
    wide_s,
    x_s,
    y_s,
    c_s,
    order_s,
    edge_out,
    edge_in,
    x_sem,
    c_sem,
    own_sem,
    row_sem,
    twin_sem,
    vec_sem,
    edge_sem,
    out_sem,
):
    step = pl.program_id(0)
    tokens = x_s.shape[0]
    chunks = tokens // CHUNK
    layer = step // (2 * chunks)
    kind = step // chunks % 2
    chunk = (step + layer * kind * (chunks // 2)) % chunks
    place = Place(n_row, n_far)
    size = row_share(n_row)
    shards = (qkv_i, proj_i, fc1_i, fc2_i)
    kept = (qkv_s, proj_s, fc1_s, fc2_s)
    outs = (qkv_wo, proj_wo, fc1_wo, fc2_wo)
    window_rows = tokens // CELL // WIN_COLS
    last_row = (window_rows - 1) * WIN_COLS
    square = n_row == 4
    direct = range(2 if square else n_row - 1)
    slots = range(n_row - 1)
    if not swap:
        x_got, c_got = x_in, c_in

    def own(l, w):
        return pltpu.make_async_copy(
            shards[w].at[l], spot(l, w, place.row, 0, HEIGHTS[w] * size), own_sem.at[l, w]
        )

    def spot(l, w, owner, first, count):
        at = pl.multiple_of(owner * HEIGHTS[w] * size + first, 16)
        return kept[w].at[l, pl.ds(at, count), :]

    def neighbour(slot):
        row = place.row
        return (row + 1 - 2 * (row % 2), (row + 2) % 4, 3 - row)[slot]

    def source(slot):
        return neighbour(slot) if square else place.row_at(n_row - 1 - slot)

    def target(slot):
        return place.at_row(neighbour(slot) if square else place.row_at(slot + 1))

    def push(l, core, w, slot, owner=None):
        first, count = shard_half(HEIGHTS[w] * size, core)
        return remote(
            shards[w].at[l, pl.ds(first, count), :],
            spot(l, w, place.row if owner is None else owner, first, count),
            row_sem.at[0, l, w, slot],
            row_sem.at[1, l, w, slot],
            target(slot),
        )

    def relay(l, core, w):
        axis = (w + core) % 2
        here = spot(l, w, source(axis), *shard_half(HEIGHTS[w] * size, core))
        return remote(
            here, here, row_sem.at[0, l, w, 2], row_sem.at[1, l, w, 2], target(1 - axis)
        )

    def hand(l, core, w, slot):
        here = spot(l, w, source(slot), *shard_half(HEIGHTS[w] * size, core))
        return remote(
            here, here, twin_sem.at[0, l, w, slot], twin_sem.at[1, l, w, slot], place.twin()
        )

    def by_core(work):
        for core in range(2):
            pl.when(place.core == core)(functools.partial(work, core))

    def start_weights(l, k):
        def work(core):
            for w in KINDS[k]:
                for slot in direct:
                    push(l, core, w, slot).start()

        by_core(work)

    def pass_weights(l, k):
        def work(core):
            for w in KINDS[k]:
                for slot in direct:
                    push(l, core, w, slot, source(slot)).wait_recv()
                    if square and slot == (w + core) % 2:
                        relay(l, core, w).start()
                    hand(l, core, w, slot).start()

        by_core(work)

    def pass_relayed(l, k):
        def work(core):
            for w in KINDS[k]:
                push(l, core, w, 2, source(2)).wait_recv()
                hand(l, core, w, 2).start()

        if square:
            by_core(work)

    def wait_weights(l, k):
        def work(core):
            for w in KINDS[k]:
                for slot in slots:
                    hand(l, 1 - core, w, slot).wait_recv()

        by_core(work)
        for w in KINDS[k]:
            own(l, w).wait()

    def end_weights():
        def work(core):
            for l in range(2):
                for w in range(4):
                    for slot in direct:
                        push(l, core, w, slot).wait_send()
                    if square:
                        relay(l, core, w).wait_send()
                    for slot in slots:
                        hand(l, core, w, slot).wait_send()

        by_core(work)

    def vector_copy(d):
        return remote(
            vec_mine,
            vec_got.at[place.row],
            vec_sem.at[0, d - 1],
            vec_sem.at[1, d - 1],
            place.in_row(d),
        )

    def edge_copy(which):
        return remote(
            edge_out.at[which],
            edge_in.at[which],
            edge_sem.at[0, which],
            edge_sem.at[1, which],
            place.in_row(1 if which == 2 else n_row - 1),
        )

    def pack_edge(which, values, first_window, first_sub):
        for col in range(WIN_COLS):
            at = CELL * (first_window + col) + BLOCK * first_sub
            edge_out[which, 2 * BLOCK * col : 2 * BLOCK * (col + 1), :] = values[
                at : at + 2 * BLOCK, :
            ].astype(bf16)

    def pick_rows(values, out):
        for c in range(chunks):
            rows = slice(CHUNK * c, CHUNK * (c + 1))
            spots = lax.broadcasted_iota(jnp.int32, (CHUNK, tokens), 1)
            pick = jnp.where(spots == place_col[rows, :], 1.0, 0.0).astype(bf16)
            out[rows, :] = dot_nn(pick, values[...]).astype(out.dtype)

    @pl.when(step == 0)
    def _():
        for l in range(2):
            for w in range(4):
                own(l, w).start()
        if swap:
            swap_own(place, x_in, x_got, x_sem).start()
            swap_own(place, c_in, c_got, c_sem).start()
            meet_all(place)
            swap_start(place, x_in, x_got, x_sem)
        else:
            meet(place.partners(far=False))
        start_weights(0, 0)
        vec_wide[...] = jnp.zeros_like(vec_wide)
        for l in range(2):
            parts = (
                qv_bias[l],
                proj_bias[l : l + 1],
                fc2_bias[l : l + 1],
                gain_ref[l],
                shift_ref[l],
            )
            vec_wide[16 * l : 16 * l + 8, 0:size] = jnp.concatenate(
                [part.astype(f32) for part in parts], axis=0
            )
            vec_wide[16 * l + 8 : 16 * l + 9, 0 : 4 * size] = fc1_bias[l : l + 1].astype(f32)
        vec_mine[...] = vec_wide[...].astype(bf16)
        for d in range(1, n_row):
            vector_copy(d).start()
        mine = pltpu.make_async_copy(vec_mine, vec_got.at[place.row], out_sem.at[4])
        mine.start()
        table_s[...] = jnp.zeros_like(table_s)
        table_s[:, :, 0:TABLE] = table_ref[...]
        bias_rows(table_s, lanes_ref, order_ref, bias_s, wide_s)
        mine.wait()
        for d in range(1, n_row):
            vector_copy(d).wait()
        for l in range(2):
            shares = [vec_got[r, 16 * l : 16 * (l + 1), :].astype(f32) for r in range(n_row)]
            rows = jnp.concatenate([share[0:8, 0:size] for share in shares], axis=1)
            vec_out[l] = rows
            qkv_b[l, 0:1, 0:D] = rows[0:1]
            qkv_b[l, 0:1, D : 2 * D] = jnp.zeros((1, D), f32)
            qkv_b[l, 0:1, 2 * D : 3 * D] = rows[1:2]
            fc1_b[l, 0:1, :] = jnp.concatenate(
                [share[8:9, 0 : 4 * size] for share in shares], axis=1
            )
        pass_weights(0, 0)
        start_weights(0, 1)
        if swap:
            swap_wait(place, x_in, x_got, x_sem)
            swap_own(place, x_in, x_got, x_sem).wait()
        pick_rows(x_got, x_s)
        pass_relayed(0, 0)
        wait_weights(0, 0)
        start_weights(1, 0)

    @pl.when(step == 1)
    def _():
        pass_weights(0, 1)
        start_weights(1, 1)

    @pl.when(step == chunks - 1)
    def _():
        pass_relayed(0, 1)

    @pl.when(step == chunks)
    def _():
        wait_weights(0, 1)
        pass_weights(1, 0)

    @pl.when(step == chunks + 2)
    def _():
        pass_relayed(1, 0)

    @pl.when(step == 2 * chunks - 1)
    def _():
        pass_weights(1, 1)

    @pl.when(step == 2 * chunks)
    def _():
        wait_weights(1, 0)
        assemble_ahead(y_s, edge_in.at[0], x_s, range(window_rows - 1))

    @pl.when(step == 2 * chunks + chunks // 2)
    def _():
        pass_relayed(1, 1)
        edge_copy(0).wait_recv()
        assemble_ahead(y_s, edge_in.at[0], x_s, range(window_rows - 1, window_rows))

    @pl.when(step == 3 * chunks)
    def _():
        wait_weights(1, 1)
        for w in range(4):
            pltpu.make_async_copy(kept[w], outs[w], out_sem.at[w]).start()

    @pl.when(step == 2 * chunks - 1)
    def _():
        if swap:
            swap_start(place, c_in, c_got, c_sem)

    @pl.when(step == 4 * chunks - 2)
    def _():
        if swap:
            swap_wait(place, c_in, c_got, c_sem)
            swap_own(place, c_in, c_got, c_sem).wait()
        pick_rows(c_got, c_s)
        pack_edge(1, c_s, 0, 0)
        edge_copy(1).start()

    here = pl.ds(pl.multiple_of(chunk * CHUNK, CHUNK), CHUNK)

    @pl.when(kind == 0)
    def _():
        x = x_s[here, :]
        x_out[0] = x
        normal, _ = norm_parts(x)
        hidden = (normal * vec_out[layer, 4:5, :] + vec_out[layer, 6:7, :]).astype(bf16)
        qkv_out[0] = (dot_nn(hidden, qkv_s[layer]) + qkv_b[layer]).astype(bf16)
        wide = (CELL, GROUP * CELL)
        apart = lax.broadcasted_iota(jnp.int32, wide, 0) ^ lax.broadcasted_iota(jnp.int32, wide, 1)
        for first in range(0, CHUNK_WINS, 4):
            spots = [(k, g) for k in range(first, first + 4) for g in range(2)]
            scores, probs, mixed = {}, {}, {}
            for k, g in spots:
                rows = slice(CELL * k, CELL * (k + 1))
                key = qkv_out[0, rows, D + 128 * g : D + 128 * g + 256]
                scores[k, g] = dot_nt(key, widen_heads(qkv_out[0, rows, 128 * g : 128 * g + 256], wide_heads_ref, g))
            for k, g in spots:
                window = chunk * CHUNK_WINS + k
                middle = (place.row * window_rows + window // WIN_COLS + 1) * WIN
                row_cut = (middle == split_ref[0]) | (middle == n_row * window_rows * WIN)
                col_cut = window % WIN_COLS == WIN_COLS - 1
                cut = layer * (jnp.where(row_cut, 32, 0) + jnp.where(col_cut, 16, 0))
                lanes = slice(GROUP * CELL * g, GROUP * CELL * (g + 1))
                score = scores[k, g] * SCALE + bias_s[layer, :, lanes]
                score = jnp.where((apart & cut) == 0, score, MASKED)
                e = jnp.exp(score - jnp.max(score, axis=0, keepdims=True))
                prob = (e * (1.0 / jnp.sum(e, axis=0, keepdims=True))).astype(bf16)
                prob_out[0, CELL * k : CELL * (k + 1), lanes] = prob
                probs[k, g] = prob
            for k, g in spots:
                val = qkv_out[0, CELL * k : CELL * (k + 1), 2 * D + 128 * g : 2 * D + 128 * g + 256]
                mixed[k, g] = gather_heads(dot_tn(probs[k, g], val), heads_ref, g)
            for k in range(first, first + 4):
                att_out[0, CELL * k : CELL * (k + 1), :] = join_groups(
                    mixed[k, 0], mixed[k, 1]
                ).astype(bf16)
        mid = x + (dot_nn(att_out[0], proj_s[layer]) + vec_out[layer, 2:3, :])
        x_s[here, :] = mid
        mid_out[0] = mid

    @pl.when(kind == 1)
    def _():
        mid = x_s[here, :]
        normal, _ = norm_parts(mid)
        hidden = (normal * vec_out[layer, 5:6, :] + vec_out[layer, 7:8, :]).astype(bf16)
        u = dot_nn(hidden, fc1_s[layer]) + fc1_b[layer]
        cdf = 0.5 * (1.0 + lax.erf(u * ROOT_HALF))
        act_out[0] = (u * cdf).astype(bf16)
        slope_out[0] = (cdf + u * (jnp.exp(-0.5 * u * u) * INV_ROOT_TAU)).astype(bf16)
        y_s[here, :] = mid + (dot_nn(act_out[0], fc2_s[layer]) + vec_out[layer, 3:4, :])

    @pl.when(step == chunks + chunks // 2 - 1)
    def _():
        pack_edge(0, y_s, 0, 0)
        edge_copy(0).start()

    @pl.when(step == 3 * chunks + chunks // 2 - 1)
    def _():
        pack_edge(2, y_s, last_row, 2)
        edge_copy(2).start()

    @pl.when(step == 4 * chunks - 1)
    def _():
        edge_copy(2).wait_recv()
        assemble_back(y_s, edge_in.at[2], order_s)
        for c in range(chunks):
            rows = slice(CHUNK * c, CHUNK * (c + 1))
            spots = lax.broadcasted_iota(jnp.int32, (CHUNK, tokens), 0) + CHUNK * c
            pick = jnp.where(spots == place_row[...], 1.0, 0.0).astype(bf16)
            y_out[rows, :] = dot_nn(pick, order_s[...]).astype(bf16)
        edge_copy(1).wait_recv()
        assemble_ahead(c_s, edge_in.at[1], up_out, range(window_rows))
        end_weights()
        for which in range(3):
            edge_copy(which).wait_send()
        for w in range(4):
            pltpu.make_async_copy(kept[w], outs[w], out_sem.at[w]).wait()
        if swap:
            swap_end(place, x_in, x_got, x_sem)
            swap_end(place, c_in, c_got, c_sem)


def gather_heads(spread, heads_ref, g):
    tiles = []
    for tile in range(2):
        lanes = slice(128 * tile, 128 * (tile + 1))
        first = 128 * (g + tile)
        total = None
        for h in range(GROUP):
            head = GROUP * g + h
            if HEAD_DIM * head >= first + 128 or HEAD_DIM * (head + 1) <= first:
                continue
            part = (
                spread[CELL * h : CELL * (h + 1), lanes]
                * heads_ref[head : head + 1, first : first + 128]
            )
            total = part if total is None else total + part
        tiles.append(total)
    return jnp.concatenate(tiles, axis=1)


def widen_heads(values, wide_heads_ref, g):
    rows = []
    for h in range(GROUP):
        head = GROUP * g + h
        tiles = []
        for tile in range(2):
            first = 128 * (g + tile)
            if HEAD_DIM * head >= first + 128 or HEAD_DIM * (head + 1) <= first:
                tiles.append(jnp.zeros((CELL, 128), bf16))
            else:
                lanes = slice(128 * tile, 128 * (tile + 1))
                tiles.append(
                    values[:, lanes] * wide_heads_ref[g, CELL * h : CELL * (h + 1), lanes]
                )
        rows.append(jnp.concatenate(tiles, axis=1))
    return jnp.concatenate(rows, axis=0)


def join_groups(low, high):
    return jnp.concatenate([low[:, :128], low[:, 128:] + high[:, :128], high[:, 128:]], axis=1)


def forward_layers(split_row, placing, x_in, c_in, shards, vectors, rel_table):
    n_row, n_far = lax.axis_size("row"), lax.axis_size("clip") // 2
    n = 2 * n_row * n_far
    tokens = x_in.shape[0]
    chunks = tokens // CHUNK
    swap = can_swap(tokens, n)
    heads, wide = head_masks()
    lanes, order, _ = table_constants()
    ff = shards[2].shape[2]
    anywhere = pl.BlockSpec(memory_space=pl.ANY)
    patches = anywhere if swap else whole((tokens, D))
    small = (
        *vectors,
        rel_table.transpose(0, 2, 1),
        jnp.asarray(lanes.reshape(2 * TABLE_PAD, 128), dtype=bf16),
        jnp.asarray(order, dtype=bf16),
        jnp.asarray(heads),
        jnp.asarray(wide, dtype=bf16),
    )
    full = [(2, shard.shape[1] * n_row, shard.shape[2]) for shard in shards]

    def attention_block(i):
        kind = i // chunks % 2
        return i // (2 * chunks), (1 - kind) * (i % chunks) + kind * (chunks - 1), 0

    def forward_block(i):
        layer, kind = i // (2 * chunks), i // chunks % 2
        half = layer * (chunks // 2)
        return layer, kind * ((i + half) % chunks) + (1 - kind) * half, 0

    saved = [
        (D, f32, attention_block),
        (3 * D, bf16, attention_block),
        (HEADS * CELL, bf16, attention_block),
        (D, bf16, attention_block),
        (D, f32, attention_block),
        (ff, bf16, forward_block),
        (ff, bf16, forward_block),
    ]
    dma = pltpu.SemaphoreType.DMA
    results = pl.pallas_call(
        functools.partial(forward_kernel, n_row, n_far, swap),
        grid=(4 * chunks,),
        in_specs=[
            pl.BlockSpec(memory_space=pltpu.SMEM),
            whole((tokens, 1)),
            whole((1, tokens)),
            patches,
            patches,
        ]
        + [anywhere] * 4
        + [whole(value.shape) for value in small],
        out_specs=[pl.BlockSpec((1, CHUNK, width), block) for width, _, block in saved]
        + [whole((tokens, D))] * 2
        + [anywhere] * 4
        + [whole((2, 8, D))],
        out_shape=[jax.ShapeDtypeStruct((2, tokens, width), kind) for width, kind, _ in saved]
        + [jax.ShapeDtypeStruct((tokens, D), bf16)] * 2
        + [jax.ShapeDtypeStruct(shape, bf16) for shape in full]
        + [jax.ShapeDtypeStruct((2, 8, D), f32)],
        scratch_shapes=[
            pltpu.VMEM((tokens if swap else 16, D), bf16),
            pltpu.VMEM((tokens if swap else 16, D), bf16),
            *[pltpu.VMEM(shape, bf16) for shape in full],
            pltpu.VMEM((32, D), f32),
            pltpu.VMEM((32, D), bf16),
            pltpu.VMEM((n_row, 32, D), bf16),
            pltpu.VMEM((2, 1, 3 * D), f32),
            pltpu.VMEM((2, 1, ff), f32),
            pltpu.VMEM((2, HEADS, TABLE_PAD), f32),
            pltpu.VMEM((2, CELL, HEADS * CELL), f32),
            pltpu.VMEM((HEADS // 2 * CELL, 2 * TABLE_PAD), f32),
            pltpu.VMEM((tokens, D), f32),
            pltpu.VMEM((tokens, D), f32),
            pltpu.VMEM((tokens, D), bf16),
            pltpu.VMEM((tokens, D), bf16),
            pltpu.VMEM((3, WIN_COLS * 2 * BLOCK, D), bf16),
            pltpu.VMEM((3, WIN_COLS * 2 * BLOCK, D), bf16),
            dma((2, n if swap else 1)),
            dma((2, n if swap else 1)),
            dma((2, 4)),
            dma((2, 2, 4, n_row - 1)),
            dma((2, 2, 4, n_row - 1)),
            dma((2, n_row - 1)),
            dma((2, 3)),
            dma((5,)),
        ],
        compiler_params=pltpu.CompilerParams(
            collective_id=0, has_side_effects=True, vmem_limit_bytes=VMEM_LIMIT
        ),
        name="forward_layers",
    )(
        split_row,
        placing.reshape(tokens, 1),
        placing.reshape(1, tokens),
        x_in,
        c_in,
        *shards,
        *small,
    )
    return results[:7], results[7], results[8], results[9:13], results[13]


BATCHES = ((1, 0), (1, 1), (1, 2), (0, 0), (0, 1), (0, 2))


def batch_rows(n_row, kind):
    size = row_share(n_row)
    low = shard_half(size, 0)[1]
    return (2 * size, 2 * size + low, size + low + 16)[kind]


def piece_rows(n_row, n_far, kind):
    return -(-batch_rows(n_row, kind) // (16 * n_far)) * 16


def backward_kernel(
    n_row,
    n_far,
    swap,
    place_row,
    up_ref,
    rows_in,
    x_ref,
    qkv_ref,
    prob_ref,
    att_ref,
    mid_ref,
    act_ref,
    slope_ref,
    qkv_w,
    proj_w,
    fc1_w,
    fc2_w,
    vec_ref,
    heads_ref,
    wide_heads_ref,
    lanes_ref,
    back_ref,
    rows_out,
    grad_out,
    final_0,
    final_1,
    final_2,
    vec_g,
    fc1_bg,
    table_g,
    g_s,
    h1_s,
    dt_s,
    ga_s,
    h2_s,
    du_s,
    gz_s,
    grad_rows,
    edge_out,
    edge_in,
    *refs,
):
    packs, got_as, got_bs, out_cs, got_cs, finals = (refs[3 * i : 3 * i + 3] for i in range(6))
    rows_sem, grad_sem, edge_sem, a_sem, b_sem, c_sem, d_sem, e_sem, done_sem = refs[18:]
    step = pl.program_id(0)
    tokens = g_s.shape[1]
    chunks = tokens // CHUNK
    layer = 1 - step // (2 * chunks)
    kind = step // chunks % 2
    chunk = (step + chunks // 2) % chunks
    place = Place(n_row, n_far)
    core, row, far = place.core, place.row, place.far
    size = row_share(n_row)
    low = shard_half(size, 0)[1]
    last_row = (tokens // CELL // WIN_COLS - 1) * WIN_COLS
    here = pl.ds(pl.multiple_of(chunk * CHUNK, CHUNK), CHUNK)

    def edge_copy():
        return remote(edge_out, edge_in, edge_sem.at[0], edge_sem.at[1], place.in_row(1))

    def start_rows(source, target, sem):
        if swap:
            swap_own(place, source, target, sem).start()
            swap_start(place, source, target, sem)
        else:
            pltpu.make_async_copy(source, target, sem.at[0, 0]).start()

    def unpick_rows(values, out):
        for c in range(chunks):
            rows = slice(CHUNK * c, CHUNK * (c + 1))
            spots = lax.broadcasted_iota(jnp.int32, (CHUNK, tokens), 0) + CHUNK * c
            pick = jnp.where(spots == place_row[...], 1.0, 0.0).astype(bf16)
            out[rows, :] = dot_nn(pick, values).astype(bf16)

    def part(ref, b, at):
        rows = got_cs[BATCHES[b][1]].shape[2]
        return ref.at[BATCHES[b][0], pl.ds(pl.multiple_of(at * rows, 16), rows), :]

    def copy_a(b):
        l, k = BATCHES[b]
        return remote(
            packs[k].at[l, 1 - core], got_as[k].at[l], a_sem.at[0, b], a_sem.at[1, b], place.twin()
        )

    def copy_b(b, d):
        l, k = BATCHES[b]
        return remote(
            packs[k].at[l, core, place.row_at(d)],
            got_bs[k].at[l, d - 1],
            b_sem.at[0, b, d - 1],
            b_sem.at[1, b, d - 1],
            place.in_row(d),
        )

    def copy_c(b, d):
        l, k = BATCHES[b]
        return remote(
            part(out_cs[k], b, place.far_at(d)),
            got_cs[k].at[l, d - 1],
            c_sem.at[0, b, d - 1],
            c_sem.at[1, b, d - 1],
            place.along(d),
        )

    def copy_d(b, d, owner):
        spot = part(finals[BATCHES[b][1]].at[core], b, owner)
        return remote(spot, spot, d_sem.at[0, b, d - 1], d_sem.at[1, b, d - 1], place.along(d))

    def copy_e(b, d, half):
        spot = part(finals[BATCHES[b][1]].at[half], b, place.far_at((n_far - d) % n_far))
        return remote(spot, spot, e_sem.at[0, b, d], e_sem.at[1, b, d], place.twin())

    def sum_cores(b):
        l, k = BATCHES[b]
        copy_a(b).wait_recv()
        for d in range(1, n_row):
            r = place.row_at(d)
            packs[k][l, core, r] = packs[k][l, core, r] + got_as[k][l, r]
            copy_b(b, d).start()
        packs[k][l, core, row] = packs[k][l, core, row] + got_as[k][l, row]

    def sum_row(b):
        l, k = BATCHES[b]
        total = packs[k][l, core, row].astype(f32)
        for d in range(1, n_row):
            copy_b(b, d).wait_recv()
            total += got_bs[k][l, d - 1].astype(f32)
        out_cs[k][l, 0 : batch_rows(n_row, k), :] = total.astype(bf16)
        for d in range(1, n_far):
            copy_c(b, d).start()

    def sum_far(b):
        l, k = BATCHES[b]
        total = part(out_cs[k], b, far)[...].astype(f32)
        for d in range(1, n_far):
            copy_c(b, d).wait_recv()
            total += got_cs[k][l, d - 1].astype(f32)
        part(finals[k].at[core], b, far)[...] = total.astype(bf16)
        for d in range(1, n_far):
            copy_d(b, d, far).start()
        copy_e(b, 0, core).start()

    def pass_on(b):
        for d in range(1, n_far):
            copy_d(b, d, place.far_at(n_far - d)).wait_recv()
            copy_e(b, d, core).start()

    def finish(b):
        copy_a(b).wait_send()
        for d in range(1, n_row):
            copy_b(b, d).wait_send()
        for d in range(1, n_far):
            copy_c(b, d).wait_send()
            copy_d(b, d, far).wait_send()
        for d in range(n_far):
            copy_e(b, d, core).wait_send()
            copy_e(b, d, 1 - core).wait_recv()

    stages = [sum_cores, sum_row, sum_far, pass_on]

    visits = {
        2: (0,),
        chunks + 1: (0, 1),
        2 * chunks - 1: (0,),
        2 * chunks: (1,),
        2 * chunks + 1: (0, 2, 3),
        2 * chunks + 2: (1,),
        3 * chunks: (2,),
        3 * chunks + 1: (1, 4),
        3 * chunks + 2: (2, 3),
    }
    reached = [0] * len(BATCHES)

    def advance(b):
        for stage in stages[reached[b] : reached[b] + 1]:
            stage(b)
        reached[b] += 1

    @pl.when(step == 0)
    def _():
        if swap:
            meet_all(place)
        else:
            meet(place.partners())
        start_rows(rows_in, rows_out, rows_sem)
        g_s[1] = up_ref[...].astype(f32)
        for k in range(3):
            valid, padded = batch_rows(n_row, k), out_cs[k].shape[1]
            if padded > valid:
                out_cs[k][:, valid:, :] = jnp.zeros((2, padded - valid, D), bf16)
        if 2 * low > size:
            spare = (2, n_row, 2 * low - size, D)
            packs[1][:, 1, :, 3 * size - low :, :] = jnp.zeros(spare, bf16)
            packs[2][:, 1, :, 2 * size - low : size + low, :] = jnp.zeros(spare, bf16)

    @pl.when(step == 2 * chunks)
    def _():
        edge_copy().wait_recv()
        assemble_back(g_s.at[1], edge_in, g_s.at[0])

    for at, due in visits.items():

        @pl.when(step == at)
        def _():
            for b in due:
                advance(b)

    @pl.when(step % (2 * chunks) == 0)
    def _():
        vec_g[...] = jnp.zeros_like(vec_g)
        fc1_bg[...] = jnp.zeros_like(fc1_bg)
        table_g[...] = jnp.zeros_like(table_g)
        gz_s[...] = g_s[layer].astype(bf16)
        vec_g[3:4, :] = column_sum(gz_s[...].astype(f32))
        count = D // (4 * size)
        for j in range(4):
            value = dot_tn(act_ref[0, :, D * j : D * (j + 1)], gz_s[...]).astype(bf16)
            for t in range(count):
                for half in range(2):
                    at = (2 * t + half) * 2 * size
                    packs[0][layer, half, j * count + t] = value[at : at + 2 * size, :]

    for b in (0, 3):

        @pl.when(step == 2 * chunks * (b // 3))
        def _():
            copy_a(b).start()

    @pl.when(kind == 0)
    def _():
        upstream = g_s[layer, here, :]
        du = (dot_nt(gz_s[here, :], fc2_w[0]) * slope_ref[0].astype(f32)).astype(bf16)
        du_s[here, :] = du
        fc1_bg[...] += column_sum(du.astype(f32))
        dn = dot_nt(du, fc1_w[0])
        normal, inverse = norm_parts(mid_ref[0])
        gain = vec_ref[layer, 5:6, :]
        h2_s[here, :] = (normal * gain + vec_ref[layer, 7:8, :]).astype(bf16)
        vec_g[5:6, :] += column_sum(dn * normal)
        vec_g[7:8, :] += column_sum(dn)
        mid_grad = upstream + norm_back(dn, normal, inverse, gain)
        g_s[layer, here, :] = mid_grad
        branch = mid_grad.astype(bf16)
        ga_s[here, :] = branch
        vec_g[2:3, :] += column_sum(branch.astype(f32))

    def put(k, half, at, value, first, count):
        for r in range(n_row):
            packs[k][layer, half, r, at : at + count, :] = value[
                size * r + first : size * r + first + count, :
            ]

    @pl.when(step % (2 * chunks) == chunks - 1)
    def _():
        for j in range(4):
            value = dot_tn(h2_s[...], du_s[:, D * j : D * (j + 1)]).astype(bf16)
            put(1, j // 2, size * (j % 2), value, 0, size)
        value = dot_tn(att_ref[0], ga_s[...]).astype(bf16)
        put(1, 0, 2 * size, value, 0, low)
        put(1, 1, 2 * size, value, low, size - low)

    for b in (1, 4):

        @pl.when(step == 2 * chunks * (b // 3) + chunks - 1)
        def _():
            copy_a(b).start()

    @pl.when(kind == 1)
    def _():
        att_grad = dot_nt(ga_s[here, :], proj_w[0]).astype(bf16)
        table = [jnp.zeros((CELL, GROUP * CELL), f32) for _ in range(2)]
        for first in range(0, CHUNK_WINS, 4):
            spots = [(k, g) for k in range(first, first + 4) for g in range(2)]
            do_wides, dps, dss, parts = {}, {}, {}, {}

            def piece(k, g, at):
                return qkv_ref[
                    0, CELL * k : CELL * (k + 1), D * at + 128 * g : D * at + 128 * g + 256
                ]

            for k, g in spots:
                do = att_grad[CELL * k : CELL * (k + 1), 128 * g : 128 * g + 256]
                do_wides[k, g] = widen_heads(do, wide_heads_ref, g)
                val = piece(k, g, 2)
                dps[k, g] = dot_nt(val, do_wides[k, g])
            for k, g in spots:
                prob_low = prob_ref[
                    0, CELL * k : CELL * (k + 1), GROUP * CELL * g : GROUP * CELL * (g + 1)
                ]
                prob = prob_low.astype(f32)
                weighted = prob * dps[k, g]
                ds = (weighted - prob * column_sum(weighted)).astype(bf16)
                table[g] += ds.astype(f32)
                dss[k, g] = ds
                parts[k, g, 2] = dot_nn(prob_low, do_wides[k, g])
            for k, g in spots:
                parts[k, g, 0] = gather_heads(dot_tn(dss[k, g], piece(k, g, 1)), heads_ref, g)
                parts[k, g, 1] = dot_nn(dss[k, g], widen_heads(piece(k, g, 0), wide_heads_ref, g))
            for k in range(first, first + 4):
                there = pl.ds(pl.multiple_of(chunk * CHUNK + CELL * k, CELL), CELL)
                for at, factor in enumerate((SCALE, SCALE, 1.0)):
                    joined = join_groups(parts[k, 0, at], parts[k, 1, at]) * factor
                    dt_s[there, D * at : D * (at + 1)] = joined.astype(bf16)
        for g in range(2):
            table_g[:, GROUP * CELL * g : GROUP * CELL * (g + 1)] += table[g]
        dt = dt_s[here, :]
        vec_g[0:1, :] += column_sum(dt[:, 0:D].astype(f32))
        vec_g[1:2, :] += column_sum(dt[:, 2 * D :].astype(f32))
        dn = dot_nt(dt, qkv_w[0])
        normal, inverse = norm_parts(x_ref[0])
        gain = vec_ref[layer, 4:5, :]
        h1_s[here, :] = (normal * gain + vec_ref[layer, 6:7, :]).astype(bf16)
        vec_g[4:5, :] += column_sum(dn * normal)
        vec_g[6:7, :] += column_sum(dn)
        g_s[layer, here, :] += norm_back(dn, normal, inverse, gain)

    @pl.when(step == chunks + chunks // 2 - 1)
    def _():
        for col in range(WIN_COLS):
            at = CELL * (last_row + col) + 2 * BLOCK
            edge_out[2 * BLOCK * col : 2 * BLOCK * (col + 1), :] = g_s[
                1, at : at + 2 * BLOCK, :
            ].astype(bf16)
        edge_copy().start()

    @pl.when(step == 4 * chunks - 1)
    def _():
        for b in (4, 3, 2):
            advance(b)
        unpick_rows(g_s[0].astype(bf16), grad_rows)
        start_rows(grad_rows, grad_out, grad_sem)

    @pl.when(step % (2 * chunks) == 2 * chunks - 1)
    def _():
        values = [dot_tn(h1_s[...], dt_s[:, D * j : D * (j + 1)]).astype(bf16) for j in range(3)]
        put(2, 0, 0, values[0], 0, size)
        put(2, 0, size, values[1], 0, low)
        put(2, 1, 0, values[2], 0, size)
        put(2, 1, size, values[1], low, size - low)
        table = table_rows(table_g[...], lanes_ref, back_ref)
        table = jnp.concatenate([table, jnp.zeros((HEADS, D - TABLE_PAD), f32)], axis=1)
        vectors = jnp.concatenate(
            [vec_g[...]]
            + [fc1_bg[:, D * j : D * (j + 1)] for j in range(4)]
            + [jnp.zeros((4, D), f32)],
            axis=0,
        )
        for r in range(n_row):
            packs[2][layer, 0, r, size + low :, :] = vectors.astype(bf16)
            packs[2][layer, 1, r, size + low :, :] = table.astype(bf16)

    @pl.when(step == 2 * chunks - 1)
    def _():
        copy_a(2).start()

    @pl.when(step == 4 * chunks - 1)
    def _():
        copy_a(5).start()
        while min(reached) < len(stages):
            for b in (5, 4, 3, 2, 1, 0):
                advance(b)
        for b in range(len(BATCHES)):
            finish(b)
        edge_copy().wait_send()
        copies = [
            pltpu.make_async_copy(finals[k], out, done_sem.at[k])
            for k, out in enumerate((final_0, final_1, final_2))
        ]
        for copy in copies:
            copy.start()
        for copy in copies:
            copy.wait()
        for source, target, sem in (
            (rows_in, rows_out, rows_sem),
            (grad_rows, grad_out, grad_sem),
        ):
            if swap:
                swap_wait(place, source, target, sem)
                swap_end(place, source, target, sem)
                swap_own(place, source, target, sem).wait()
            else:
                pltpu.make_async_copy(source, target, sem.at[0, 0]).wait()


def backward_layers(placing, upstream, y, saved, full, vec):
    n_row, n_far = lax.axis_size("row"), lax.axis_size("clip") // 2
    n = 2 * n_row * n_far
    tokens = upstream.shape[0]
    chunks = tokens // CHUNK
    swap = can_swap(tokens, n)
    heads, wide = head_masks()
    lanes, _, back = table_constants()
    ff = full[2].shape[2]
    size = row_share(n_row)
    anywhere = pl.BlockSpec(memory_space=pl.ANY)

    def at(i):
        return 1 - i // (2 * chunks), i // chunks % 2, (i + chunks // 2) % chunks

    def layer_block(i):
        return 1 - i // (2 * chunks), 0, 0

    def forward_block(i):
        layer, kind, chunk = at(i)
        return (1 - kind) * layer, (1 - kind) * chunk + kind * (chunks // 2 - 1 + layer), 0

    def attention_block(i):
        layer, kind, chunk = at(i)
        return layer, kind * chunk + (1 - kind) * (chunks // 2), 0

    def chunked(value, block):
        return pl.BlockSpec((1, CHUNK, value.shape[2]), block)

    def layered(value):
        return pl.BlockSpec((1, *value.shape[1:]), layer_block)

    x, qkv, prob, att, mid, act, slope = saved
    constants = (
        vec,
        jnp.asarray(heads),
        jnp.asarray(wide, dtype=bf16),
        jnp.asarray(lanes.reshape(2 * TABLE_PAD, 128), dtype=bf16),
        jnp.asarray(back, dtype=bf16),
    )
    valid = [batch_rows(n_row, k) for k in range(3)]
    piece = [piece_rows(n_row, n_far, k) for k in range(3)]
    final = [(2, 2, n_far * piece[k], D) for k in range(3)]
    dma = pltpu.SemaphoreType.DMA

    def each(shape_of):
        return [pltpu.VMEM(shape_of(k), bf16) for k in range(3)]

    return pl.pallas_call(
        functools.partial(backward_kernel, n_row, n_far, swap),
        grid=(4 * chunks,),
        in_specs=[
            whole((1, tokens)),
            whole((tokens, D)),
            whole((tokens, D)),
            chunked(x, attention_block),
            chunked(qkv, attention_block),
            chunked(prob, attention_block),
            layered(att),
            chunked(mid, forward_block),
            layered(act),
            chunked(slope, forward_block),
        ]
        + [layered(weight) for weight in full]
        + [whole(constant.shape) for constant in constants],
        out_specs=[anywhere] * 5,
        out_shape=[jax.ShapeDtypeStruct((tokens, D), bf16)] * 2
        + [jax.ShapeDtypeStruct(shape, bf16) for shape in final],
        scratch_shapes=[
            pltpu.VMEM((8, D), f32),
            pltpu.VMEM((1, ff), f32),
            pltpu.VMEM((CELL, HEADS * CELL), f32),
            pltpu.VMEM((2, tokens, D), f32),
            pltpu.VMEM((tokens, D), bf16),
            pltpu.VMEM((tokens, 3 * D), bf16),
            pltpu.VMEM((tokens, D), bf16),
            pltpu.VMEM((tokens, D), bf16),
            pltpu.VMEM((tokens, ff), bf16),
            *[pltpu.VMEM((tokens, D), bf16)] * 2,
            pltpu.VMEM((WIN_COLS * 2 * BLOCK, D), bf16),
            pltpu.VMEM((WIN_COLS * 2 * BLOCK, D), bf16),
            *each(lambda k: (2, 2, n_row, valid[k], D)),
            *each(lambda k: (2, n_row, valid[k], D)),
            *each(lambda k: (2, n_row - 1, valid[k], D)),
            *each(lambda k: (2, n_far * piece[k], D)),
            *each(lambda k: (2, n_far - 1, piece[k], D)),
            *each(lambda k: final[k]),
            dma((2, n if swap else 1)),
            dma((2, n if swap else 1)),
            dma((2,)),
            dma((2, len(BATCHES))),
            dma((2, len(BATCHES), n_row - 1)),
            dma((2, len(BATCHES), n_far - 1)),
            dma((2, len(BATCHES), n_far - 1)),
            dma((2, len(BATCHES), n_far)),
            dma((3,)),
        ],
        compiler_params=pltpu.CompilerParams(
            collective_id=1, has_side_effects=True, vmem_limit_bytes=VMEM_LIMIT
        ),
        name="backward_layers",
    )(placing.reshape(1, tokens), upstream, y, x, qkv, prob, att, mid, act, slope, *full, *constants)


def close_kernel(
    n_row,
    fc2_ref,
    fc1_ref,
    qkv_ref,
    rows_ref,
    grad_ref,
    rows_o,
    grad_o,
    qkv_o,
    qvb_o,
    proj_o,
    projb_o,
    fc1_o,
    fc1b_o,
    fc2_o,
    fc2b_o,
    gain_o,
    shift_o,
    table_o,
):
    rows_o[...] = rows_ref[...]
    grad_o[...] = grad_ref[...].astype(f32)
    row = lax.axis_index("row")
    size = row_share(n_row)
    low = shard_half(size, 0)[1]
    layer = pl.program_id(0)
    for j in range(2):
        qkv_o[0, :, 2 * D * j : 2 * D * j + D] = qkv_ref[j, 0, 0:size, :].astype(f32)
    qkv_o[0, 0:low, D : 2 * D] = qkv_ref[0, 0, size : size + low, :].astype(f32)
    qkv_o[0, low:size, D : 2 * D] = qkv_ref[1, 0, size : 2 * size - low, :].astype(f32)
    proj_o[0, 0:low, :] = fc1_ref[0, 0, 2 * size : 2 * size + low, :].astype(f32)
    proj_o[0, low:size, :] = fc1_ref[1, 0, 2 * size : 3 * size - low, :].astype(f32)
    for j in range(4):
        at = size * (j % 2)
        fc1_o[0, :, D * j : D * (j + 1)] = fc1_ref[j // 2, 0, at : at + size, :].astype(f32)
    for j in range(2):
        fc2_o[0, 2 * size * j : 2 * size * (j + 1), :] = fc2_ref[j, 0, 0 : 2 * size, :].astype(f32)
    vectors = qkv_ref[0, 0, size + low : size + low + 16, :]
    lane = lax.broadcasted_iota(jnp.int32, (D, size), 0)
    want = lax.broadcasted_iota(jnp.int32, (D, size), 1)
    mine = dot_nn(vectors, jnp.where(lane == want + size * row, 1.0, 0.0).astype(bf16))
    start = 4 * size * row
    lane = lax.broadcasted_iota(jnp.int32, (D, 4 * size), 0)
    want = lax.broadcasted_iota(jnp.int32, (D, 4 * size), 1)
    spot = lax.broadcasted_iota(jnp.int32, (16, 4 * size), 0)
    wide = dot_nn(vectors, jnp.where(lane == want + start % D, 1.0, 0.0).astype(bf16))
    wide = column_sum(jnp.where(spot == 8 + start // D, wide, 0.0))
    qvb_o[0] = mine[0:2]
    gain_o[0] = mine[4:6]
    shift_o[0] = mine[6:8]
    for at in range(2):

        @pl.when(layer == at)
        def _():
            projb_o[at : at + 1, :] = mine[2:3]
            fc2b_o[at : at + 1, :] = mine[3:4]
            fc1b_o[at : at + 1, :] = wide

    table_o[0] = qkv_ref[1, 0, size + low : size + low + 16, 0:TABLE].astype(f32)


def close(rows, grads, finals):
    n_row = lax.axis_size("row")
    size = row_share(n_row)
    tokens = rows.shape[0]
    half = tokens // 2
    shapes = [
        (2, size, 3 * D),
        (2, 2, size),
        (2, size, D),
        (2, size),
        (2, size, 4 * D),
        (2, 4 * size),
        (2, 4 * size, D),
        (2, size),
        (2, 2, size),
        (2, 2, size),
        (2, HEADS, TABLE),
    ]

    def layered(shape):
        if len(shape) == 2:
            return whole(shape)
        return pl.BlockSpec((1, *shape[1:]), lambda i: (i, 0, 0))

    return pl.pallas_call(
        functools.partial(close_kernel, n_row),
        grid=(2,),
        in_specs=[
            pl.BlockSpec((2, 1, *final.shape[2:]), lambda i: (0, i, 0, 0)) for final in finals
        ]
        + [rows_of((half, D))] * 2,
        out_specs=[rows_of((half, D))] * 2 + [layered(shape) for shape in shapes],
        out_shape=[
            jax.ShapeDtypeStruct((tokens, D), bf16),
            jax.ShapeDtypeStruct((tokens, D), f32),
        ]
        + [jax.ShapeDtypeStruct(shape, f32) for shape in shapes],
        compiler_params=pltpu.CompilerParams(vmem_limit_bytes=VMEM_LIMIT),
        name="close",
    )(*finals, rows, grads)


def exchange(values):
    return lax.all_to_all(values, ("clip", "row"), split_axis=0, concat_axis=0, tiled=True)


def body(
    inputs,
    cotangent,
    source_of,
    split_row,
    qkv_weight,
    qv_bias,
    proj_weight,
    proj_bias,
    fc1_weight,
    fc1_bias,
    fc2_weight,
    fc2_bias,
    norm_gain,
    norm_bias,
    rel_table,
):
    clip_count = lax.axis_size("clip")
    row_count = lax.axis_size("row")
    tokens = inputs.shape[0]
    block_rows = tokens // (clip_count * row_count)
    grid_rows = tokens // GRID_COLS
    window_rows = grid_rows // WIN

    placing = source_of // tokens * block_rows + source_of % block_rows
    placing = placing.reshape(window_rows, 2, SHIFT, WIN_COLS, 2, SHIFT)
    placing = placing.transpose(0, 3, 1, 4, 2, 5).reshape(tokens)
    if not can_swap(tokens, clip_count * row_count):
        inputs, cotangent = exchange(inputs), exchange(cotangent)
    saved, upstream, layer_two, full, vec_rows = forward_layers(
        split_row,
        placing,
        inputs,
        cotangent,
        (qkv_weight, proj_weight, fc1_weight, fc2_weight),
        (qv_bias, proj_bias, fc1_bias, fc2_bias, norm_gain, norm_bias),
        rel_table,
    )
    output, input_grad, *finals = backward_layers(placing, upstream, layer_two, saved, full, vec_rows)
    if not can_swap(tokens, clip_count * row_count):
        output, input_grad = exchange(output), exchange(input_grad)
    output, input_grad, *totals = close(output, input_grad, finals)
    totals[-1] = totals[-1].transpose(0, 2, 1)
    return (output, input_grad, *totals)


def solution(mesh):
    placed = (
        P(("clip", "row"), None),
        P(("clip", "row"), None),
        P(("clip", "row")),
        P("clip"),
        P(None, "row", None),
        P(None, None, "row"),
        P(None, "row", None),
        P(None, "row"),
        P(None, "row", None),
        P(None, "row"),
        P(None, "row", None),
        P(None, "row"),
        P(None, None, "row"),
        P(None, None, "row"),
        P(),
    )
    return jax.shard_map(
        body,
        mesh=mesh,
        in_specs=placed,
        out_specs=(
            P(("clip", "row"), None),
            P(("clip", "row"), None),
            P(None, "row", None),
            P(None, None, "row"),
            P(None, "row", None),
            P(None, "row"),
            P(None, "row", None),
            P(None, "row"),
            P(None, "row", None),
            P(None, "row"),
            P(None, None, "row"),
            P(None, None, "row"),
            P(),
        ),
        check_vma=False,
    )
```

```python
import functools

import jax
import jax.numpy as jnp
import numpy as np
from jax import lax
from jax.experimental import pallas as pl
from jax.experimental.pallas import tpu as pltpu
from jax.sharding import PartitionSpec as P

WIN = 8
SHIFT = 4
GRID_COLS = 64
EPSILON = 1e-05
MASKED = -1000000000.0
ROOT_HALF = 0.7071067811865476
INV_ROOT_TAU = 0.3989422804014327

HEADS = 16
HEAD_DIM = 24
D = HEADS * HEAD_DIM
GROUP = 8
CELL = WIN * WIN
BLOCK = SHIFT * SHIFT
WIN_COLS = GRID_COLS // WIN
SPREAD = 2 * WIN - 1
TABLE = SPREAD * SPREAD
TABLE_PAD = 256
SCALE = HEAD_DIM**-0.5
CHUNK = 256
CHUNK_WINS = CHUNK // CELL
VMEM_LIMIT = 56 * 1024 * 1024

MESH = pl.DeviceIdType.MESH
f32 = jnp.float32
bf16 = jnp.bfloat16


def window_places():
    spot = np.arange(CELL)
    row = (spot // 32) * SHIFT + (spot % BLOCK) // SHIFT
    col = (spot // BLOCK % 2) * SHIFT + spot % SHIFT
    return row, col


def head_masks():
    feature = np.arange(D) // HEAD_DIM
    rows = (feature[None, :] == np.arange(HEADS)[:, None]).astype(np.float32)
    wide = np.stack(
        [
            np.repeat(rows[GROUP * g : GROUP * (g + 1), 128 * g : 128 * g + 256], CELL, axis=0)
            for g in range(2)
        ]
    )
    return rows, wide


def table_constants():
    row, col = window_places()
    natural = row * WIN + col
    lanes = np.zeros((2, TABLE_PAD, 128), np.float32)
    for half in range(2):
        lanes[half, row * SPREAD + col, half * CELL + np.arange(CELL)] = 1.0
    order = np.zeros((CELL, CELL), np.float32)
    order[np.arange(CELL), natural] = 1.0
    back = np.zeros((CELL, CELL), np.float32)
    back[row * WIN + (WIN - 1 - col), np.arange(CELL)] = 1.0
    return lanes, order, back


def dot_nn(a, b):
    return lax.dot_general(a, b, (((1,), (0,)), ((), ())), preferred_element_type=f32)


def dot_nt(a, b):
    return lax.dot_general(a, b, (((1,), (1,)), ((), ())), preferred_element_type=f32)


def dot_tn(a, b):
    return lax.dot_general(a, b, (((0,), (0,)), ((), ())), preferred_element_type=f32)


def dot_exact(a, b, dims):
    return lax.dot_general(
        a, b, (dims, ((), ())), precision=lax.Precision.HIGHEST, preferred_element_type=f32
    )


def split(values):
    high = values.astype(bf16)
    rest = values - high.astype(f32)
    middle = rest.astype(bf16)
    return high, middle, (rest - middle.astype(f32)).astype(bf16)


def whole(shape):
    zeros = (0,) * len(shape)
    return pl.BlockSpec(shape, lambda i: zeros)


def rows_of(shape):
    return pl.BlockSpec(shape, lambda i: (i, 0))


def norm_parts(values):
    centred = values - jnp.mean(values, axis=-1, keepdims=True)
    inverse = lax.rsqrt(jnp.mean(centred * centred, axis=-1, keepdims=True) + EPSILON)
    return centred * inverse, inverse


def norm_back(upstream, normal, inverse, gain):
    scaled = upstream * gain
    centred = scaled - jnp.mean(scaled, axis=-1, keepdims=True)
    return inverse * (centred - normal * jnp.mean(scaled * normal, axis=-1, keepdims=True))


def column_sum(values):
    return jnp.sum(values, axis=0, keepdims=True)


def bias_rows(table_ref, lanes_ref, order_ref, out_ref, wide_ref):
    for layer in range(2):
        for head in range(HEADS):
            pair, half = divmod(head, 2)
            spread = jnp.broadcast_to(table_ref[layer, head : head + 1, :], (WIN, TABLE_PAD))
            for i in range(WIN):
                at = CELL * pair + WIN * i
                wide_ref[at : at + WIN, TABLE_PAD * half : TABLE_PAD * (half + 1)] = pltpu.roll(
                    spread, (SPREAD * i - 112) % TABLE_PAD, 1, stride=1, stride_axis=0
                )
        picked = sum(dot_nn(part, lanes_ref[...]) for part in reversed(split(wide_ref[...])))
        joined = jnp.concatenate(
            [picked[CELL * pair : CELL * (pair + 1), :] for pair in range(HEADS // 2)], axis=1
        )
        out_ref[layer] = sum(dot_nn(order_ref[...], part) for part in reversed(split(joined)))


def table_rows(grads, lanes_ref, back_ref):
    turned = sum(dot_nn(back_ref[...], part) for part in reversed(split(grads)))
    stacked = jnp.concatenate([turned[:, 128 * i : 128 * (i + 1)] for i in range(HEADS // 2)], axis=0)
    spread = sum(dot_nt(part, lanes_ref[...]) for part in reversed(split(stacked)))
    rows = []
    for head in range(HEADS):
        pair, half = divmod(head, 2)
        total = jnp.zeros((WIN, TABLE_PAD), f32)
        for i in range(WIN):
            at = CELL * pair + WIN * i
            total += pltpu.roll(
                spread[at : at + WIN, TABLE_PAD * half : TABLE_PAD * (half + 1)],
                (112 - SPREAD * i - (WIN - 1)) % TABLE_PAD,
                1,
                stride=1,
                stride_axis=0,
            )
        rows.append(column_sum(total))
    return jnp.concatenate(rows, axis=0)


def quarter(window, sub):
    return pl.ds(CELL * window + BLOCK * sub, BLOCK)


def assemble_back(main_ref, edge_ref, out_ref):
    windows = main_ref.shape[0] // CELL
    for window in range(windows):
        wr, wc = divmod(window, WIN_COLS)
        before = (wc - 1) % WIN_COLS
        out_ref[quarter(window, 3), :] = main_ref[quarter(window, 0), :].astype(out_ref.dtype)
        out_ref[quarter(window, 2), :] = main_ref[
            quarter(wr * WIN_COLS + before, 1), :
        ].astype(out_ref.dtype)
        for sub, col, piece in ((1, wc, 0), (0, before, 1)):
            if wr == 0:
                value = edge_ref[pl.ds(2 * BLOCK * col + BLOCK * piece, BLOCK), :]
            else:
                value = main_ref[quarter((wr - 1) * WIN_COLS + col, 2 + piece), :]
            out_ref[quarter(window, sub), :] = value.astype(out_ref.dtype)


def assemble_ahead(main_ref, edge_ref, out_ref, window_rows):
    last = main_ref.shape[0] // CELL // WIN_COLS - 1
    for wr in window_rows:
        for wc in range(WIN_COLS):
            window = wr * WIN_COLS + wc
            after = (wc + 1) % WIN_COLS
            out_ref[quarter(window, 0), :] = main_ref[quarter(window, 3), :].astype(out_ref.dtype)
            out_ref[quarter(window, 1), :] = main_ref[
                quarter(wr * WIN_COLS + after, 2), :
            ].astype(out_ref.dtype)
            for sub, col, piece in ((2, wc, 1), (3, after, 0)):
                if wr == last:
                    value = edge_ref[pl.ds(2 * BLOCK * col + BLOCK * piece, BLOCK), :]
                else:
                    value = main_ref[quarter((wr + 1) * WIN_COLS + col, piece), :]
                out_ref[quarter(window, sub), :] = value.astype(out_ref.dtype)


class Place:
    def __init__(self, n_row, n_far):
        clip = lax.axis_index("clip")
        self.n_row, self.n_far = n_row, n_far
        self.core, self.far, self.row = clip % 2, clip // 2, lax.axis_index("row")
        self.n = 2 * n_far * n_row
        self.index = clip * n_row + self.row

    def index_at(self, d):
        return (self.index + d) % self.n

    def device(self, d):
        at = self.index_at(d)
        return (at // self.n_row, at % self.n_row)

    def row_at(self, d):
        return (self.row + d) % self.n_row

    def far_at(self, d):
        return (self.far + d) % self.n_far

    def twin(self):
        return (2 * self.far + 1 - self.core, self.row)

    def at_row(self, row):
        return (2 * self.far + self.core, row)

    def in_row(self, d):
        return self.at_row(self.row_at(d))

    def at_far(self, far):
        return (2 * far + self.core, self.row)

    def along(self, d):
        return self.at_far(self.far_at(d))

    def partners(self, far=True):
        found = [self.twin()] + [self.in_row(d) for d in range(1, self.n_row)]
        return found + ([self.along(d) for d in range(1, self.n_far)] if far else [])


def meet(partners):
    barrier = pltpu.get_barrier_semaphore()
    for partner in partners:
        pl.semaphore_signal(barrier, inc=1, device_id=partner, device_id_type=MESH)
    pl.semaphore_wait(barrier, len(partners))


def send(src, dst, send_sem, recv_sem, target):
    copy = pltpu.make_async_remote_copy(
        src_ref=src,
        dst_ref=dst,
        send_sem=send_sem,
        recv_sem=recv_sem,
        device_id=target,
        device_id_type=MESH,
    )
    copy.start()
    return copy


def remote(src, dst, send_sem, recv_sem, target):
    return pltpu.make_async_remote_copy(
        src_ref=src,
        dst_ref=dst,
        send_sem=send_sem,
        recv_sem=recv_sem,
        device_id=target,
        device_id_type=MESH,
    )


def can_swap(tokens, n):
    return tokens // n % 16 == 0


def meet_all(place, meanwhile):
    barrier = pltpu.get_barrier_semaphore()

    def greet(d, carry):
        pl.semaphore_signal(barrier, inc=1, device_id=place.device(d), device_id_type=MESH)
        return carry

    lax.fori_loop(1, place.n, greet, 0)
    meanwhile()
    pl.semaphore_wait(barrier, place.n - 1)


def swap_block(place, ref, index):
    count = ref.shape[0] // place.n
    return ref.at[pl.ds(pl.multiple_of(index * count, 16), count), :]


def swap_own(place, src, dst, sem):
    return pltpu.make_async_copy(
        swap_block(place, src, place.index), swap_block(place, dst, place.index), sem.at[0, 0]
    )


def swap_copy(place, src, dst, sem, d, owner):
    return remote(
        swap_block(place, src, place.index_at(d)),
        swap_block(place, dst, owner),
        sem.at[0, d],
        sem.at[1, d],
        place.device(d),
    )


def swap_start(place, src, dst, sem):
    def work(d, carry):
        swap_copy(place, src, dst, sem, d, place.index).start()
        return carry

    lax.fori_loop(1, place.n, work, 0)


def swap_wait(place, src, dst, sem):
    def work(d, carry):
        swap_copy(place, src, dst, sem, d, place.index_at(place.n - d)).wait_recv()
        return carry

    lax.fori_loop(1, place.n, work, 0)


def swap_end(place, src, dst, sem):
    def work(d, carry):
        swap_copy(place, src, dst, sem, d, place.index).wait_send()
        return carry

    lax.fori_loop(1, place.n, work, 0)


def row_share(n_row):
    return D // n_row


HEIGHTS = (1, 1, 1, 4)
KINDS = ((0, 1), (2, 3))


def shard_half(height, core):
    low = -(-height // 32) * 16
    return (0, low) if core == 0 else (low, height - low)


def forward_kernel(
    n_row,
    n_far,
    swap,
    split_ref,
    place_col,
    place_row,
    x_in,
    c_in,
    qkv_i,
    proj_i,
    fc1_i,
    fc2_i,
    qv_bias,
    proj_bias,
    fc1_bias,
    fc2_bias,
    gain_ref,
    shift_ref,
    table_ref,
    lanes_ref,
    order_ref,
    heads_ref,
    wide_heads_ref,
    x_out,
    qkv_out,
    prob_out,
    att_out,
    mid_out,
    act_out,
    slope_out,
    up_out,
    y_out,
    qkv_wo,
    proj_wo,
    fc1_wo,
    fc2_wo,
    vec_out,
    x_got,
    c_got,
    qkv_s,
    proj_s,
    fc1_s,
    fc2_s,
    vec_wide,
    vec_mine,
    vec_got,
    qkv_b,
    fc1_b,
    table_s,
    bias_s,
    wide_s,
    x_s,
    y_s,
    c_s,
    order_s,
    edge_out,
    edge_in,
    x_sem,
    c_sem,
    own_sem,
    row_sem,
    twin_sem,
    vec_sem,
    edge_sem,
    out_sem,
):
    step = pl.program_id(0)
    tokens = x_s.shape[0]
    chunks = tokens // CHUNK
    layer = step // (2 * chunks)
    kind = step // chunks % 2
    chunk = (step + layer * kind * (chunks // 2)) % chunks
    place = Place(n_row, n_far)
    size = row_share(n_row)
    shards = (qkv_i, proj_i, fc1_i, fc2_i)
    kept = (qkv_s, proj_s, fc1_s, fc2_s)
    outs = (qkv_wo, proj_wo, fc1_wo, fc2_wo)
    window_rows = tokens // CELL // WIN_COLS
    last_row = (window_rows - 1) * WIN_COLS
    square = n_row == 4
    direct = range(2 if square else n_row - 1)
    slots = range(n_row - 1)
    if not swap:
        x_got, c_got = x_in, c_in

    def own(l, w):
        return pltpu.make_async_copy(
            shards[w].at[l], spot(l, w, place.row, 0, HEIGHTS[w] * size), own_sem.at[l, w]
        )

    def spot(l, w, owner, first, count):
        at = pl.multiple_of(owner * HEIGHTS[w] * size + first, 16)
        return kept[w].at[l, pl.ds(at, count), :]

    def neighbour(slot):
        row = place.row
        return (row + 1 - 2 * (row % 2), (row + 2) % 4, 3 - row)[slot]

    def source(slot):
        return neighbour(slot) if square else place.row_at(n_row - 1 - slot)

    def target(slot):
        return place.at_row(neighbour(slot) if square else place.row_at(slot + 1))

    def push(l, core, w, slot, owner=None):
        first, count = shard_half(HEIGHTS[w] * size, core)
        return remote(
            shards[w].at[l, pl.ds(first, count), :],
            spot(l, w, place.row if owner is None else owner, first, count),
            row_sem.at[0, l, w, slot],
            row_sem.at[1, l, w, slot],
            target(slot),
        )

    def relay(l, core, w):
        axis = (w + core) % 2
        here = spot(l, w, source(axis), *shard_half(HEIGHTS[w] * size, core))
        return remote(
            here, here, row_sem.at[0, l, w, 2], row_sem.at[1, l, w, 2], target(1 - axis)
        )

    def hand(l, core, w, slot):
        here = spot(l, w, source(slot), *shard_half(HEIGHTS[w] * size, core))
        return remote(
            here, here, twin_sem.at[0, l, w, slot], twin_sem.at[1, l, w, slot], place.twin()
        )

    def by_core(work):
        for core in range(2):
            pl.when(place.core == core)(functools.partial(work, core))

    def start_weights(l, k):
        def work(core):
            for w in KINDS[k]:
                for slot in direct:
                    push(l, core, w, slot).start()

        by_core(work)

    def pass_weights(l, k):
        def work(core):
            for w in KINDS[k]:
                for slot in direct:
                    push(l, core, w, slot, source(slot)).wait_recv()
                    if square and slot == (w + core) % 2:
                        relay(l, core, w).start()
                    hand(l, core, w, slot).start()

        by_core(work)

    def pass_relayed(l, k):
        def work(core):
            for w in KINDS[k]:
                push(l, core, w, 2, source(2)).wait_recv()
                hand(l, core, w, 2).start()

        if square:
            by_core(work)

    def wait_weights(l, k):
        def work(core):
            for w in KINDS[k]:
                for slot in slots:
                    hand(l, 1 - core, w, slot).wait_recv()

        by_core(work)
        for w in KINDS[k]:
            own(l, w).wait()

    def end_weights():
        def work(core):
            for l in range(2):
                for w in range(4):
                    for slot in direct:
                        push(l, core, w, slot).wait_send()
                    if square:
                        relay(l, core, w).wait_send()
                    for slot in slots:
                        hand(l, core, w, slot).wait_send()

        by_core(work)

    def vector_copy(d):
        return remote(
            vec_mine,
            vec_got.at[place.row],
            vec_sem.at[0, d - 1],
            vec_sem.at[1, d - 1],
            place.in_row(d),
        )

    def edge_copy(which):
        return remote(
            edge_out.at[which],
            edge_in.at[which],
            edge_sem.at[0, which],
            edge_sem.at[1, which],
            place.in_row(1 if which == 2 else n_row - 1),
        )

    def pack_edge(which, values, first_window, first_sub):
        for col in range(WIN_COLS):
            at = CELL * (first_window + col) + BLOCK * first_sub
            edge_out[which, 2 * BLOCK * col : 2 * BLOCK * (col + 1), :] = values[
                at : at + 2 * BLOCK, :
            ].astype(bf16)

    def pick_rows(values, out):
        for c in range(chunks):
            rows = slice(CHUNK * c, CHUNK * (c + 1))
            spots = lax.broadcasted_iota(jnp.int32, (CHUNK, tokens), 1)
            pick = jnp.where(spots == place_col[rows, :], 1.0, 0.0).astype(bf16)
            out[rows, :] = dot_nn(pick, values[...]).astype(out.dtype)

    @pl.when(step == 0)
    def _():
        def start_own():
            for l in range(2):
                for w in range(4):
                    own(l, w).start()
            if swap:
                swap_own(place, x_in, x_got, x_sem).start()
                swap_own(place, c_in, c_got, c_sem).start()

        if swap:
            meet_all(place, start_own)
            swap_start(place, x_in, x_got, x_sem)
        else:
            start_own()
            meet(place.partners(far=False))
        start_weights(0, 0)
        vec_wide[...] = jnp.zeros_like(vec_wide)
        for l in range(2):
            parts = (
                qv_bias[l],
                proj_bias[l : l + 1],
                fc2_bias[l : l + 1],
                gain_ref[l],
                shift_ref[l],
            )
            vec_wide[16 * l : 16 * l + 8, 0:size] = jnp.concatenate(
                [part.astype(f32) for part in parts], axis=0
            )
            vec_wide[16 * l + 8 : 16 * l + 9, 0 : 4 * size] = fc1_bias[l : l + 1].astype(f32)
        vec_mine[...] = vec_wide[...].astype(bf16)
        for d in range(1, n_row):
            vector_copy(d).start()
        mine = pltpu.make_async_copy(vec_mine, vec_got.at[place.row], out_sem.at[4])
        mine.start()
        table_s[...] = jnp.zeros_like(table_s)
        table_s[:, :, 0:TABLE] = table_ref[...]
        bias_rows(table_s, lanes_ref, order_ref, bias_s, wide_s)
        mine.wait()
        for d in range(1, n_row):
            vector_copy(d).wait()
        for l in range(2):
            shares = [vec_got[r, 16 * l : 16 * (l + 1), :].astype(f32) for r in range(n_row)]
            rows = jnp.concatenate([share[0:8, 0:size] for share in shares], axis=1)
            vec_out[l] = rows
            qkv_b[l, 0:1, 0:D] = rows[0:1]
            qkv_b[l, 0:1, D : 2 * D] = jnp.zeros((1, D), f32)
            qkv_b[l, 0:1, 2 * D : 3 * D] = rows[1:2]
            fc1_b[l, 0:1, :] = jnp.concatenate(
                [share[8:9, 0 : 4 * size] for share in shares], axis=1
            )
        pass_weights(0, 0)
        start_weights(0, 1)
        if swap:
            swap_wait(place, x_in, x_got, x_sem)
            swap_own(place, x_in, x_got, x_sem).wait()
        pick_rows(x_got, x_s)
        pass_relayed(0, 0)
        wait_weights(0, 0)
        start_weights(1, 0)

    @pl.when(step == 1)
    def _():
        pass_weights(0, 1)
        start_weights(1, 1)

    @pl.when(step == chunks - 1)
    def _():
        pass_relayed(0, 1)

    @pl.when(step == chunks)
    def _():
        wait_weights(0, 1)
        pass_weights(1, 0)

    @pl.when(step == chunks + 2)
    def _():
        pass_relayed(1, 0)

    @pl.when(step == 2 * chunks - 1)
    def _():
        pass_weights(1, 1)

    @pl.when(step == 2 * chunks)
    def _():
        wait_weights(1, 0)
        assemble_ahead(y_s, edge_in.at[0], x_s, range(window_rows - 1))

    @pl.when(step == 2 * chunks + chunks // 2)
    def _():
        pass_relayed(1, 1)
        edge_copy(0).wait_recv()
        assemble_ahead(y_s, edge_in.at[0], x_s, range(window_rows - 1, window_rows))

    @pl.when(step == 3 * chunks)
    def _():
        wait_weights(1, 1)
        for w in range(4):
            pltpu.make_async_copy(kept[w], outs[w], out_sem.at[w]).start()

    @pl.when(step == 2 * chunks - 1)
    def _():
        if swap:
            swap_start(place, c_in, c_got, c_sem)

    @pl.when(step == 4 * chunks - 2)
    def _():
        if swap:
            swap_wait(place, c_in, c_got, c_sem)
            swap_own(place, c_in, c_got, c_sem).wait()
        pick_rows(c_got, c_s)
        pack_edge(1, c_s, 0, 0)
        edge_copy(1).start()

    here = pl.ds(pl.multiple_of(chunk * CHUNK, CHUNK), CHUNK)

    @pl.when(kind == 0)
    def _():
        x = x_s[here, :]
        x_out[0] = x
        normal, _ = norm_parts(x)
        hidden = (normal * vec_out[layer, 4:5, :] + vec_out[layer, 6:7, :]).astype(bf16)
        qkv_out[0] = (dot_nn(hidden, qkv_s[layer]) + qkv_b[layer]).astype(bf16)
        wide = (CELL, GROUP * CELL)
        apart = lax.broadcasted_iota(jnp.int32, wide, 0) ^ lax.broadcasted_iota(jnp.int32, wide, 1)
        for first in range(0, CHUNK_WINS, 4):
            spots = [(k, g) for k in range(first, first + 4) for g in range(2)]
            scores, probs, mixed = {}, {}, {}
            for k, g in spots:
                rows = slice(CELL * k, CELL * (k + 1))
                key = qkv_out[0, rows, D + 128 * g : D + 128 * g + 256]
                scores[k, g] = dot_nt(key, widen_heads(qkv_out[0, rows, 128 * g : 128 * g + 256], wide_heads_ref, g))
            for k, g in spots:
                window = chunk * CHUNK_WINS + k
                middle = (place.row * window_rows + window // WIN_COLS + 1) * WIN
                row_cut = (middle == split_ref[0]) | (middle == n_row * window_rows * WIN)
                col_cut = window % WIN_COLS == WIN_COLS - 1
                cut = layer * (jnp.where(row_cut, 32, 0) + jnp.where(col_cut, 16, 0))
                lanes = slice(GROUP * CELL * g, GROUP * CELL * (g + 1))
                score = scores[k, g] * SCALE + bias_s[layer, :, lanes]
                score = jnp.where((apart & cut) == 0, score, MASKED)
                e = jnp.exp(score - jnp.max(score, axis=0, keepdims=True))
                prob = (e * (1.0 / jnp.sum(e, axis=0, keepdims=True))).astype(bf16)
                prob_out[0, CELL * k : CELL * (k + 1), lanes] = prob
                probs[k, g] = prob
            for k, g in spots:
                val = qkv_out[0, CELL * k : CELL * (k + 1), 2 * D + 128 * g : 2 * D + 128 * g + 256]
                mixed[k, g] = gather_heads(dot_tn(probs[k, g], val), heads_ref, g)
            for k in range(first, first + 4):
                att_out[0, CELL * k : CELL * (k + 1), :] = join_groups(
                    mixed[k, 0], mixed[k, 1]
                ).astype(bf16)
        mid = x + (dot_nn(att_out[0], proj_s[layer]) + vec_out[layer, 2:3, :])
        x_s[here, :] = mid
        mid_out[0] = mid

    @pl.when(kind == 1)
    def _():
        mid = x_s[here, :]
        normal, _ = norm_parts(mid)
        hidden = (normal * vec_out[layer, 5:6, :] + vec_out[layer, 7:8, :]).astype(bf16)
        u = dot_nn(hidden, fc1_s[layer]) + fc1_b[layer]
        cdf = 0.5 * (1.0 + lax.erf(u * ROOT_HALF))
        act_out[0] = (u * cdf).astype(bf16)
        slope_out[0] = (cdf + u * (jnp.exp(-0.5 * u * u) * INV_ROOT_TAU)).astype(bf16)
        y_s[here, :] = mid + (dot_nn(act_out[0], fc2_s[layer]) + vec_out[layer, 3:4, :])

    @pl.when(step == chunks + chunks // 2 - 1)
    def _():
        pack_edge(0, y_s, 0, 0)
        edge_copy(0).start()

    @pl.when(step == 3 * chunks + chunks // 2 - 1)
    def _():
        pack_edge(2, y_s, last_row, 2)
        edge_copy(2).start()

    @pl.when(step == 4 * chunks - 1)
    def _():
        edge_copy(2).wait_recv()
        assemble_back(y_s, edge_in.at[2], order_s)
        for c in range(chunks):
            rows = slice(CHUNK * c, CHUNK * (c + 1))
            spots = lax.broadcasted_iota(jnp.int32, (CHUNK, tokens), 0) + CHUNK * c
            pick = jnp.where(spots == place_row[...], 1.0, 0.0).astype(bf16)
            y_out[rows, :] = dot_nn(pick, order_s[...]).astype(bf16)
        edge_copy(1).wait_recv()
        assemble_ahead(c_s, edge_in.at[1], up_out, range(window_rows))
        end_weights()
        for which in range(3):
            edge_copy(which).wait_send()
        for w in range(4):
            pltpu.make_async_copy(kept[w], outs[w], out_sem.at[w]).wait()
        if swap:
            swap_end(place, x_in, x_got, x_sem)
            swap_end(place, c_in, c_got, c_sem)


def gather_heads(spread, heads_ref, g):
    tiles = []
    for tile in range(2):
        lanes = slice(128 * tile, 128 * (tile + 1))
        first = 128 * (g + tile)
        total = None
        for h in range(GROUP):
            head = GROUP * g + h
            if HEAD_DIM * head >= first + 128 or HEAD_DIM * (head + 1) <= first:
                continue
            part = (
                spread[CELL * h : CELL * (h + 1), lanes]
                * heads_ref[head : head + 1, first : first + 128]
            )
            total = part if total is None else total + part
        tiles.append(total)
    return jnp.concatenate(tiles, axis=1)


def widen_heads(values, wide_heads_ref, g):
    rows = []
    for h in range(GROUP):
        head = GROUP * g + h
        tiles = []
        for tile in range(2):
            first = 128 * (g + tile)
            if HEAD_DIM * head >= first + 128 or HEAD_DIM * (head + 1) <= first:
                tiles.append(jnp.zeros((CELL, 128), bf16))
            else:
                lanes = slice(128 * tile, 128 * (tile + 1))
                tiles.append(
                    values[:, lanes] * wide_heads_ref[g, CELL * h : CELL * (h + 1), lanes]
                )
        rows.append(jnp.concatenate(tiles, axis=1))
    return jnp.concatenate(rows, axis=0)


def join_groups(low, high):
    return jnp.concatenate([low[:, :128], low[:, 128:] + high[:, :128], high[:, 128:]], axis=1)


def forward_layers(split_row, placing, x_in, c_in, shards, vectors, rel_table):
    n_row, n_far = lax.axis_size("row"), lax.axis_size("clip") // 2
    n = 2 * n_row * n_far
    tokens = x_in.shape[0]
    chunks = tokens // CHUNK
    swap = can_swap(tokens, n)
    heads, wide = head_masks()
    lanes, order, _ = table_constants()
    ff = shards[2].shape[2]
    anywhere = pl.BlockSpec(memory_space=pl.ANY)
    patches = anywhere if swap else whole((tokens, D))
    small = (
        *vectors,
        rel_table.transpose(0, 2, 1),
        jnp.asarray(lanes.reshape(2 * TABLE_PAD, 128), dtype=bf16),
        jnp.asarray(order, dtype=bf16),
        jnp.asarray(heads),
        jnp.asarray(wide, dtype=bf16),
    )
    full = [(2, shard.shape[1] * n_row, shard.shape[2]) for shard in shards]

    def attention_block(i):
        kind = i // chunks % 2
        return i // (2 * chunks), (1 - kind) * (i % chunks) + kind * (chunks - 1), 0

    def forward_block(i):
        layer, kind = i // (2 * chunks), i // chunks % 2
        half = layer * (chunks // 2)
        return layer, kind * ((i + half) % chunks) + (1 - kind) * half, 0

    saved = [
        (D, f32, attention_block),
        (3 * D, bf16, attention_block),
        (HEADS * CELL, bf16, attention_block),
        (D, bf16, attention_block),
        (D, f32, attention_block),
        (ff, bf16, forward_block),
        (ff, bf16, forward_block),
    ]
    dma = pltpu.SemaphoreType.DMA
    results = pl.pallas_call(
        functools.partial(forward_kernel, n_row, n_far, swap),
        grid=(4 * chunks,),
        in_specs=[
            pl.BlockSpec(memory_space=pltpu.SMEM),
            whole((tokens, 1)),
            whole((1, tokens)),
            patches,
            patches,
        ]
        + [anywhere] * 4
        + [whole(value.shape) for value in small],
        out_specs=[pl.BlockSpec((1, CHUNK, width), block) for width, _, block in saved]
        + [whole((tokens, D))] * 2
        + [anywhere] * 4
        + [whole((2, 8, D))],
        out_shape=[jax.ShapeDtypeStruct((2, tokens, width), kind) for width, kind, _ in saved]
        + [jax.ShapeDtypeStruct((tokens, D), bf16)] * 2
        + [jax.ShapeDtypeStruct(shape, bf16) for shape in full]
        + [jax.ShapeDtypeStruct((2, 8, D), f32)],
        scratch_shapes=[
            pltpu.VMEM((tokens if swap else 16, D), bf16),
            pltpu.VMEM((tokens if swap else 16, D), bf16),
            *[pltpu.VMEM(shape, bf16) for shape in full],
            pltpu.VMEM((32, D), f32),
            pltpu.VMEM((32, D), bf16),
            pltpu.VMEM((n_row, 32, D), bf16),
            pltpu.VMEM((2, 1, 3 * D), f32),
            pltpu.VMEM((2, 1, ff), f32),
            pltpu.VMEM((2, HEADS, TABLE_PAD), f32),
            pltpu.VMEM((2, CELL, HEADS * CELL), f32),
            pltpu.VMEM((HEADS // 2 * CELL, 2 * TABLE_PAD), f32),
            pltpu.VMEM((tokens, D), f32),
            pltpu.VMEM((tokens, D), f32),
            pltpu.VMEM((tokens, D), bf16),
            pltpu.VMEM((tokens, D), bf16),
            pltpu.VMEM((3, WIN_COLS * 2 * BLOCK, D), bf16),
            pltpu.VMEM((3, WIN_COLS * 2 * BLOCK, D), bf16),
            dma((2, n if swap else 1)),
            dma((2, n if swap else 1)),
            dma((2, 4)),
            dma((2, 2, 4, n_row - 1)),
            dma((2, 2, 4, n_row - 1)),
            dma((2, n_row - 1)),
            dma((2, 3)),
            dma((5,)),
        ],
        compiler_params=pltpu.CompilerParams(
            collective_id=0, has_side_effects=True, vmem_limit_bytes=VMEM_LIMIT
        ),
        name="forward_layers",
    )(
        split_row,
        placing.reshape(tokens, 1),
        placing.reshape(1, tokens),
        x_in,
        c_in,
        *shards,
        *small,
    )
    return results[:7], results[7], results[8], results[9:13], results[13]


BATCHES = ((1, 0), (1, 1), (1, 2), (0, 0), (0, 1), (0, 2))


def batch_rows(n_row, kind):
    size = row_share(n_row)
    low = shard_half(size, 0)[1]
    return (2 * size, 2 * size + low, size + low + 16)[kind]


def piece_rows(n_row, n_far, kind):
    return -(-batch_rows(n_row, kind) // (16 * n_far)) * 16


def backward_kernel(
    n_row,
    n_far,
    swap,
    place_row,
    up_ref,
    rows_in,
    x_ref,
    qkv_ref,
    prob_ref,
    att_ref,
    mid_ref,
    act_ref,
    slope_ref,
    qkv_w,
    proj_w,
    fc1_w,
    fc2_w,
    vec_ref,
    heads_ref,
    wide_heads_ref,
    lanes_ref,
    back_ref,
    rows_out,
    grad_out,
    final_0,
    final_1,
    final_2,
    vec_g,
    fc1_bg,
    table_g,
    g_s,
    h1_s,
    dt_s,
    ga_s,
    h2_s,
    du_s,
    gz_s,
    grad_rows,
    edge_out,
    edge_in,
    *refs,
):
    packs, got_as, got_bs, out_cs, got_cs, finals = (refs[3 * i : 3 * i + 3] for i in range(6))
    rows_sem, grad_sem, edge_sem, a_sem, b_sem, c_sem, d_sem, e_sem, done_sem = refs[18:]
    step = pl.program_id(0)
    tokens = g_s.shape[1]
    chunks = tokens // CHUNK
    layer = 1 - step // (2 * chunks)
    kind = step // chunks % 2
    chunk = (step + chunks // 2) % chunks
    place = Place(n_row, n_far)
    core, row, far = place.core, place.row, place.far
    size = row_share(n_row)
    low = shard_half(size, 0)[1]
    last_row = (tokens // CELL // WIN_COLS - 1) * WIN_COLS
    here = pl.ds(pl.multiple_of(chunk * CHUNK, CHUNK), CHUNK)

    def edge_copy():
        return remote(edge_out, edge_in, edge_sem.at[0], edge_sem.at[1], place.in_row(1))

    def start_rows(source, target, sem):
        if swap:
            swap_own(place, source, target, sem).start()
            swap_start(place, source, target, sem)
        else:
            pltpu.make_async_copy(source, target, sem.at[0, 0]).start()

    def unpick_rows(values, out):
        for c in range(chunks):
            rows = slice(CHUNK * c, CHUNK * (c + 1))
            spots = lax.broadcasted_iota(jnp.int32, (CHUNK, tokens), 0) + CHUNK * c
            pick = jnp.where(spots == place_row[...], 1.0, 0.0).astype(bf16)
            out[rows, :] = dot_nn(pick, values).astype(bf16)

    def part(ref, b, at):
        rows = got_cs[BATCHES[b][1]].shape[2]
        return ref.at[BATCHES[b][0], pl.ds(pl.multiple_of(at * rows, 16), rows), :]

    def copy_a(b):
        l, k = BATCHES[b]
        return remote(
            packs[k].at[l, 1 - core], got_as[k].at[l], a_sem.at[0, b], a_sem.at[1, b], place.twin()
        )

    def copy_b(b, d):
        l, k = BATCHES[b]
        return remote(
            packs[k].at[l, core, place.row_at(d)],
            got_bs[k].at[l, d - 1],
            b_sem.at[0, b, d - 1],
            b_sem.at[1, b, d - 1],
            place.in_row(d),
        )

    def copy_c(b, d):
        l, k = BATCHES[b]
        return remote(
            part(out_cs[k], b, place.far_at(d)),
            got_cs[k].at[l, d - 1],
            c_sem.at[0, b, d - 1],
            c_sem.at[1, b, d - 1],
            place.along(d),
        )

    def copy_d(b, d, owner):
        spot = part(finals[BATCHES[b][1]].at[core], b, owner)
        return remote(spot, spot, d_sem.at[0, b, d - 1], d_sem.at[1, b, d - 1], place.along(d))

    def copy_e(b, d, half):
        spot = part(finals[BATCHES[b][1]].at[half], b, place.far_at((n_far - d) % n_far))
        return remote(spot, spot, e_sem.at[0, b, d], e_sem.at[1, b, d], place.twin())

    def sum_cores(b):
        l, k = BATCHES[b]
        copy_a(b).wait_recv()
        for d in range(1, n_row):
            r = place.row_at(d)
            packs[k][l, core, r] = packs[k][l, core, r] + got_as[k][l, r]
            copy_b(b, d).start()
        packs[k][l, core, row] = packs[k][l, core, row] + got_as[k][l, row]

    def sum_row(b):
        l, k = BATCHES[b]
        total = packs[k][l, core, row].astype(f32)
        for d in range(1, n_row):
            copy_b(b, d).wait_recv()
            total += got_bs[k][l, d - 1].astype(f32)
        out_cs[k][l, 0 : batch_rows(n_row, k), :] = total.astype(bf16)
        for d in range(1, n_far):
            copy_c(b, d).start()

    def sum_far(b):
        l, k = BATCHES[b]
        total = part(out_cs[k], b, far)[...].astype(f32)
        for d in range(1, n_far):
            copy_c(b, d).wait_recv()
            total += got_cs[k][l, d - 1].astype(f32)
        part(finals[k].at[core], b, far)[...] = total.astype(bf16)
        for d in range(1, n_far):
            copy_d(b, d, far).start()
        copy_e(b, 0, core).start()

    def pass_on(b):
        for d in range(1, n_far):
            copy_d(b, d, place.far_at(n_far - d)).wait_recv()
            copy_e(b, d, core).start()

    def finish(b):
        copy_a(b).wait_send()
        for d in range(1, n_row):
            copy_b(b, d).wait_send()
        for d in range(1, n_far):
            copy_c(b, d).wait_send()
            copy_d(b, d, far).wait_send()
        for d in range(n_far):
            copy_e(b, d, core).wait_send()
            copy_e(b, d, 1 - core).wait_recv()

    stages = [sum_cores, sum_row, sum_far, pass_on]

    visits = {
        2: (0,),
        chunks + 1: (0, 1),
        2 * chunks - 1: (0,),
        2 * chunks: (1,),
        2 * chunks + 1: (0, 2, 3),
        2 * chunks + 2: (1,),
        3 * chunks: (2,),
        3 * chunks + 1: (1, 4),
        3 * chunks + 2: (2, 3),
        3 * chunks + 3: (4,),
    }
    reached = [0] * len(BATCHES)

    def advance(b):
        for stage in stages[reached[b] : reached[b] + 1]:
            stage(b)
        reached[b] += 1

    @pl.when(step == 0)
    def _():
        def widen_up():
            g_s[1] = up_ref[...].astype(f32)

        if swap:
            meet_all(place, widen_up)
        else:
            widen_up()
            meet(place.partners())
        start_rows(rows_in, rows_out, rows_sem)
        for k in range(3):
            valid, padded = batch_rows(n_row, k), out_cs[k].shape[1]
            if padded > valid:
                out_cs[k][:, valid:, :] = jnp.zeros((2, padded - valid, D), bf16)
        if 2 * low > size:
            spare = (2, n_row, 2 * low - size, D)
            packs[1][:, 1, :, 3 * size - low :, :] = jnp.zeros(spare, bf16)
            packs[2][:, 1, :, 2 * size - low : size + low, :] = jnp.zeros(spare, bf16)

    @pl.when(step == 2 * chunks)
    def _():
        edge_copy().wait_recv()
        assemble_back(g_s.at[1], edge_in, g_s.at[0])

    for at, due in visits.items():

        @pl.when(step == at)
        def _():
            for b in due:
                advance(b)

    @pl.when(step % (2 * chunks) == 0)
    def _():
        vec_g[...] = jnp.zeros_like(vec_g)
        fc1_bg[...] = jnp.zeros_like(fc1_bg)
        table_g[...] = jnp.zeros_like(table_g)
        gz_s[...] = g_s[layer].astype(bf16)
        vec_g[3:4, :] = column_sum(gz_s[...].astype(f32))
        count = D // (4 * size)
        for j in range(4):
            value = dot_tn(act_ref[0, :, D * j : D * (j + 1)], gz_s[...]).astype(bf16)
            for t in range(count):
                for half in range(2):
                    at = (2 * t + half) * 2 * size
                    packs[0][layer, half, j * count + t] = value[at : at + 2 * size, :]

    for b in (0, 3):

        @pl.when(step == 2 * chunks * (b // 3))
        def _():
            copy_a(b).start()

    @pl.when(kind == 0)
    def _():
        upstream = g_s[layer, here, :]
        du = (dot_nt(gz_s[here, :], fc2_w[0]) * slope_ref[0].astype(f32)).astype(bf16)
        du_s[here, :] = du
        fc1_bg[...] += column_sum(du.astype(f32))
        dn = dot_nt(du, fc1_w[0])
        normal, inverse = norm_parts(mid_ref[0])
        gain = vec_ref[layer, 5:6, :]
        h2_s[here, :] = (normal * gain + vec_ref[layer, 7:8, :]).astype(bf16)
        vec_g[5:6, :] += column_sum(dn * normal)
        vec_g[7:8, :] += column_sum(dn)
        mid_grad = upstream + norm_back(dn, normal, inverse, gain)
        g_s[layer, here, :] = mid_grad
        branch = mid_grad.astype(bf16)
        ga_s[here, :] = branch
        vec_g[2:3, :] += column_sum(branch.astype(f32))

    def put(k, half, at, value, first, count):
        for r in range(n_row):
            packs[k][layer, half, r, at : at + count, :] = value[
                size * r + first : size * r + first + count, :
            ]

    @pl.when(step % (2 * chunks) == chunks - 1)
    def _():
        for j in range(4):
            value = dot_tn(h2_s[...], du_s[:, D * j : D * (j + 1)]).astype(bf16)
            put(1, j // 2, size * (j % 2), value, 0, size)
        value = dot_tn(att_ref[0], ga_s[...]).astype(bf16)
        put(1, 0, 2 * size, value, 0, low)
        put(1, 1, 2 * size, value, low, size - low)

    for b in (1, 4):

        @pl.when(step == 2 * chunks * (b // 3) + chunks - 1)
        def _():
            copy_a(b).start()

    @pl.when(kind == 1)
    def _():
        att_grad = dot_nt(ga_s[here, :], proj_w[0]).astype(bf16)
        table = [jnp.zeros((CELL, GROUP * CELL), f32) for _ in range(2)]
        for first in range(0, CHUNK_WINS, 4):
            spots = [(k, g) for k in range(first, first + 4) for g in range(2)]
            do_wides, dps, dss, parts = {}, {}, {}, {}

            def piece(k, g, at):
                return qkv_ref[
                    0, CELL * k : CELL * (k + 1), D * at + 128 * g : D * at + 128 * g + 256
                ]

            for k, g in spots:
                do = att_grad[CELL * k : CELL * (k + 1), 128 * g : 128 * g + 256]
                do_wides[k, g] = widen_heads(do, wide_heads_ref, g)
                val = piece(k, g, 2)
                dps[k, g] = dot_nt(val, do_wides[k, g])
            for k, g in spots:
                prob_low = prob_ref[
                    0, CELL * k : CELL * (k + 1), GROUP * CELL * g : GROUP * CELL * (g + 1)
                ]
                prob = prob_low.astype(f32)
                weighted = prob * dps[k, g]
                ds = (weighted - prob * column_sum(weighted)).astype(bf16)
                table[g] += ds.astype(f32)
                dss[k, g] = ds
                parts[k, g, 2] = dot_nn(prob_low, do_wides[k, g])
            for k, g in spots:
                parts[k, g, 0] = gather_heads(dot_tn(dss[k, g], piece(k, g, 1)), heads_ref, g)
                parts[k, g, 1] = dot_nn(dss[k, g], widen_heads(piece(k, g, 0), wide_heads_ref, g))
            for k in range(first, first + 4):
                there = pl.ds(pl.multiple_of(chunk * CHUNK + CELL * k, CELL), CELL)
                for at, factor in enumerate((SCALE, SCALE, 1.0)):
                    joined = join_groups(parts[k, 0, at], parts[k, 1, at]) * factor
                    dt_s[there, D * at : D * (at + 1)] = joined.astype(bf16)
        for g in range(2):
            table_g[:, GROUP * CELL * g : GROUP * CELL * (g + 1)] += table[g]
        dt = dt_s[here, :]
        vec_g[0:1, :] += column_sum(dt[:, 0:D].astype(f32))
        vec_g[1:2, :] += column_sum(dt[:, 2 * D :].astype(f32))
        dn = dot_nt(dt, qkv_w[0])
        normal, inverse = norm_parts(x_ref[0])
        gain = vec_ref[layer, 4:5, :]
        h1_s[here, :] = (normal * gain + vec_ref[layer, 6:7, :]).astype(bf16)
        vec_g[4:5, :] += column_sum(dn * normal)
        vec_g[6:7, :] += column_sum(dn)
        g_s[layer, here, :] += norm_back(dn, normal, inverse, gain)

    @pl.when(step == chunks + chunks // 2 - 1)
    def _():
        for col in range(WIN_COLS):
            at = CELL * (last_row + col) + 2 * BLOCK
            edge_out[2 * BLOCK * col : 2 * BLOCK * (col + 1), :] = g_s[
                1, at : at + 2 * BLOCK, :
            ].astype(bf16)
        edge_copy().start()

    @pl.when(step == 4 * chunks - 1)
    def _():
        for b in (3, 2):
            advance(b)
        unpick_rows(g_s[0].astype(bf16), grad_rows)
        start_rows(grad_rows, grad_out, grad_sem)

    @pl.when(step % (2 * chunks) == 2 * chunks - 1)
    def _():
        values = [dot_tn(h1_s[...], dt_s[:, D * j : D * (j + 1)]).astype(bf16) for j in range(3)]
        put(2, 0, 0, values[0], 0, size)
        put(2, 0, size, values[1], 0, low)
        put(2, 1, 0, values[2], 0, size)
        put(2, 1, size, values[1], low, size - low)
        table = table_rows(table_g[...], lanes_ref, back_ref)
        table = jnp.concatenate([table, jnp.zeros((HEADS, D - TABLE_PAD), f32)], axis=1)
        vectors = jnp.concatenate(
            [vec_g[...]]
            + [fc1_bg[:, D * j : D * (j + 1)] for j in range(4)]
            + [jnp.zeros((4, D), f32)],
            axis=0,
        )
        for r in range(n_row):
            packs[2][layer, 0, r, size + low :, :] = vectors.astype(bf16)
            packs[2][layer, 1, r, size + low :, :] = table.astype(bf16)

    @pl.when(step == 2 * chunks - 1)
    def _():
        copy_a(2).start()

    @pl.when(step == 4 * chunks - 1)
    def _():
        copy_a(5).start()
        while min(reached) < len(stages):
            for b in (5, 4, 3, 2, 1, 0):
                advance(b)
        for b in range(len(BATCHES)):
            finish(b)
        edge_copy().wait_send()
        copies = [
            pltpu.make_async_copy(finals[k], out, done_sem.at[k])
            for k, out in enumerate((final_0, final_1, final_2))
        ]
        for copy in copies:
            copy.start()
        for copy in copies:
            copy.wait()
        for source, target, sem in (
            (rows_in, rows_out, rows_sem),
            (grad_rows, grad_out, grad_sem),
        ):
            if swap:
                swap_wait(place, source, target, sem)
                swap_end(place, source, target, sem)
                swap_own(place, source, target, sem).wait()
            else:
                pltpu.make_async_copy(source, target, sem.at[0, 0]).wait()


def backward_layers(placing, upstream, y, saved, full, vec):
    n_row, n_far = lax.axis_size("row"), lax.axis_size("clip") // 2
    n = 2 * n_row * n_far
    tokens = upstream.shape[0]
    chunks = tokens // CHUNK
    swap = can_swap(tokens, n)
    heads, wide = head_masks()
    lanes, _, back = table_constants()
    ff = full[2].shape[2]
    size = row_share(n_row)
    anywhere = pl.BlockSpec(memory_space=pl.ANY)

    def at(i):
        return 1 - i // (2 * chunks), i // chunks % 2, (i + chunks // 2) % chunks

    def layer_block(i):
        return 1 - i // (2 * chunks), 0, 0

    def forward_block(i):
        layer, kind, chunk = at(i)
        return (1 - kind) * layer, (1 - kind) * chunk + kind * (chunks // 2 - 1 + layer), 0

    def attention_block(i):
        layer, kind, chunk = at(i)
        return layer, kind * chunk + (1 - kind) * (chunks // 2), 0

    def chunked(value, block):
        return pl.BlockSpec((1, CHUNK, value.shape[2]), block)

    def layered(value):
        return pl.BlockSpec((1, *value.shape[1:]), layer_block)

    x, qkv, prob, att, mid, act, slope = saved
    constants = (
        vec,
        jnp.asarray(heads),
        jnp.asarray(wide, dtype=bf16),
        jnp.asarray(lanes.reshape(2 * TABLE_PAD, 128), dtype=bf16),
        jnp.asarray(back, dtype=bf16),
    )
    valid = [batch_rows(n_row, k) for k in range(3)]
    piece = [piece_rows(n_row, n_far, k) for k in range(3)]
    final = [(2, 2, n_far * piece[k], D) for k in range(3)]
    dma = pltpu.SemaphoreType.DMA

    def each(shape_of):
        return [pltpu.VMEM(shape_of(k), bf16) for k in range(3)]

    return pl.pallas_call(
        functools.partial(backward_kernel, n_row, n_far, swap),
        grid=(4 * chunks,),
        in_specs=[
            whole((1, tokens)),
            whole((tokens, D)),
            whole((tokens, D)),
            chunked(x, attention_block),
            chunked(qkv, attention_block),
            chunked(prob, attention_block),
            layered(att),
            chunked(mid, forward_block),
            layered(act),
            chunked(slope, forward_block),
        ]
        + [layered(weight) for weight in full]
        + [whole(constant.shape) for constant in constants],
        out_specs=[anywhere] * 5,
        out_shape=[jax.ShapeDtypeStruct((tokens, D), bf16)] * 2
        + [jax.ShapeDtypeStruct(shape, bf16) for shape in final],
        scratch_shapes=[
            pltpu.VMEM((8, D), f32),
            pltpu.VMEM((1, ff), f32),
            pltpu.VMEM((CELL, HEADS * CELL), f32),
            pltpu.VMEM((2, tokens, D), f32),
            pltpu.VMEM((tokens, D), bf16),
            pltpu.VMEM((tokens, 3 * D), bf16),
            pltpu.VMEM((tokens, D), bf16),
            pltpu.VMEM((tokens, D), bf16),
            pltpu.VMEM((tokens, ff), bf16),
            *[pltpu.VMEM((tokens, D), bf16)] * 2,
            pltpu.VMEM((WIN_COLS * 2 * BLOCK, D), bf16),
            pltpu.VMEM((WIN_COLS * 2 * BLOCK, D), bf16),
            *each(lambda k: (2, 2, n_row, valid[k], D)),
            *each(lambda k: (2, n_row, valid[k], D)),
            *each(lambda k: (2, n_row - 1, valid[k], D)),
            *each(lambda k: (2, n_far * piece[k], D)),
            *each(lambda k: (2, n_far - 1, piece[k], D)),
            *each(lambda k: final[k]),
            dma((2, n if swap else 1)),
            dma((2, n if swap else 1)),
            dma((2,)),
            dma((2, len(BATCHES))),
            dma((2, len(BATCHES), n_row - 1)),
            dma((2, len(BATCHES), n_far - 1)),
            dma((2, len(BATCHES), n_far - 1)),
            dma((2, len(BATCHES), n_far)),
            dma((3,)),
        ],
        compiler_params=pltpu.CompilerParams(
            collective_id=1, has_side_effects=True, vmem_limit_bytes=VMEM_LIMIT
        ),
        name="backward_layers",
    )(placing.reshape(1, tokens), upstream, y, x, qkv, prob, att, mid, act, slope, *full, *constants)


def close_kernel(
    n_row,
    fc2_ref,
    fc1_ref,
    qkv_ref,
    rows_ref,
    grad_ref,
    rows_o,
    grad_o,
    qkv_o,
    qvb_o,
    proj_o,
    projb_o,
    fc1_o,
    fc1b_o,
    fc2_o,
    fc2b_o,
    gain_o,
    shift_o,
    table_o,
):
    rows_o[...] = rows_ref[...]
    grad_o[...] = grad_ref[...].astype(f32)
    row = lax.axis_index("row")
    size = row_share(n_row)
    low = shard_half(size, 0)[1]
    layer = pl.program_id(0)
    for j in range(2):
        qkv_o[0, :, 2 * D * j : 2 * D * j + D] = qkv_ref[j, 0, 0:size, :].astype(f32)
    qkv_o[0, 0:low, D : 2 * D] = qkv_ref[0, 0, size : size + low, :].astype(f32)
    qkv_o[0, low:size, D : 2 * D] = qkv_ref[1, 0, size : 2 * size - low, :].astype(f32)
    proj_o[0, 0:low, :] = fc1_ref[0, 0, 2 * size : 2 * size + low, :].astype(f32)
    proj_o[0, low:size, :] = fc1_ref[1, 0, 2 * size : 3 * size - low, :].astype(f32)
    for j in range(4):
        at = size * (j % 2)
        fc1_o[0, :, D * j : D * (j + 1)] = fc1_ref[j // 2, 0, at : at + size, :].astype(f32)
    for j in range(2):
        fc2_o[0, 2 * size * j : 2 * size * (j + 1), :] = fc2_ref[j, 0, 0 : 2 * size, :].astype(f32)
    vectors = qkv_ref[0, 0, size + low : size + low + 16, :]
    lane = lax.broadcasted_iota(jnp.int32, (D, size), 0)
    want = lax.broadcasted_iota(jnp.int32, (D, size), 1)
    mine = dot_nn(vectors, jnp.where(lane == want + size * row, 1.0, 0.0).astype(bf16))
    start = 4 * size * row
    lane = lax.broadcasted_iota(jnp.int32, (D, 4 * size), 0)
    want = lax.broadcasted_iota(jnp.int32, (D, 4 * size), 1)
    spot = lax.broadcasted_iota(jnp.int32, (16, 4 * size), 0)
    wide = dot_nn(vectors, jnp.where(lane == want + start % D, 1.0, 0.0).astype(bf16))
    wide = column_sum(jnp.where(spot == 8 + start // D, wide, 0.0))
    qvb_o[0] = mine[0:2]
    gain_o[0] = mine[4:6]
    shift_o[0] = mine[6:8]
    for at in range(2):

        @pl.when(layer == at)
        def _():
            projb_o[at : at + 1, :] = mine[2:3]
            fc2b_o[at : at + 1, :] = mine[3:4]
            fc1b_o[at : at + 1, :] = wide

    table_o[0] = qkv_ref[1, 0, size + low : size + low + 16, 0:TABLE].astype(f32)


def close(rows, grads, finals):
    n_row = lax.axis_size("row")
    size = row_share(n_row)
    tokens = rows.shape[0]
    half = tokens // 2
    shapes = [
        (2, size, 3 * D),
        (2, 2, size),
        (2, size, D),
        (2, size),
        (2, size, 4 * D),
        (2, 4 * size),
        (2, 4 * size, D),
        (2, size),
        (2, 2, size),
        (2, 2, size),
        (2, HEADS, TABLE),
    ]

    def layered(shape):
        if len(shape) == 2:
            return whole(shape)
        return pl.BlockSpec((1, *shape[1:]), lambda i: (i, 0, 0))

    return pl.pallas_call(
        functools.partial(close_kernel, n_row),
        grid=(2,),
        in_specs=[
            pl.BlockSpec((2, 1, *final.shape[2:]), lambda i: (0, i, 0, 0)) for final in finals
        ]
        + [rows_of((half, D))] * 2,
        out_specs=[rows_of((half, D))] * 2 + [layered(shape) for shape in shapes],
        out_shape=[
            jax.ShapeDtypeStruct((tokens, D), bf16),
            jax.ShapeDtypeStruct((tokens, D), f32),
        ]
        + [jax.ShapeDtypeStruct(shape, f32) for shape in shapes],
        compiler_params=pltpu.CompilerParams(vmem_limit_bytes=VMEM_LIMIT),
        name="close",
    )(*finals, rows, grads)


def exchange(values):
    return lax.all_to_all(values, ("clip", "row"), split_axis=0, concat_axis=0, tiled=True)


def body(
    inputs,
    cotangent,
    source_of,
    split_row,
    qkv_weight,
    qv_bias,
    proj_weight,
    proj_bias,
    fc1_weight,
    fc1_bias,
    fc2_weight,
    fc2_bias,
    norm_gain,
    norm_bias,
    rel_table,
):
    clip_count = lax.axis_size("clip")
    row_count = lax.axis_size("row")
    tokens = inputs.shape[0]
    block_rows = tokens // (clip_count * row_count)
    grid_rows = tokens // GRID_COLS
    window_rows = grid_rows // WIN

    placing = source_of // tokens * block_rows + source_of % block_rows
    placing = placing.reshape(window_rows, 2, SHIFT, WIN_COLS, 2, SHIFT)
    placing = placing.transpose(0, 3, 1, 4, 2, 5).reshape(tokens)
    if not can_swap(tokens, clip_count * row_count):
        inputs, cotangent = exchange(inputs), exchange(cotangent)
    saved, upstream, layer_two, full, vec_rows = forward_layers(
        split_row,
        placing,
        inputs,
        cotangent,
        (qkv_weight, proj_weight, fc1_weight, fc2_weight),
        (qv_bias, proj_bias, fc1_bias, fc2_bias, norm_gain, norm_bias),
        rel_table,
    )
    output, input_grad, *finals = backward_layers(placing, upstream, layer_two, saved, full, vec_rows)
    if not can_swap(tokens, clip_count * row_count):
        output, input_grad = exchange(output), exchange(input_grad)
    output, input_grad, *totals = close(output, input_grad, finals)
    totals[-1] = totals[-1].transpose(0, 2, 1)
    return (output, input_grad, *totals)


def solution(mesh):
    placed = (
        P(("clip", "row"), None),
        P(("clip", "row"), None),
        P(("clip", "row")),
        P("clip"),
        P(None, "row", None),
        P(None, None, "row"),
        P(None, "row", None),
        P(None, "row"),
        P(None, "row", None),
        P(None, "row"),
        P(None, "row", None),
        P(None, "row"),
        P(None, None, "row"),
        P(None, None, "row"),
        P(),
    )
    return jax.shard_map(
        body,
        mesh=mesh,
        in_specs=placed,
        out_specs=(
            P(("clip", "row"), None),
            P(("clip", "row"), None),
            P(None, "row", None),
            P(None, None, "row"),
            P(None, "row", None),
            P(None, "row"),
            P(None, "row", None),
            P(None, "row"),
            P(None, "row", None),
            P(None, "row"),
            P(None, None, "row"),
            P(None, None, "row"),
            P(),
        ),
        check_vma=False,
    )
```
